256 devices in a mesh: row: 16 (over x, z_hi, core), col: 16 (over y, z_lo).
Axes of the slice: x: 4, y: 4, z: 8 (z_hi: 2, z_lo: 4; z = z_hi * 4 + z_lo), core: 2. Of those that a mesh axis runs over, the one named last changes fastest.
Arguments:
- object_field: float32 [2, 6144, 6144], P(None, 'row', 'col'), may hold values from -6 to 6
- probe: float32 [2, 2, 256, 256], replicated, may hold values from -6 to 6
- patterns: float32 [16, 16, 6, 256, 256], P('row', 'col'), may hold values from 0.01 to 4
- positions: int32 [16, 16, 6, 2], P('row', 'col'), may hold values from -127 to 6015, as said below
- counts: int32 [16, 16], P('row', 'col'), may hold values from 1 to 6
Outputs:
- object_new: float32 [2, 6144, 6144], P(None, 'row', 'col')
- probe_new: float32 [2, 2, 256, 256], replicated
- position_step: float32 [16, 16, 6, 2], P('row', 'col')
The draws below stay inside these ranges and needn't reach their ends.
Inputs may be any that keep to these rules, and one draw needn't show every extreme that they name: `positions`: the centre (top-left plus 256 // 2) of every slot's patch, live or not, lies inside the tile of the device that holds the slot, at least one pixel from the tile's first row and first column.
All inputs are finite; a program needn't handle non-finite values.
Results may differ from the reference program's by a relative error of at most 0.00018.
Values sent between devices are 32-bit elements; how exact they have to be, the bound alone decides.
A program may use at most 64 MiB of HBM per device.

```python
import math
import jax
import jax.numpy as jnp
from jax import lax

WIN = 256
MODES = 2
TILE = 384
CAP = 6
NY = 6144
NX = 6144
N_ROW = 16
N_COL = 16


def draw_positions(key, part):
    key = jax.random.fold_in(key, 11)
    centres = jax.random.randint(key, (N_ROW, N_COL, CAP, 2), 1, TILE)
    row_ids = jnp.arange(N_ROW)[:, None] + jnp.zeros((1, N_COL), jnp.int32)
    col_ids = jnp.zeros((N_ROW, 1), jnp.int32) + jnp.arange(N_COL)[None, :]
    first_row = jnp.where((row_ids + col_ids) % 2 == 0, 1, TILE - 1)
    first_col = jnp.where(row_ids % 2 == 0, TILE - 1, 1)
    centres = centres.at[:, :, 0, 0].set(first_row).at[:, :, 0, 1].set(first_col)
    starts = jnp.stack([row_ids * TILE, col_ids * TILE], axis=-1)[:, :, None, :]
    return (starts + centres - WIN // 2).astype(jnp.int32)


def draw_counts(key, part):
    key = jax.random.fold_in(key, 13)
    first_key, second_key = jax.random.split(key)
    total = N_ROW * N_COL
    base = jax.random.randint(first_key, (total,), 1, CAP + 1)
    order = jax.random.permutation(second_key, total)
    base = base.at[order[0]].set(CAP).at[order[1]].set(1)
    return base.reshape(N_ROW, N_COL).astype(jnp.int32)


def block_levels(key, extent, cuts, smallest, high):
    def one(axis_at, shards_of):
        steps = jax.random.uniform(jax.random.fold_in(jax.random.fold_in(key, 6), axis_at), (shards_of,), jnp.float32, smallest / len(cuts), high / len(cuts))
        return jnp.repeat(jnp.exp(steps), extent[axis_at] // shards_of).reshape((-1,) + (1,) * (len(extent) - axis_at - 1))

    factor_of = one(*cuts[0])
    for cut in cuts[1:]:
        factor_of = factor_of * one(*cut)
    return factor_of


def bell_draw(key, shape, deviation, bound, pieces=(), dtype=jnp.bfloat16):
    array = jax.random.normal(key, shape, jnp.float32) * deviation
    if len(pieces) > 0:
        array = block_levels(key, shape, pieces, -0.22, 0.18) * array
    return jnp.clip(array, min=-bound, max=bound).astype(dtype)


def setup_inputs(seed: int = 0) -> dict:
    splits = jax.random.split(jax.random.key(seed), 6)
    return {
        "object_field": bell_draw(splits[0], (2, NY, NX), 1.0, 6.0, ((1, 16), (2, 16)), jnp.float32),
        "probe": bell_draw(splits[1], (MODES, 2, WIN, WIN), 1.0, 6.0, (), jnp.float32),
        "patterns": jnp.clip(jnp.exp(math.log(4.0) - 5.9914646 * jax.random.uniform(splits[2], (N_ROW, N_COL, CAP, WIN, WIN), jnp.float32) ** block_levels(splits[2], (N_ROW, N_COL, CAP, WIN, WIN), ((0, 16), (1, 16)), -0.2, 0.2)), 0.01, 4.0),
        "positions": draw_positions(jax.random.fold_in(splits[5], 71), 0),
        "counts": draw_counts(jax.random.fold_in(splits[5], 71), 0),
    }


def slot_terms(padded, probe_re, probe_im, corner, intensity):
    window = probe_re.shape[-1]
    cells = lax.dynamic_slice(padded, (jnp.int32(0), corner[0] - 1, corner[1] - 1), (2, window + 2, window + 2))
    patch = cells[:, 1:-1, 1:-1]
    obj_c = patch[0] + 1j * patch[1]
    downward = 0.5 * (cells[:, 2:, 1:-1] - cells[:, :-2, 1:-1])
    sideways = 0.5 * (cells[:, 1:-1, 2:] - cells[:, 1:-1, :-2])
    probe_c = probe_re + 1j * probe_im
    exit_wave = probe_c * obj_c[None]
    far_field = jnp.fft.fft2(exit_wave, norm='ortho')
    amplitude = jnp.sqrt(lax.optimization_barrier(jnp.sum(far_field.real ** 2 + far_field.imag ** 2, axis=0)))
    factor = jnp.sqrt(intensity) / jnp.maximum(amplitude, 0.25)
    revised = jnp.fft.ifft2(far_field * factor[None], norm='ortho')
    change = revised - exit_wave
    grad_obj = lax.optimization_barrier(jnp.sum(jnp.conj(probe_c) * change, axis=0))
    weight_obj = lax.optimization_barrier(jnp.sum(probe_re ** 2 + probe_im ** 2, axis=0))
    grad_probe = jnp.conj(obj_c)[None] * change
    weight_probe = patch[0] ** 2 + patch[1] ** 2
    raws = []
    for slope_part in (downward, sideways):
        slope = probe_c * (slope_part[0] + 1j * slope_part[1])[None]
        numer = jnp.sum((jnp.conj(change) * slope).real)
        denom = jnp.sum(slope.real ** 2 + slope.imag ** 2)
        raws.append(numer / jnp.sqrt(denom + 1e-06))
    obj_terms = jnp.stack([grad_obj.real, grad_obj.imag, weight_obj])
    probe_terms = jnp.stack([grad_probe.real, grad_probe.imag], axis=1)
    return (obj_terms, probe_terms, weight_probe, jnp.stack(raws))

def reference(object_field, probe, patterns, positions, counts):
    half_win = WIN // 2
    padded = jnp.pad(object_field, ((0, 0), (half_win, half_win), (half_win, half_win)))
    corners = positions.reshape(-1, 2).astype(jnp.int32) + half_win
    intensities = patterns.reshape(-1, WIN, WIN)
    live = (jnp.arange(CAP)[None, None, :] < counts[:, :, None]).reshape(-1).astype(jnp.float32)
    probe_re = probe[:, 0]
    probe_im = probe[:, 1]

    def visit(carry, item):
        grad_all, probe_acc, weight_acc = carry
        corner, intensity, alive = item
        obj_terms, probe_terms, weight_probe, raw = slot_terms(padded, probe_re, probe_im, corner, intensity)
        start = (jnp.int32(0), corner[0], corner[1])
        current = lax.dynamic_slice(grad_all, start, (3, WIN, WIN))
        grad_all = lax.dynamic_update_slice(grad_all, current + alive * obj_terms, start)
        return ((grad_all, probe_acc + alive * probe_terms, weight_acc + alive * weight_probe), raw * alive)
    init = (jnp.zeros((3, NY + WIN, NX + WIN), jnp.float32), jnp.zeros((MODES, 2, WIN, WIN), jnp.float32), jnp.zeros((WIN, WIN), jnp.float32))
    (grad_all, probe_acc, weight_acc), raws = lax.scan(visit, init, (corners, intensities, live))
    core = grad_all[:, half_win:half_win + NY, half_win:half_win + NX]
    probe_power = jnp.max(lax.optimization_barrier(jnp.sum(probe ** 2, axis=(0, 1))))
    object_new = object_field + core[:2] / (core[2] + 0.1 * probe_power)[None]
    probe_new = probe + probe_acc / (weight_acc + 0.1 * jnp.max(weight_acc))[None, None]
    mean_raw = lax.optimization_barrier(jnp.sum(raws, axis=0)) / jnp.sum(live)
    position_step = ((raws - mean_raw[None]) * live[:, None]).reshape(N_ROW, N_COL, CAP, 2)
    return (object_new, probe_new, position_step)
```

```python
import functools

import jax
import jax.numpy as jnp
import ml_dtypes
import numpy as np
from jax import lax
from jax.experimental import pallas as pl
from jax.experimental.pallas import tpu as pltpu
from jax.sharding import PartitionSpec as P

MESH = pl.DeviceIdType.MESH
VMEM = pltpu.VMEM
f32 = jnp.float32
bf16 = jnp.bfloat16

WIN = 256
HALF = 128
TILE = 384
CAP = 6
EXT_ROWS = 8 + HALF + TILE + HALF + 8
OFFSETS = [(-1, 0), (1, 0), (0, -1), (0, 1), (-1, -1), (-1, 1), (1, -1), (1, 1)]


def dft_tables():
    k = np.arange(HALF)
    even = np.exp(-2j * np.pi * np.outer(2 * k, k) / WIN) / np.sqrt(WIN)
    odd = np.exp(-2j * np.pi * np.outer(2 * k + 1, k) / WIN) / np.sqrt(WIN)

    def block(z):
        return np.block([[z.real, -z.imag], [z.imag, z.real]])

    out = []
    for mat in (block(even), block(odd), block(even).T, block(odd).T):
        high = mat.astype(np.float32).astype(ml_dtypes.bfloat16)
        low = (mat - high.astype(np.float64)).astype(np.float32).astype(ml_dtypes.bfloat16)
        out += [high, low]
    return np.stack(out)


def order_table():
    table = np.zeros((WIN, WIN), np.float32)
    k = np.arange(HALF)
    table[2 * k, k] = 1
    table[2 * k + 1, HALF + k] = 1
    return table.astype(ml_dtypes.bfloat16)


def split(x):
    high = x.astype(bf16)
    return high, (x - high.astype(f32)).astype(bf16)


def mm(a, b):
    return jnp.dot(a, b, preferred_element_type=f32)


def neighbour(step):
    n_row, n_col = lax.axis_size("row"), lax.axis_size("col")
    r, c = lax.axis_index("row"), lax.axis_index("col")
    return (lax.rem(r + step[0] + n_row, n_row), lax.rem(c + step[1] + n_col, n_col))


def greet():
    barrier = pltpu.get_barrier_semaphore()
    for step in OFFSETS:
        pl.semaphore_signal(barrier, inc=1, device_id=neighbour(step), device_id_type=MESH)
    pl.semaphore_wait(barrier, len(OFFSETS))


def send_rows(d):
    return {-1: (136, 128), 0: (136, 384), 1: (392, 128)}[d]


def land_rows(d):
    return {-1: (520, 128), 0: (136, 384), 1: (8, 128)}[d]


def send_cols(d):
    return {-1: (1, 1), 0: (1, 3), 1: (3, 1)}[d]


def land_cols(d):
    return {-1: (4, 1), 0: (1, 3), 1: (0, 1)}[d]


def halo_kernel(obj, pats, meta, order, ext, spat, metas, turned, ssem, rsem, msend, mrecv):
    greet()
    for t in range(3):
        for ch in range(2):
            ext[ch, 1 + t, 136:520, :] = obj[ch, :, 128 * t : 128 * (t + 1)]
    metas[4] = meta[...]
    copies = []
    for i, (dr, dc) in enumerate(OFFSETS):
        r0, rn = send_rows(dr)
        q0, _ = land_rows(dr)
        c0, cn = send_cols(dc)
        e0, _ = land_cols(dc)
        copy = pltpu.make_async_remote_copy(
            src_ref=ext.at[:, pl.ds(c0, cn), pl.ds(r0, rn), :],
            dst_ref=ext.at[:, pl.ds(e0, cn), pl.ds(q0, rn), :],
            send_sem=ssem.at[i],
            recv_sem=rsem.at[i],
            device_id=neighbour((dr, dc)),
            device_id_type=MESH,
        )
        copy.start()
        copies.append(copy)
    for i, (dr, dc) in enumerate(OFFSETS):
        copy = pltpu.make_async_remote_copy(
            src_ref=metas.at[4],
            dst_ref=metas.at[(1 - dr) * 3 + 1 - dc],
            send_sem=msend.at[i],
            recv_sem=mrecv.at[i],
            device_id=neighbour((dr, dc)),
            device_id_type=MESH,
        )
        copy.start()
        copies.append(copy)

    def reorder(slot, _):
        high, low = split(jnp.sqrt(pats[slot]))
        sorted_cols = mm(high, order[...]) + mm(low, order[...])
        for j in range(2):
            turned[j] = sorted_cols[:, 128 * j : 128 * (j + 1)]
        for parity in range(2):
            for j in range(2):
                spat[slot, 128 * parity : 128 * (parity + 1), 128 * j : 128 * (j + 1)] = turned[
                    j, pl.ds(parity, 128, stride=2), :
                ]
        return 0

    lax.fori_loop(0, CAP, reorder, 0)
    for copy in copies:
        copy.wait()
    r, c = lax.axis_index("row"), lax.axis_index("col")
    for ch in range(2):
        for t in range(5):
            ext[ch, t, 0:8, :] = jnp.zeros((8, 128), f32)
            ext[ch, t, 648:656, :] = jnp.zeros((8, 128), f32)

    @pl.when(r == 0)
    def _():
        ext[:, :, 8:136, :] = jnp.zeros((2, 5, 128, 128), f32)

    @pl.when(r == lax.axis_size("row") - 1)
    def _():
        ext[:, :, 520:648, :] = jnp.zeros((2, 5, 128, 128), f32)

    @pl.when(c == 0)
    def _():
        ext[:, 0, 8:648, :] = jnp.zeros((2, 640, 128), f32)

    @pl.when(c == lax.axis_size("col") - 1)
    def _():
        ext[:, 4, 8:648, :] = jnp.zeros((2, 640, 128), f32)


def halo(obj, pats, meta, order):
    return pl.pallas_call(
        halo_kernel,
        out_shape=(
            jax.ShapeDtypeStruct((2, 5, EXT_ROWS, 128), f32),
            jax.ShapeDtypeStruct((CAP, WIN, WIN), f32),
            jax.ShapeDtypeStruct((9, 8, 128), jnp.int32),
        ),
        in_specs=[pl.BlockSpec(memory_space=VMEM)] * 4,
        out_specs=[pl.BlockSpec(memory_space=VMEM)] * 3,
        scratch_shapes=[
            VMEM((2, WIN, 128), f32),
            pltpu.SemaphoreType.DMA((8,)),
            pltpu.SemaphoreType.DMA((8,)),
            pltpu.SemaphoreType.DMA((8,)),
            pltpu.SemaphoreType.DMA((8,)),
        ],
        compiler_params=pltpu.CompilerParams(
            collective_id=0, has_side_effects=True, vmem_limit_bytes=40 * 2**20
        ),
        name="halo_in",
    )(obj, pats, meta, order)


def turn(x, shift):
    return pltpu.roll(x, shift, 1)


def slots_kernel(
    where,
    ext,
    probe,
    spat,
    tables,
    grad,
    weight,
    probe_out,
    raw,
    patch,
    slope,
    xs,
    ts,
    zs,
    rev,
    power,
    canvas,
    hg,
):
    r, c = lax.axis_index("row"), lax.axis_index("col")
    row_start, col_start = r * TILE, c * TILE
    lane = lax.broadcasted_iota(jnp.int32, (8, 128), 1)
    zero = jnp.zeros((8, 128), f32)

    def clear(ref, lead, rows):
        def step(i, _):
            for ix in lead:
                ref[(*ix, pl.ds(pl.multiple_of(i * 8, 8), 8), slice(None))] = zero
            return 0

        lax.fori_loop(0, rows // 8, step, 0)

    clear(grad, [(ch, t) for ch in range(2) for t in range(5)], EXT_ROWS)
    clear(canvas, [(t,) for t in range(8)], 904)
    clear(probe_out, [(i, t) for i in range(5) for t in range(2)], WIN)
    raw[...] = zero

    def fill_power(i, _):
        rows = pl.ds(pl.multiple_of(i * 8, 8), 8)
        for j in range(2):
            cols = slice(128 * j, 128 * (j + 1))
            power[j, rows, :] = (
                probe[0, 0, rows, cols] ** 2
                + probe[0, 1, rows, cols] ** 2
                + probe[1, 0, rows, cols] ** 2
                + probe[1, 1, rows, cols] ** 2
            )
        return 0

    lax.fori_loop(0, WIN // 8, fill_power, 0)

    for j in range(9):
        jr, jc = j // 3 - 1, j % 3 - 1
        inside = (r + jr >= 0) & (r + jr < lax.axis_size("row")) & (c + jc >= 0) & (c + jc < lax.axis_size("col"))
        live = jnp.where(inside, where[j, 0, 2 * CAP], 0)

        def place(slot, _, j=j):
            top = where[j, 0, 2 * slot] - row_start
            left = where[j, 0, 2 * slot + 1] - col_start

            @pl.when((top > -WIN) & (top < TILE) & (left > -WIN) & (left < TILE))
            def _():
                at = left + WIN
                tile, shift = at // 128, lax.rem(at, 128)
                keep = lane >= shift

                def rows_step(i, _):
                    src = pl.ds(pl.multiple_of(i * 8, 8), 8)
                    dst = pl.ds(top + WIN + i * 8, 8)
                    a, b = turn(power[0, src, :], shift), turn(power[1, src, :], shift)
                    canvas[tile, dst, :] += jnp.where(keep, a, 0.0)
                    canvas[tile + 1, dst, :] += jnp.where(keep, b, a)
                    canvas[tile + 2, dst, :] += jnp.where(keep, 0.0, b)
                    return 0

                lax.fori_loop(0, WIN // 8, rows_step, 0, unroll=4)

            return 0

        lax.fori_loop(0, live, place, 0)

    for t in range(3):
        weight[:, 128 * t : 128 * (t + 1)] = canvas[2 + t, pl.ds(WIN, TILE), :]

    def visit(slot, _):
        top = where[4, 0, 2 * slot] - row_start + HALF
        left = where[4, 0, 2 * slot + 1] - col_start + HALF

        base = left - 1
        tile, shift = base // 128, lax.rem(base, 128)
        last = jnp.minimum(tile + 3, 4)

        def take(i, _):
            src = pl.ds(top + i * 8, 8)
            dst = pl.ds(pl.multiple_of(i * 8, 8), 8)
            for ch in range(2):
                x = [ext[ch, tile, src, :], ext[ch, tile + 1, src, :], ext[ch, tile + 2, src, :], ext[ch, last, src, :]]
                got = []
                for more in range(3):
                    s = shift + more
                    back = lax.rem(256 - s, 128)
                    y = [turn(v, back) for v in x]
                    near = lane < 128 - s
                    over = lane < 256 - s
                    got.append(
                        [
                            jnp.where(near, y[j], jnp.where(over, y[j + 1], y[min(j + 2, 3)]))
                            for j in range(2)
                        ]
                    )
                for j in range(2):
                    patch[ch, j, dst, :] = got[1][j]
                    slope[ch, j, dst, :] = 0.5 * (got[2][j] - got[0][j])
            return 0

        lax.fori_loop(0, 34, take, 0, unroll=2)

        def leave(i, _):
            rows = [pl.multiple_of(i * 16 + 128 * h, 16) for h in range(2)]
            for j in range(2):
                cols = slice(128 * j, 128 * (j + 1))
                o = [[patch[ch, j, pl.ds(rw + 8, 16), :] for ch in range(2)] for rw in rows]
                for m in range(2):
                    e = []
                    for h in range(2):
                        pr = probe[m, 0, pl.ds(rows[h], 16), cols]
                        pi = probe[m, 1, pl.ds(rows[h], 16), cols]
                        e.append((pr * o[h][0] - pi * o[h][1], pr * o[h][1] + pi * o[h][0]))
                    for ch in range(2):
                        at = pl.ds(pl.multiple_of(i * 16 + 128 * ch, 16), 16)
                        for k, v in enumerate((e[0][ch] + e[1][ch], e[0][ch] - e[1][ch])):
                            high, low = split(v)
                            xs[m, 2 * k, at, cols] = high
                            xs[m, 2 * k + 1, at, cols] = low
            return 0

        lax.fori_loop(0, 8, leave, 0)

        def left_mm(k, high, low):
            return mm(tables[2 * k], high) + mm(tables[2 * k], low) + mm(tables[2 * k + 1], high)

        def right_mm(k, high, low):
            return mm(high, tables[2 * k]) + mm(low, tables[2 * k]) + mm(high, tables[2 * k + 1])

        for m in range(2):
            for k in range(2):
                y = left_mm(k, xs[m, 2 * k], xs[m, 2 * k + 1])
                for ch in range(2):
                    a, b = y[128 * ch : 128 * (ch + 1), :128], y[128 * ch : 128 * (ch + 1), 128:]
                    for q, v in enumerate((a + b, a - b)):
                        high, low = split(v)
                        at = (slice(128 * k, 128 * (k + 1)), slice(128 * ch, 128 * (ch + 1)))
                        ts[m, 2 * q, *at] = high
                        ts[m, 2 * q + 1, *at] = low
            for q in range(2):
                zs[m, q] = right_mm(2 + q, ts[m, 2 * q], ts[m, 2 * q + 1])

        def project(i, _):
            at = pl.ds(pl.multiple_of(i * 16, 16), 16)
            for q in range(2):
                z = [[zs[m, q, at, 128 * ch : 128 * (ch + 1)] for ch in range(2)] for m in range(2)]
                amp = z[0][0] ** 2 + z[0][1] ** 2 + z[1][0] ** 2 + z[1][1] ** 2
                factor = spat[slot, at, 128 * q : 128 * (q + 1)] * lax.rsqrt(jnp.maximum(amp, 0.0625))
                for m in range(2):
                    for ch in range(2):
                        high, low = split(z[m][ch] * factor)
                        ts[m, 2 * q, at, 128 * ch : 128 * (ch + 1)] = high
                        ts[m, 2 * q + 1, at, 128 * ch : 128 * (ch + 1)] = low
            return 0

        lax.fori_loop(0, 16, project, 0)

        for m in range(2):
            a = right_mm(0, ts[m, 0], ts[m, 1])
            b = right_mm(1, ts[m, 2], ts[m, 3])
            for half, v in enumerate((a + b, a - b)):
                high, low = split(v)
                for k in range(2):
                    for ch in range(2):
                        at = (slice(128 * ch, 128 * (ch + 1)), slice(128 * half, 128 * (half + 1)))
                        pick = (slice(128 * k, 128 * (k + 1)), slice(128 * ch, 128 * (ch + 1)))
                        xs[m, 2 * k, *at] = high[pick]
                        xs[m, 2 * k + 1, *at] = low[pick]
            u = left_mm(2, xs[m, 0], xs[m, 1])
            v = left_mm(3, xs[m, 2], xs[m, 3])
            for ch in range(2):
                at = slice(128 * ch, 128 * (ch + 1))
                rev[m, ch, 0:128, :] = u[at] + v[at]
                rev[m, ch, 128:256, :] = u[at] - v[at]

        hg[...] = jnp.zeros((4, 8, 128), f32)
        tile_g, shift_g = left // 128, lax.rem(left, 128)
        keep = lane >= shift_g

        def finish(i, _):
            at = pl.ds(pl.multiple_of(i * 8, 8), 8)
            dst = pl.ds(top + 8 + i * 8, 8)
            g = []
            acc = [zero] * 4
            for j in range(2):
                cols = slice(128 * j, 128 * (j + 1))
                o_re = patch[0, j, pl.ds(i * 8 + 8, 8), :]
                o_im = patch[1, j, pl.ds(i * 8 + 8, 8), :]
                w = power[j, at, :]
                g_re, g_im = -w * o_re, -w * o_im
                for m in range(2):
                    p_re, p_im = probe[m, 0, at, cols], probe[m, 1, at, cols]
                    v_re, v_im = rev[m, 0, at, cols], rev[m, 1, at, cols]
                    g_re += p_re * v_re + p_im * v_im
                    g_im += p_re * v_im - p_im * v_re
                    probe_out[2 * m, j, at, :] += o_re * v_re + o_im * v_im
                    probe_out[2 * m + 1, j, at, :] += o_re * v_im - o_im * v_re
                probe_out[4, j, at, :] += o_re * o_re + o_im * o_im
                d_re = 0.5 * (patch[0, j, pl.ds(i * 8 + 9, 8), :] - patch[0, j, pl.ds(i * 8 + 7, 8), :])
                d_im = 0.5 * (patch[1, j, pl.ds(i * 8 + 9, 8), :] - patch[1, j, pl.ds(i * 8 + 7, 8), :])
                s_re = slope[0, j, pl.ds(i * 8 + 8, 8), :]
                s_im = slope[1, j, pl.ds(i * 8 + 8, 8), :]
                acc[0] += g_re * d_re + g_im * d_im
                acc[1] += w * (d_re * d_re + d_im * d_im)
                acc[2] += g_re * s_re + g_im * s_im
                acc[3] += w * (s_re * s_re + s_im * s_im)
                g.append((g_re, g_im))
            for k in range(4):
                hg[k] += acc[k]
            for ch in range(2):
                a, b = turn(g[0][ch], shift_g), turn(g[1][ch], shift_g)
                grad[ch, tile_g, dst, :] += jnp.where(keep, a, 0.0)
                grad[ch, tile_g + 1, dst, :] += jnp.where(keep, b, a)
                grad[ch, tile_g + 2, dst, :] += jnp.where(keep, 0.0, b)
            return 0

        lax.fori_loop(0, WIN // 8, finish, 0, unroll=2)
        total = [jnp.sum(hg[k], axis=(0, 1), keepdims=True) for k in range(4)]
        at_row = lax.broadcasted_iota(jnp.int32, (8, 128), 0) == slot
        for k in range(2):
            value = total[2 * k] * lax.rsqrt(total[2 * k + 1] + 1e-6)
            raw[...] += jnp.where(at_row & (lane == k), value, 0.0)
        return 0

    lax.fori_loop(0, where[4, 0, 2 * CAP], visit, 0)


def slots(where, ext, probe, spat, tables):
    v = pl.BlockSpec(memory_space=VMEM)
    return pl.pallas_call(
        slots_kernel,
        out_shape=(
            jax.ShapeDtypeStruct((2, 5, EXT_ROWS, 128), f32),
            jax.ShapeDtypeStruct((TILE, TILE), f32),
            jax.ShapeDtypeStruct((5, 2, WIN, 128), f32),
            jax.ShapeDtypeStruct((8, 128), f32),
        ),
        in_specs=[pl.BlockSpec(memory_space=pltpu.SMEM), v, v, v, v],
        out_specs=[v, v, v, v],
        scratch_shapes=[
            VMEM((2, 2, 272, 128), f32),
            VMEM((2, 2, 272, 128), f32),
            VMEM((2, 4, WIN, WIN), bf16),
            VMEM((2, 4, WIN, WIN), bf16),
            VMEM((2, 2, WIN, WIN), f32),
            VMEM((2, 2, WIN, WIN), f32),
            VMEM((2, WIN, 128), f32),
            VMEM((8, 904, 128), f32),
            VMEM((4, 8, 128), f32),
        ],
        compiler_params=pltpu.CompilerParams(vmem_limit_bytes=50 * 2**20),
        name="slots",
    )(where, ext, probe, spat, tables)


def on_device(object_field, probe, patterns, positions, counts):
    meta = jnp.concatenate([positions.reshape(1, 2 * CAP), counts.reshape(1, 1)], axis=1)
    meta = jnp.pad(meta, ((0, 7), (0, 128 - 2 * CAP - 1)))
    ext, spat, where = halo(object_field, patterns[0, 0], meta, jnp.asarray(order_table()))
    grad, weight, probe_sum, raw = slots(where, ext, probe, spat, jnp.asarray(dft_tables()))
    return finish_all(object_field, probe, grad, weight, probe_sum, raw, counts)


def finish_all(object_field, probe, grad, weight, probe_sum, raw, counts):
    n_row, n_col = lax.axis_size("row"), lax.axis_size("col")

    def shifted(block, axis, distance):
        n = lax.axis_size(axis)
        route = [(i - distance, i) for i in range(n) if 0 <= i - distance < n]
        return lax.ppermute(block, axis, route)

    g = grad[:, :, 8:648, :].transpose(0, 2, 1, 3).reshape(2, 640, 640)
    from_above = shifted(g[:, 512:, :], "row", 1)
    from_below = shifted(g[:, :128, :], "row", -1)
    g = g.at[:, 128:256, :].add(from_above).at[:, 384:512, :].add(from_below)[:, 128:512, :]
    from_left = shifted(g[:, :, 512:], "col", 1)
    from_right = shifted(g[:, :, :128], "col", -1)
    g = g.at[:, :, 128:256].add(from_left).at[:, :, 384:512].add(from_right)[:, :, 128:512]
    power = jnp.max(jnp.sum(probe**2, axis=(0, 1)))
    object_new = object_field + g / (weight + 0.1 * power)[None]
    raw_all = raw[:CAP, :2]
    live = (jnp.arange(CAP) < counts[0, 0]).astype(f32)
    total, raw_total, count = lax.psum(
        (probe_sum, raw_all.sum(axis=0), counts[0, 0].astype(f32)), ("row", "col")
    )
    total = total.transpose(0, 2, 1, 3).reshape(5, WIN, WIN)
    wp = total[4]
    gp = total[:4].reshape(2, 2, WIN, WIN) - probe * wp
    probe_new = probe + gp / (wp + 0.1 * jnp.max(wp))
    step = ((raw_all - (raw_total / count)[None]) * live[:, None]).reshape(1, 1, CAP, 2)
    return object_new, probe_new, step


def solution(mesh):
    placed = (
        P(None, "row", "col"),
        P(),
        P("row", "col", None, None, None),
        P("row", "col", None, None),
        P("row", "col"),
    )
    return jax.shard_map(
        on_device,
        mesh=mesh,
        in_specs=placed,
        out_specs=(P(None, "row", "col"), P(), P("row", "col", None, None)),
        check_vma=False,
    )
```

```python
import functools

import jax
import jax.numpy as jnp
import ml_dtypes
import numpy as np
from jax import lax
from jax.experimental import pallas as pl
from jax.experimental.pallas import tpu as pltpu
from jax.sharding import PartitionSpec as P

MESH = pl.DeviceIdType.MESH
VMEM = pltpu.VMEM
f32 = jnp.float32
bf16 = jnp.bfloat16

WIN = 256
HALF = 128
TILE = 384
CAP = 6
EXT_ROWS = 8 + HALF + TILE + HALF + 8
OFFSETS = [(-1, 0), (1, 0), (0, -1), (0, 1), (-1, -1), (-1, 1), (1, -1), (1, 1)]


def dft_tables():
    k = np.arange(HALF)
    even = np.exp(-2j * np.pi * np.outer(2 * k, k) / WIN) / np.sqrt(WIN)
    odd = np.exp(-2j * np.pi * np.outer(2 * k + 1, k) / WIN) / np.sqrt(WIN)

    def block(z):
        return np.block([[z.real, -z.imag], [z.imag, z.real]])

    out = []
    for mat in (block(even), block(odd), block(even).T, block(odd).T):
        high = mat.astype(np.float32).astype(ml_dtypes.bfloat16)
        low = (mat - high.astype(np.float64)).astype(np.float32).astype(ml_dtypes.bfloat16)
        out += [high, low]
    return np.stack(out)


def order_table():
    table = np.zeros((WIN, WIN), np.float32)
    k = np.arange(HALF)
    table[2 * k, k] = 1
    table[2 * k + 1, HALF + k] = 1
    return table.astype(ml_dtypes.bfloat16)


def split(x):
    high = x.astype(bf16)
    return high, (x - high.astype(f32)).astype(bf16)


def mm(a, b):
    return jnp.dot(a, b, preferred_element_type=f32)


def neighbour(step):
    n_row, n_col = lax.axis_size("row"), lax.axis_size("col")
    r, c = lax.axis_index("row"), lax.axis_index("col")
    return (lax.rem(r + step[0] + n_row, n_row), lax.rem(c + step[1] + n_col, n_col))


def greet():
    barrier = pltpu.get_barrier_semaphore()
    for step in OFFSETS:
        pl.semaphore_signal(barrier, inc=1, device_id=neighbour(step), device_id_type=MESH)
    pl.semaphore_wait(barrier, len(OFFSETS))


def send_rows(d):
    return {-1: (136, 128), 0: (136, 384), 1: (392, 128)}[d]


def land_rows(d):
    return {-1: (520, 128), 0: (136, 384), 1: (8, 128)}[d]


def send_cols(d):
    return {-1: (1, 1), 0: (1, 3), 1: (3, 1)}[d]


def land_cols(d):
    return {-1: (4, 1), 0: (1, 3), 1: (0, 1)}[d]


def halo_kernel(obj, pats, meta, order, ext, spat, metas, turned, ssem, rsem, msend, mrecv):
    greet()
    for t in range(3):
        for ch in range(2):
            ext[ch, 1 + t, 136:520, :] = obj[ch, :, 128 * t : 128 * (t + 1)]
    metas[4] = meta[...]
    copies = []
    for i, (dr, dc) in enumerate(OFFSETS):
        r0, rn = send_rows(dr)
        q0, _ = land_rows(dr)
        c0, cn = send_cols(dc)
        e0, _ = land_cols(dc)
        copy = pltpu.make_async_remote_copy(
            src_ref=ext.at[:, pl.ds(c0, cn), pl.ds(r0, rn), :],
            dst_ref=ext.at[:, pl.ds(e0, cn), pl.ds(q0, rn), :],
            send_sem=ssem.at[i],
            recv_sem=rsem.at[i],
            device_id=neighbour((dr, dc)),
            device_id_type=MESH,
        )
        copy.start()
        copies.append(copy)
    for i, (dr, dc) in enumerate(OFFSETS):
        copy = pltpu.make_async_remote_copy(
            src_ref=metas.at[4],
            dst_ref=metas.at[(1 - dr) * 3 + 1 - dc],
            send_sem=msend.at[i],
            recv_sem=mrecv.at[i],
            device_id=neighbour((dr, dc)),
            device_id_type=MESH,
        )
        copy.start()
        copies.append(copy)

    def reorder(slot, _):
        high, low = split(jnp.sqrt(pats[slot]))
        sorted_cols = mm(high, order[...]) + mm(low, order[...])
        for j in range(2):
            turned[j] = sorted_cols[:, 128 * j : 128 * (j + 1)]
        for parity in range(2):
            for j in range(2):
                spat[slot, 128 * parity : 128 * (parity + 1), 128 * j : 128 * (j + 1)] = turned[
                    j, pl.ds(parity, 128, stride=2), :
                ]
        return 0

    lax.fori_loop(0, CAP, reorder, 0)
    for copy in copies:
        copy.wait()
    r, c = lax.axis_index("row"), lax.axis_index("col")
    for ch in range(2):
        for t in range(5):
            ext[ch, t, 0:8, :] = jnp.zeros((8, 128), f32)
            ext[ch, t, 648:656, :] = jnp.zeros((8, 128), f32)

    @pl.when(r == 0)
    def _():
        ext[:, :, 8:136, :] = jnp.zeros((2, 5, 128, 128), f32)

    @pl.when(r == lax.axis_size("row") - 1)
    def _():
        ext[:, :, 520:648, :] = jnp.zeros((2, 5, 128, 128), f32)

    @pl.when(c == 0)
    def _():
        ext[:, 0, 8:648, :] = jnp.zeros((2, 640, 128), f32)

    @pl.when(c == lax.axis_size("col") - 1)
    def _():
        ext[:, 4, 8:648, :] = jnp.zeros((2, 640, 128), f32)


def halo(obj, pats, meta, order):
    return pl.pallas_call(
        halo_kernel,
        out_shape=(
            jax.ShapeDtypeStruct((2, 5, EXT_ROWS, 128), f32),
            jax.ShapeDtypeStruct((CAP, WIN, WIN), f32),
            jax.ShapeDtypeStruct((9, 8, 128), jnp.int32),
        ),
        in_specs=[pl.BlockSpec(memory_space=VMEM)] * 4,
        out_specs=[pl.BlockSpec(memory_space=VMEM)] * 3,
        scratch_shapes=[
            VMEM((2, WIN, 128), f32),
            pltpu.SemaphoreType.DMA((8,)),
            pltpu.SemaphoreType.DMA((8,)),
            pltpu.SemaphoreType.DMA((8,)),
            pltpu.SemaphoreType.DMA((8,)),
        ],
        compiler_params=pltpu.CompilerParams(
            collective_id=0, has_side_effects=True, vmem_limit_bytes=40 * 2**20
        ),
        name="halo_in",
    )(obj, pats, meta, order)


def turn(x, shift):
    return pltpu.roll(x, shift, 1)


def slots_kernel(
    where,
    ext,
    probe,
    spat,
    tables,
    grad,
    weight,
    probe_out,
    raw,
    patch,
    slope,
    xs,
    ts,
    zs,
    rev,
    power,
    canvas,
    hg,
):
    r, c = lax.axis_index("row"), lax.axis_index("col")
    row_start, col_start = r * TILE, c * TILE
    lane = lax.broadcasted_iota(jnp.int32, (8, 128), 1)
    zero = jnp.zeros((8, 128), f32)

    def clear(ref, lead, rows):
        def step(i, _):
            for ix in lead:
                ref[(*ix, pl.ds(pl.multiple_of(i * 8, 8), 8), slice(None))] = zero
            return 0

        lax.fori_loop(0, rows // 8, step, 0)

    clear(grad, [(ch, t) for ch in range(2) for t in range(5)], EXT_ROWS)
    clear(canvas, [(t,) for t in range(8)], 904)
    clear(probe_out, [(i, t) for i in range(5) for t in range(2)], WIN)
    raw[...] = jnp.where(
        (lax.broadcasted_iota(jnp.int32, (8, 128), 0) == 7) & (lane == 2),
        where[4, 0, 2 * CAP].astype(f32),
        0.0,
    )

    def fill_power(i, _):
        rows = pl.ds(pl.multiple_of(i * 8, 8), 8)
        for j in range(2):
            cols = slice(128 * j, 128 * (j + 1))
            power[j, rows, :] = (
                probe[0, 0, rows, cols] ** 2
                + probe[0, 1, rows, cols] ** 2
                + probe[1, 0, rows, cols] ** 2
                + probe[1, 1, rows, cols] ** 2
            )
        return 0

    lax.fori_loop(0, WIN // 8, fill_power, 0)

    for j in range(9):
        jr, jc = j // 3 - 1, j % 3 - 1
        inside = (r + jr >= 0) & (r + jr < lax.axis_size("row")) & (c + jc >= 0) & (c + jc < lax.axis_size("col"))
        live = jnp.where(inside, where[j, 0, 2 * CAP], 0)

        def place(slot, _, j=j):
            top = where[j, 0, 2 * slot] - row_start
            left = where[j, 0, 2 * slot + 1] - col_start

            @pl.when((top > -WIN) & (top < TILE) & (left > -WIN) & (left < TILE))
            def _():
                at = left + WIN
                tile, shift = at // 128, lax.rem(at, 128)
                keep = lane >= shift

                def rows_step(i, _):
                    src = pl.ds(pl.multiple_of(i * 8, 8), 8)
                    dst = pl.ds(top + WIN + i * 8, 8)
                    a, b = turn(power[0, src, :], shift), turn(power[1, src, :], shift)
                    canvas[tile, dst, :] += jnp.where(keep, a, 0.0)
                    canvas[tile + 1, dst, :] += jnp.where(keep, b, a)
                    canvas[tile + 2, dst, :] += jnp.where(keep, 0.0, b)
                    return 0

                lax.fori_loop(0, WIN // 8, rows_step, 0, unroll=4)

            return 0

        lax.fori_loop(0, live, place, 0)

    for t in range(3):
        weight[:, 128 * t : 128 * (t + 1)] = canvas[2 + t, pl.ds(WIN, TILE), :]

    def visit(slot, _):
        top = where[4, 0, 2 * slot] - row_start + HALF
        left = where[4, 0, 2 * slot + 1] - col_start + HALF

        base = left - 1
        tile, shift = base // 128, lax.rem(base, 128)
        last = jnp.minimum(tile + 3, 4)

        def take(i, _):
            src = pl.ds(top + i * 8, 8)
            dst = pl.ds(pl.multiple_of(i * 8, 8), 8)
            for ch in range(2):
                x = [ext[ch, tile, src, :], ext[ch, tile + 1, src, :], ext[ch, tile + 2, src, :], ext[ch, last, src, :]]
                got = []
                for more in range(3):
                    s = shift + more
                    back = lax.rem(256 - s, 128)
                    y = [turn(v, back) for v in x]
                    near = lane < 128 - s
                    over = lane < 256 - s
                    got.append(
                        [
                            jnp.where(near, y[j], jnp.where(over, y[j + 1], y[min(j + 2, 3)]))
                            for j in range(2)
                        ]
                    )
                for j in range(2):
                    patch[ch, j, dst, :] = got[1][j]
                    slope[ch, j, dst, :] = 0.5 * (got[2][j] - got[0][j])
            return 0

        lax.fori_loop(0, 34, take, 0, unroll=2)

        def leave(i, _):
            rows = [pl.multiple_of(i * 16 + 128 * h, 16) for h in range(2)]
            for j in range(2):
                cols = slice(128 * j, 128 * (j + 1))
                o = [[patch[ch, j, pl.ds(rw + 8, 16), :] for ch in range(2)] for rw in rows]
                for m in range(2):
                    e = []
                    for h in range(2):
                        pr = probe[m, 0, pl.ds(rows[h], 16), cols]
                        pi = probe[m, 1, pl.ds(rows[h], 16), cols]
                        e.append((pr * o[h][0] - pi * o[h][1], pr * o[h][1] + pi * o[h][0]))
                    for ch in range(2):
                        at = pl.ds(pl.multiple_of(i * 16 + 128 * ch, 16), 16)
                        for k, v in enumerate((e[0][ch] + e[1][ch], e[0][ch] - e[1][ch])):
                            high, low = split(v)
                            xs[m, 2 * k, at, cols] = high
                            xs[m, 2 * k + 1, at, cols] = low
            return 0

        lax.fori_loop(0, 8, leave, 0)

        def left_mm(k, high, low):
            return mm(tables[2 * k], high) + mm(tables[2 * k], low) + mm(tables[2 * k + 1], high)

        def right_mm(k, high, low):
            return mm(high, tables[2 * k]) + mm(low, tables[2 * k]) + mm(high, tables[2 * k + 1])

        for m in range(2):
            for k in range(2):
                y = left_mm(k, xs[m, 2 * k], xs[m, 2 * k + 1])
                for ch in range(2):
                    a, b = y[128 * ch : 128 * (ch + 1), :128], y[128 * ch : 128 * (ch + 1), 128:]
                    for q, v in enumerate((a + b, a - b)):
                        high, low = split(v)
                        at = (slice(128 * k, 128 * (k + 1)), slice(128 * ch, 128 * (ch + 1)))
                        ts[m, 2 * q, *at] = high
                        ts[m, 2 * q + 1, *at] = low
            for q in range(2):
                zs[m, q] = right_mm(2 + q, ts[m, 2 * q], ts[m, 2 * q + 1])

        def project(i, _):
            at = pl.ds(pl.multiple_of(i * 16, 16), 16)
            for q in range(2):
                z = [[zs[m, q, at, 128 * ch : 128 * (ch + 1)] for ch in range(2)] for m in range(2)]
                amp = z[0][0] ** 2 + z[0][1] ** 2 + z[1][0] ** 2 + z[1][1] ** 2
                factor = spat[slot, at, 128 * q : 128 * (q + 1)] * lax.rsqrt(jnp.maximum(amp, 0.0625))
                for m in range(2):
                    for ch in range(2):
                        high, low = split(z[m][ch] * factor)
                        ts[m, 2 * q, at, 128 * ch : 128 * (ch + 1)] = high
                        ts[m, 2 * q + 1, at, 128 * ch : 128 * (ch + 1)] = low
            return 0

        lax.fori_loop(0, 16, project, 0)

        for m in range(2):
            a = right_mm(0, ts[m, 0], ts[m, 1])
            b = right_mm(1, ts[m, 2], ts[m, 3])
            for half, v in enumerate((a + b, a - b)):
                high, low = split(v)
                for k in range(2):
                    for ch in range(2):
                        at = (slice(128 * ch, 128 * (ch + 1)), slice(128 * half, 128 * (half + 1)))
                        pick = (slice(128 * k, 128 * (k + 1)), slice(128 * ch, 128 * (ch + 1)))
                        xs[m, 2 * k, *at] = high[pick]
                        xs[m, 2 * k + 1, *at] = low[pick]
            u = left_mm(2, xs[m, 0], xs[m, 1])
            v = left_mm(3, xs[m, 2], xs[m, 3])
            for ch in range(2):
                at = slice(128 * ch, 128 * (ch + 1))
                rev[m, ch, 0:128, :] = u[at] + v[at]
                rev[m, ch, 128:256, :] = u[at] - v[at]

        hg[...] = jnp.zeros((4, 8, 128), f32)
        tile_g, shift_g = left // 128, lax.rem(left, 128)
        keep = lane >= shift_g

        def finish(i, _):
            at = pl.ds(pl.multiple_of(i * 8, 8), 8)
            dst = pl.ds(top + 8 + i * 8, 8)
            g = []
            acc = [zero] * 4
            for j in range(2):
                cols = slice(128 * j, 128 * (j + 1))
                o_re = patch[0, j, pl.ds(i * 8 + 8, 8), :]
                o_im = patch[1, j, pl.ds(i * 8 + 8, 8), :]
                w = power[j, at, :]
                g_re, g_im = -w * o_re, -w * o_im
                for m in range(2):
                    p_re, p_im = probe[m, 0, at, cols], probe[m, 1, at, cols]
                    v_re, v_im = rev[m, 0, at, cols], rev[m, 1, at, cols]
                    g_re += p_re * v_re + p_im * v_im
                    g_im += p_re * v_im - p_im * v_re
                    probe_out[2 * m, j, at, :] += o_re * v_re + o_im * v_im
                    probe_out[2 * m + 1, j, at, :] += o_re * v_im - o_im * v_re
                probe_out[4, j, at, :] += o_re * o_re + o_im * o_im
                d_re = 0.5 * (patch[0, j, pl.ds(i * 8 + 9, 8), :] - patch[0, j, pl.ds(i * 8 + 7, 8), :])
                d_im = 0.5 * (patch[1, j, pl.ds(i * 8 + 9, 8), :] - patch[1, j, pl.ds(i * 8 + 7, 8), :])
                s_re = slope[0, j, pl.ds(i * 8 + 8, 8), :]
                s_im = slope[1, j, pl.ds(i * 8 + 8, 8), :]
                acc[0] += g_re * d_re + g_im * d_im
                acc[1] += w * (d_re * d_re + d_im * d_im)
                acc[2] += g_re * s_re + g_im * s_im
                acc[3] += w * (s_re * s_re + s_im * s_im)
                g.append((g_re, g_im))
            for k in range(4):
                hg[k] += acc[k]
            for ch in range(2):
                a, b = turn(g[0][ch], shift_g), turn(g[1][ch], shift_g)
                grad[ch, tile_g, dst, :] += jnp.where(keep, a, 0.0)
                grad[ch, tile_g + 1, dst, :] += jnp.where(keep, b, a)
                grad[ch, tile_g + 2, dst, :] += jnp.where(keep, 0.0, b)
            return 0

        lax.fori_loop(0, WIN // 8, finish, 0, unroll=2)
        total = [jnp.sum(hg[k], axis=(0, 1), keepdims=True) for k in range(4)]
        at_row = lax.broadcasted_iota(jnp.int32, (8, 128), 0) == slot
        for k in range(2):
            value = total[2 * k] * lax.rsqrt(total[2 * k + 1] + 1e-6)
            raw[...] += jnp.where(at_row & (lane == k), value, 0.0)
        return 0

    lax.fori_loop(0, where[4, 0, 2 * CAP], visit, 0)


def slots(where, ext, probe, spat, tables):
    v = pl.BlockSpec(memory_space=VMEM)
    return pl.pallas_call(
        slots_kernel,
        out_shape=(
            jax.ShapeDtypeStruct((2, 5, EXT_ROWS, 128), f32),
            jax.ShapeDtypeStruct((TILE, TILE), f32),
            jax.ShapeDtypeStruct((5, 2, WIN, 128), f32),
            jax.ShapeDtypeStruct((8, 128), f32),
        ),
        in_specs=[pl.BlockSpec(memory_space=pltpu.SMEM), v, v, v, v],
        out_specs=[v, v, v, v],
        scratch_shapes=[
            VMEM((2, 2, 272, 128), f32),
            VMEM((2, 2, 272, 128), f32),
            VMEM((2, 4, WIN, WIN), bf16),
            VMEM((2, 4, WIN, WIN), bf16),
            VMEM((2, 2, WIN, WIN), f32),
            VMEM((2, 2, WIN, WIN), f32),
            VMEM((2, WIN, 128), f32),
            VMEM((8, 904, 128), f32),
            VMEM((4, 8, 128), f32),
        ],
        compiler_params=pltpu.CompilerParams(vmem_limit_bytes=50 * 2**20),
        name="slots",
    )(where, ext, probe, spat, tables)


SHARDS = 32
SHARD = 80
PIECE = SHARD + 8


def plane(dx, dy):
    r, c = lax.axis_index("row"), lax.axis_index("col")
    return (lax.rem(r + 4 * dx, 16), lax.rem(c + 4 * dy, 16))


def depth_of():
    r, c = lax.axis_index("row"), lax.axis_index("col")
    return 4 * lax.rem(r // 2, 2) + lax.rem(c, 4)


def along(dz):
    r, c = lax.axis_index("row"), lax.axis_index("col")
    z = lax.rem(depth_of() + dz, 8)
    return (r // 4 * 4 + z // 4 * 2 + lax.rem(r, 2), c // 4 * 4 + lax.rem(z, 4))


def sums_kernel(
    grad,
    weight,
    obj,
    probe,
    part,
    raw,
    obj_new,
    probe_new,
    step,
    strips,
    sides,
    corners,
    mine,
    mate_part,
    plane_part,
    deep,
    deep_part,
    deep_all,
    all_sum,
    flat,
    hsend,
    hrecv,
    csend,
    crecv,
    psend,
    precv,
    zsend,
    zrecv,
):
    r, c = lax.axis_index("row"), lax.axis_index("col")
    core = lax.rem(r, 2)
    own = r // 4 * 4 + c // 4
    z = depth_of()
    mate = (r + 1 - 2 * core, c)
    planes = [(dx, dy) for dx in range(4) for dy in range(4) if (dx, dy) != (0, 0)]

    barrier = pltpu.get_barrier_semaphore()
    partners = [neighbour(s) for s in OFFSETS] + [mate]
    partners += [plane(*p) for p in planes] + [along(d) for d in range(1, 8)]
    for partner in partners:
        pl.semaphore_signal(barrier, inc=1, device_id=partner, device_id_type=MESH)

    def gather(i, _):
        mine[i, 0:SHARD, :] = part[pl.ds(pl.multiple_of(i * SHARD, SHARD), SHARD), :]
        mine[i, SHARD:PIECE, :] = raw[...]
        return 0

    lax.fori_loop(0, SHARDS, gather, 0)
    pl.semaphore_wait(barrier, len(partners))

    def send(src, dst, ssem, rsem, to):
        copy = pltpu.make_async_remote_copy(
            src_ref=src, dst_ref=dst, send_sem=ssem, recv_sem=rsem, device_id=to, device_id_type=MESH
        )
        copy.start()
        return copy

    half = SHARDS // 2
    to_mate = send(
        mine.at[pl.ds(half * (1 - core), half)], mate_part, csend.at[0], crecv.at[0], mate
    )
    halos = []
    for i, (dr, dc) in enumerate(OFFSETS):
        q0, qn = {-1: (8, 128), 0: (136, 384), 1: (520, 128)}[dr]
        e0, en = {-1: (0, 1), 0: (1, 3), 1: (4, 1)}[dc]
        src = grad.at[:, pl.ds(e0, en), pl.ds(q0, qn), :]
        dst = strips.at[i] if i < 2 else sides.at[i - 2] if i < 4 else corners.at[i - 4]
        halos.append(send(src, dst, hsend.at[i], hrecv.at[i], neighbour((dr, dc))))

    to_mate.wait()

    def add_mate(i, _):
        mine[half * core + i] += mate_part[i]
        return 0

    lax.fori_loop(0, half, add_mate, 0)
    copies = []
    for i, (dx, dy) in enumerate(planes):
        to = plane(dx, dy)
        owner = to[0] // 4 * 4 + to[1] // 4
        copies.append(
            send(mine.at[half * core + owner], plane_part.at[i], psend.at[i], precv.at[i], to)
        )
    for copy in copies:
        copy.wait()
    total = mine[half * core + own]
    for i in range(15):
        total = total + plane_part[i]
    deep[0:PIECE, :] = total
    deep[PIECE:128, :] = jnp.zeros((128 - PIECE, 128), f32)
    copies = []
    for d in range(1, 8):
        there = lax.rem(z + d, 8)
        copies.append(
            send(
                deep.at[pl.ds(pl.multiple_of(there * 16, 16), 16)],
                deep_part.at[d - 1],
                zsend.at[d - 1],
                zrecv.at[d - 1],
                along(d),
            )
        )
    for copy in copies:
        copy.wait()
    total = deep[pl.ds(pl.multiple_of(z * 16, 16), 16), :]
    for d in range(7):
        total = total + deep_part[d]
    here = deep_all.at[pl.ds(pl.multiple_of(z * 16, 16), 16)]
    deep_all[pl.ds(pl.multiple_of(z * 16, 16), 16), :] = total
    copies = [send(here, here, zsend.at[6 + d], zrecv.at[6 + d], along(d)) for d in range(1, 8)]
    for copy in copies:
        copy.wait()
    all_sum[half * core + own] = deep_all[0:PIECE, :]
    block = all_sum.at[half * core + own]
    copies = [
        send(block, block, psend.at[15 + i], precv.at[15 + i], plane(*p)) for i, p in enumerate(planes)
    ]
    for copy in copies:
        copy.wait()
    block = all_sum.at[pl.ds(half * core, half)]
    to_mate = send(block, block, csend.at[1], crecv.at[1], mate)

    for copy in halos:
        copy.wait()
    n_row, n_col = lax.axis_size("row"), lax.axis_size("col")
    row_ok = {-1: r < n_row - 1, 1: r > 0, 0: r >= 0}
    col_ok = {-1: c < n_col - 1, 1: c > 0, 0: c >= 0}
    ok = [row_ok[dr] & col_ok[dc] for dr, dc in OFFSETS]

    def peak(i, top):
        rows = pl.ds(pl.multiple_of(i * 8, 8), 8)
        power = probe[0, 0, rows, :] ** 2 + probe[0, 1, rows, :] ** 2
        power = power + probe[1, 0, rows, :] ** 2 + probe[1, 1, rows, :] ** 2
        return jnp.maximum(top, power)

    top = lax.fori_loop(0, WIN // 8, peak, jnp.zeros((8, WIN), f32))
    floor = 0.1 * jnp.max(top, axis=(0, 1), keepdims=True)

    for band in range(3):

        def update(i, _, band=band):
            rows = pl.ds(pl.multiple_of(band * 128 + i * 8, 8), 8)
            thin = pl.ds(pl.multiple_of(i * 8, 8), 8)
            for t in range(3):
                cols = slice(128 * t, 128 * (t + 1))
                down = weight[rows, cols] + floor
                for ch in range(2):
                    g = grad[ch, 1 + t, pl.ds(pl.multiple_of(136 + band * 128 + i * 8, 8), 8), :]
                    for k, (dr, dc) in enumerate(OFFSETS):
                        in_rows = dr == 0 or (dr == -1 and band == 2) or (dr == 1 and band == 0)
                        in_cols = dc == 0 or (dc == -1 and t == 2) or (dc == 1 and t == 0)
                        if not (in_rows and in_cols):
                            continue
                        if k < 2:
                            v = strips[k, ch, t, thin, :]
                        elif k < 4:
                            v = sides[k - 2, ch, 0, rows, :]
                        else:
                            v = corners[k - 4, ch, 0, thin, :]
                        g = g + jnp.where(ok[k], v, 0.0)
                    obj_new[ch, rows, cols] = obj[ch, rows, cols] + g / down
            return 0

        lax.fori_loop(0, 16, update, 0)

    to_mate.wait()

    def spread(i, _):
        flat[pl.ds(pl.multiple_of(i * SHARD, SHARD), SHARD), :] = all_sum[i, 0:SHARD, :]
        return 0

    lax.fori_loop(0, SHARDS, spread, 0)

    def peak_sum(i, top):
        return jnp.maximum(top, flat[pl.ds(pl.multiple_of(2048 + i * 8, 8), 8), :])

    top = lax.fori_loop(0, 64, peak_sum, jnp.zeros((8, 128), f32))
    floor_p = 0.1 * jnp.max(top, axis=(0, 1), keepdims=True)

    def renew(i, _):
        rows = pl.ds(pl.multiple_of(i * 8, 8), 8)
        for j in range(2):
            cols = slice(128 * j, 128 * (j + 1))

            def at(k):
                return flat[pl.ds(pl.multiple_of((2 * k + j) * WIN + i * 8, 8), 8), :]

            wp = at(4)
            scale = 1.0 / (wp + floor_p)
            for m in range(2):
                for ch in range(2):
                    old = probe[m, ch, rows, cols]
                    probe_new[m, ch, rows, cols] = old + (at(2 * m + ch) - old * wp) * scale
        return 0

    lax.fori_loop(0, WIN // 8, renew, 0)

    rows8 = lax.broadcasted_iota(jnp.int32, (8, 128), 0)
    lanes8 = lax.broadcasted_iota(jnp.int32, (8, 128), 1)
    is_count = (rows8 == 7) & (lanes8 == 2)
    sums = all_sum[0, SHARD:PIECE, :]
    count = jnp.sum(jnp.where(is_count, sums, 0.0), axis=(0, 1), keepdims=True)
    mine_count = jnp.sum(jnp.where(is_count, raw[...], 0.0), axis=(0, 1), keepdims=True)
    mean = jnp.sum(sums, axis=0, keepdims=True) / count
    step[...] = jnp.where(rows8.astype(f32) < mine_count, raw[...] - mean, 0.0)


def sums(grad, weight, obj, probe, part, raw):
    v = pl.BlockSpec(memory_space=VMEM)
    dma = pltpu.SemaphoreType.DMA
    return pl.pallas_call(
        sums_kernel,
        out_shape=(
            jax.ShapeDtypeStruct((2, TILE, TILE), f32),
            jax.ShapeDtypeStruct((2, 2, WIN, WIN), f32),
            jax.ShapeDtypeStruct((8, 128), f32),
        ),
        in_specs=[v] * 6,
        out_specs=[v] * 3,
        scratch_shapes=[
            VMEM((2, 2, 3, 128, 128), f32),
            VMEM((2, 2, 1, TILE, 128), f32),
            VMEM((4, 2, 1, 128, 128), f32),
            VMEM((SHARDS, PIECE, 128), f32),
            VMEM((SHARDS // 2, PIECE, 128), f32),
            VMEM((15, PIECE, 128), f32),
            VMEM((128, 128), f32),
            VMEM((7, 16, 128), f32),
            VMEM((128, 128), f32),
            VMEM((SHARDS, PIECE, 128), f32),
            VMEM((SHARDS * SHARD, 128), f32),
            dma((8,)),
            dma((8,)),
            dma((2,)),
            dma((2,)),
            dma((30,)),
            dma((30,)),
            dma((14,)),
            dma((14,)),
        ],
        compiler_params=pltpu.CompilerParams(
            collective_id=1, has_side_effects=True, vmem_limit_bytes=50 * 2**20
        ),
        name="sums",
    )(grad, weight, obj, probe, part, raw)


def on_device(object_field, probe, patterns, positions, counts):
    meta = jnp.concatenate([positions.reshape(1, 2 * CAP), counts.reshape(1, 1)], axis=1)
    meta = jnp.pad(meta, ((0, 7), (0, 128 - 2 * CAP - 1)))
    ext, spat, where = halo(object_field, patterns[0, 0], meta, jnp.asarray(order_table()))
    grad, weight, part, raw = slots(where, ext, probe, spat, jnp.asarray(dft_tables()))
    object_new, probe_new, step = sums(
        grad, weight, object_field, probe, part.reshape(SHARDS * SHARD, 128), raw
    )
    return object_new, probe_new, step[:CAP, :2].reshape(1, 1, CAP, 2)


def solution(mesh):
    placed = (
        P(None, "row", "col"),
        P(),
        P("row", "col", None, None, None),
        P("row", "col", None, None),
        P("row", "col"),
    )
    return jax.shard_map(
        on_device,
        mesh=mesh,
        in_specs=placed,
        out_specs=(P(None, "row", "col"), P(), P("row", "col", None, None)),
        check_vma=False,
    )
```

```python
import functools

import jax
import jax.numpy as jnp
import ml_dtypes
import numpy as np
from jax import lax
from jax.experimental import pallas as pl
from jax.experimental.pallas import tpu as pltpu
from jax.sharding import PartitionSpec as P

MESH = pl.DeviceIdType.MESH
VMEM = pltpu.VMEM
f32 = jnp.float32
bf16 = jnp.bfloat16

WIN = 256
HALF = 128
TILE = 384
CAP = 6
STEP = 32
EXT_ROWS = 8 + HALF + TILE + HALF + 8
OFFSETS = [(-1, 0), (1, 0), (0, -1), (0, 1), (-1, -1), (-1, 1), (1, -1), (1, 1)]


def dft_tables():
    k = np.arange(HALF)
    even = np.exp(-2j * np.pi * np.outer(2 * k, k) / WIN) / np.sqrt(WIN)
    odd = np.exp(-2j * np.pi * np.outer(2 * k + 1, k) / WIN) / np.sqrt(WIN)

    def block(z):
        return np.block([[z.real, -z.imag], [z.imag, z.real]])

    out = []
    for mat in (block(even), block(odd), block(even).T, block(odd).T):
        high = mat.astype(np.float32).astype(ml_dtypes.bfloat16)
        low = (mat - high.astype(np.float64)).astype(np.float32).astype(ml_dtypes.bfloat16)
        out += [high, low]
    return np.stack(out)


def order_table():
    table = np.zeros((WIN, WIN), np.float32)
    k = np.arange(HALF)
    table[2 * k, k] = 1
    table[2 * k + 1, HALF + k] = 1
    return table.astype(ml_dtypes.bfloat16)


def split(x):
    high = x.astype(bf16)
    return high, (x - high.astype(f32)).astype(bf16)


def mm(a, b):
    return jnp.dot(a, b, preferred_element_type=f32)


def neighbour(step):
    n_row, n_col = lax.axis_size("row"), lax.axis_size("col")
    r, c = lax.axis_index("row"), lax.axis_index("col")
    return (lax.rem(r + step[0] + n_row, n_row), lax.rem(c + step[1] + n_col, n_col))


def greet():
    barrier = pltpu.get_barrier_semaphore()
    for step in OFFSETS:
        pl.semaphore_signal(barrier, inc=1, device_id=neighbour(step), device_id_type=MESH)
    pl.semaphore_wait(barrier, len(OFFSETS))


def send(src, dst, ssem, rsem, to):
    copy = pltpu.make_async_remote_copy(
        src_ref=src, dst_ref=dst, send_sem=ssem, recv_sem=rsem, device_id=to, device_id_type=MESH
    )
    copy.start()
    return copy


def halo_kernel(obj, pats, meta, order, ext, spat, metas, turned, ssem, rsem, msend, mrecv):
    core = lax.rem(lax.axis_index("row"), 2)
    greet()
    for t in range(3):
        for ch in range(2):
            ext[ch, 1 + t, 136:520, :] = obj[ch, :, 128 * t : 128 * (t + 1)]
    metas[4] = meta[...]

    def strip(tile, tiles, row, rows):
        return ext.at[:, pl.ds(tile, tiles), pl.ds(row, rows), :]

    tops = [
        send(strip(1, 3, 136, 128), strip(1, 3, 520, 128), ssem.at[0], rsem.at[0], neighbour((-1, 0))),
        send(strip(1, 3, 392, 128), strip(1, 3, 8, 128), ssem.at[1], rsem.at[1], neighbour((1, 0))),
    ]
    small = [
        send(
            metas.at[4],
            metas.at[(1 - dr) * 3 + 1 - dc],
            msend.at[i],
            mrecv.at[i],
            neighbour((dr, dc)),
        )
        for i, (dr, dc) in enumerate(OFFSETS)
    ]

    def reorder(slot, _):
        high, low = split(jnp.sqrt(pats[slot]))
        sorted_cols = mm(high, order[...]) + mm(low, order[...])
        for j in range(2):
            turned[j] = sorted_cols[:, 128 * j : 128 * (j + 1)]
        for parity in range(2):
            for j in range(2):
                spat[slot, 128 * parity : 128 * (parity + 1), 128 * j : 128 * (j + 1)] = turned[
                    j, pl.ds(parity, 128, stride=2), :
                ]
        return 0

    lax.fori_loop(0, CAP, reorder, 0)
    for copy in tops:
        copy.wait()
    outer = pl.multiple_of(8 + 512 * core, 8)
    left, right = neighbour((0, -1)), neighbour((0, 1))
    far = [
        send(strip(1, 1, outer, 128), strip(4, 1, outer, 128), ssem.at[2], rsem.at[2], left),
        send(strip(3, 1, outer, 128), strip(0, 1, outer, 128), ssem.at[3], rsem.at[3], right),
    ]
    sides = [
        send(strip(1, 1, 136, 384), strip(4, 1, 136, 384), ssem.at[4], rsem.at[4], left),
        send(strip(3, 1, 136, 384), strip(0, 1, 136, 384), ssem.at[5], rsem.at[5], right),
    ]
    mate = (lax.axis_index("row") + 1 - 2 * core, lax.axis_index("col"))
    near = pl.multiple_of(392 - 256 * core, 8)
    for k, tile in enumerate((4, 0)):
        sides[k].wait()
        far.append(
            send(strip(tile, 1, near, 128), strip(tile, 1, outer, 128), ssem.at[6 + k], rsem.at[6 + k], mate)
        )
    for copy in far + small:
        copy.wait()
    r, c = lax.axis_index("row"), lax.axis_index("col")
    for ch in range(2):
        for t in range(5):
            ext[ch, t, 0:8, :] = jnp.zeros((8, 128), f32)
            ext[ch, t, 648:656, :] = jnp.zeros((8, 128), f32)

    @pl.when(r == 0)
    def _():
        ext[:, :, 8:136, :] = jnp.zeros((2, 5, 128, 128), f32)

    @pl.when(r == lax.axis_size("row") - 1)
    def _():
        ext[:, :, 520:648, :] = jnp.zeros((2, 5, 128, 128), f32)

    @pl.when(c == 0)
    def _():
        ext[:, 0, 8:648, :] = jnp.zeros((2, 640, 128), f32)

    @pl.when(c == lax.axis_size("col") - 1)
    def _():
        ext[:, 4, 8:648, :] = jnp.zeros((2, 640, 128), f32)


def halo(obj, pats, meta, order):
    return pl.pallas_call(
        halo_kernel,
        out_shape=(
            jax.ShapeDtypeStruct((2, 5, EXT_ROWS, 128), f32),
            jax.ShapeDtypeStruct((CAP, WIN, WIN), f32),
            jax.ShapeDtypeStruct((9, 8, 128), jnp.int32),
        ),
        in_specs=[pl.BlockSpec(memory_space=VMEM)] * 4,
        out_specs=[pl.BlockSpec(memory_space=VMEM)] * 3,
        scratch_shapes=[
            VMEM((2, WIN, 128), f32),
            pltpu.SemaphoreType.DMA((8,)),
            pltpu.SemaphoreType.DMA((8,)),
            pltpu.SemaphoreType.DMA((8,)),
            pltpu.SemaphoreType.DMA((8,)),
        ],
        compiler_params=pltpu.CompilerParams(
            collective_id=0, has_side_effects=True, vmem_limit_bytes=20 * 2**20
        ),
        name="halo_in",
    )(obj, pats, meta, order)


def turn(x, shift):
    return pltpu.roll(x, shift, 1)


def slots_kernel(
    where,
    ext,
    probe,
    spat,
    tables,
    grad,
    weight,
    probe_out,
    raw,
    patch,
    slope,
    xs,
    ts,
    zs,
    rev,
    power,
    canvas,
):
    r, c = lax.axis_index("row"), lax.axis_index("col")
    row_start, col_start = r * TILE, c * TILE
    lane = lax.broadcasted_iota(jnp.int32, (8, 128), 1)
    zero = jnp.zeros((8, 128), f32)

    def clear(ref, lead, rows):
        def step(i, _):
            for ix in lead:
                ref[(*ix, pl.ds(pl.multiple_of(i * 8, 8), 8), slice(None))] = zero
            return 0

        lax.fori_loop(0, rows // 8, step, 0, unroll=2)

    clear(grad, [(ch, t) for ch in range(2) for t in range(5)], EXT_ROWS)
    clear(probe_out, [(i, t) for i in range(5) for t in range(2)], WIN)
    for t in range(3):
        canvas[2 + t, WIN : WIN + TILE, :] = jnp.zeros((TILE, 128), f32)
    raw[...] = jnp.where(
        (lax.broadcasted_iota(jnp.int32, (8, 128), 0) == 7) & (lane == 2),
        where[4, 0, 2 * CAP].astype(f32),
        0.0,
    )

    def fill_power(i, _):
        rows = pl.ds(pl.multiple_of(i * 8, 8), 8)
        for j in range(2):
            cols = slice(128 * j, 128 * (j + 1))
            power[j, rows, :] = (
                probe[0, 0, rows, cols] ** 2
                + probe[0, 1, rows, cols] ** 2
                + probe[1, 0, rows, cols] ** 2
                + probe[1, 1, rows, cols] ** 2
            )
        return 0

    lax.fori_loop(0, WIN // 8, fill_power, 0, unroll=4)

    for j in range(9):
        jr, jc = j // 3 - 1, j % 3 - 1
        inside = (r + jr >= 0) & (r + jr < lax.axis_size("row")) & (c + jc >= 0) & (c + jc < lax.axis_size("col"))
        live = jnp.where(inside, where[j, 0, 2 * CAP], 0)

        def place(slot, _, j=j):
            top = where[j, 0, 2 * slot] - row_start
            left = where[j, 0, 2 * slot + 1] - col_start

            @pl.when((top > -WIN) & (top < TILE) & (left > -WIN) & (left < TILE))
            def _():
                at = left + WIN
                tile, shift = at // 128, lax.rem(at, 128)
                keep = lax.broadcasted_iota(jnp.int32, (32, 128), 1) >= shift

                def rows_step(i, _):
                    src = pl.ds(pl.multiple_of(i * 32, 32), 32)
                    dst = pl.ds(top + WIN + i * 32, 32)
                    a, b = turn(power[0, src, :], shift), turn(power[1, src, :], shift)
                    canvas[tile, dst, :] += jnp.where(keep, a, 0.0)
                    canvas[tile + 1, dst, :] += jnp.where(keep, b, a)
                    canvas[tile + 2, dst, :] += jnp.where(keep, 0.0, b)
                    return 0

                lax.fori_loop(jnp.maximum(-top, 0) // 32, (jnp.minimum(TILE - top, WIN) + 31) // 32, rows_step, 0)

            return 0

        lax.fori_loop(0, live, place, 0)

    for t in range(3):
        weight[:, 128 * t : 128 * (t + 1)] = canvas[2 + t, pl.ds(WIN, TILE), :]

    def visit(slot, _):
        top = where[4, 0, 2 * slot] - row_start + HALF
        left = where[4, 0, 2 * slot + 1] - col_start + HALF

        base = left - 1
        tile, shift = base // 128, lax.rem(base, 128)
        last = jnp.minimum(tile + 3, 4)
        apart = lax.broadcasted_iota(jnp.int32, (512, 256), 0) - lax.broadcasted_iota(
            jnp.int32, (512, 256), 1
        )
        move = jnp.where(apart == shift + 1, 1.0, 0.0).astype(bf16)
        differ = jnp.where(apart == shift + 2, 0.5, jnp.where(apart == shift, -0.5, 0.0)).astype(bf16)
        shifter = jnp.concatenate([move, differ], axis=1)
        for ch in range(2):
            x = [ext[ch, t, pl.ds(top, 272), :] for t in (tile, tile + 1, tile + 2, last)]
            high, low = split(jnp.concatenate(x, axis=1))
            y = mm(high, shifter) + mm(low, shifter)
            for j in range(2):
                patch[ch, j] = y[:, 128 * j : 128 * (j + 1)]
                slope[ch, j] = y[:, 256 + 128 * j : 256 + 128 * (j + 1)]

        def leave(i, _):
            rows = [pl.multiple_of(i * 16 + 128 * h, 16) for h in range(2)]
            for j in range(2):
                cols = slice(128 * j, 128 * (j + 1))
                o = [[patch[ch, j, pl.ds(rw + 8, 16), :] for ch in range(2)] for rw in rows]
                for m in range(2):
                    e = []
                    for h in range(2):
                        pr = probe[m, 0, pl.ds(rows[h], 16), cols]
                        pi = probe[m, 1, pl.ds(rows[h], 16), cols]
                        e.append((pr * o[h][0] - pi * o[h][1], pr * o[h][1] + pi * o[h][0]))
                    for ch in range(2):
                        at = pl.ds(pl.multiple_of(i * 16 + 128 * ch, 16), 16)
                        for k, v in enumerate((e[0][ch] + e[1][ch], e[0][ch] - e[1][ch])):
                            high, low = split(v)
                            xs[m, 2 * k, at, cols] = high
                            xs[m, 2 * k + 1, at, cols] = low
            return 0

        lax.fori_loop(0, 8, leave, 0, unroll=True)

        def left_mm(k, high, low):
            return mm(tables[2 * k], high) + mm(tables[2 * k], low) + mm(tables[2 * k + 1], high)

        def right_mm(k, high, low):
            return mm(high, tables[2 * k]) + mm(low, tables[2 * k]) + mm(high, tables[2 * k + 1])

        for m in range(2):
            for k in range(2):
                y = left_mm(k, xs[m, 2 * k], xs[m, 2 * k + 1])
                for ch in range(2):
                    a, b = y[128 * ch : 128 * (ch + 1), :128], y[128 * ch : 128 * (ch + 1), 128:]
                    for q, v in enumerate((a + b, a - b)):
                        high, low = split(v)
                        at = (slice(128 * k, 128 * (k + 1)), slice(128 * ch, 128 * (ch + 1)))
                        ts[m, 2 * q, *at] = high
                        ts[m, 2 * q + 1, *at] = low
            for q in range(2):
                zs[m, q] = right_mm(2 + q, ts[m, 2 * q], ts[m, 2 * q + 1])

        def project(i, _):
            at = pl.ds(pl.multiple_of(i * 16, 16), 16)
            for q in range(2):
                z = [[zs[m, q, at, 128 * ch : 128 * (ch + 1)] for ch in range(2)] for m in range(2)]
                amp = z[0][0] ** 2 + z[0][1] ** 2 + z[1][0] ** 2 + z[1][1] ** 2
                factor = spat[slot, at, 128 * q : 128 * (q + 1)] * lax.rsqrt(jnp.maximum(amp, 0.0625))
                for m in range(2):
                    for ch in range(2):
                        high, low = split(z[m][ch] * factor)
                        ts[m, 2 * q, at, 128 * ch : 128 * (ch + 1)] = high
                        ts[m, 2 * q + 1, at, 128 * ch : 128 * (ch + 1)] = low
            return 0

        lax.fori_loop(0, 16, project, 0, unroll=True)

        for m in range(2):
            a = right_mm(0, ts[m, 0], ts[m, 1])
            b = right_mm(1, ts[m, 2], ts[m, 3])
            for half, v in enumerate((a + b, a - b)):
                high, low = split(v)
                for k in range(2):
                    for ch in range(2):
                        at = (slice(128 * ch, 128 * (ch + 1)), slice(128 * half, 128 * (half + 1)))
                        pick = (slice(128 * k, 128 * (k + 1)), slice(128 * ch, 128 * (ch + 1)))
                        xs[m, 2 * k, *at] = high[pick]
                        xs[m, 2 * k + 1, *at] = low[pick]
            u = left_mm(2, xs[m, 0], xs[m, 1])
            v = left_mm(3, xs[m, 2], xs[m, 3])
            for ch in range(2):
                at = slice(128 * ch, 128 * (ch + 1))
                rev[m, ch, 0:128, :] = u[at] + v[at]
                rev[m, ch, 128:256, :] = u[at] - v[at]

        tile_g, shift_g = left // 128, lax.rem(left, 128)
        keep = lax.broadcasted_iota(jnp.int32, (STEP, 128), 1) >= shift_g

        def fold(x):
            return sum(x[8 * k : 8 * (k + 1)] for k in range(STEP // 8))

        def finish(i, acc):
            at = pl.ds(pl.multiple_of(i * STEP, STEP), STEP)
            dst = pl.ds(top + 8 + i * STEP, STEP)
            g = []
            acc = list(acc)
            for j in range(2):
                cols = slice(128 * j, 128 * (j + 1))
                o_re = patch[0, j, pl.ds(i * STEP + 8, STEP), :]
                o_im = patch[1, j, pl.ds(i * STEP + 8, STEP), :]
                w = power[j, at, :]
                g_re, g_im = -w * o_re, -w * o_im
                for m in range(2):
                    p_re, p_im = probe[m, 0, at, cols], probe[m, 1, at, cols]
                    v_re, v_im = rev[m, 0, at, cols], rev[m, 1, at, cols]
                    g_re += p_re * v_re + p_im * v_im
                    g_im += p_re * v_im - p_im * v_re
                    probe_out[2 * m, j, at, :] += o_re * v_re + o_im * v_im
                    probe_out[2 * m + 1, j, at, :] += o_re * v_im - o_im * v_re
                probe_out[4, j, at, :] += o_re * o_re + o_im * o_im
                d_re = 0.5 * (
                    patch[0, j, pl.ds(i * STEP + 9, STEP), :] - patch[0, j, pl.ds(i * STEP + 7, STEP), :]
                )
                d_im = 0.5 * (
                    patch[1, j, pl.ds(i * STEP + 9, STEP), :] - patch[1, j, pl.ds(i * STEP + 7, STEP), :]
                )
                s_re = slope[0, j, pl.ds(i * STEP + 8, STEP), :]
                s_im = slope[1, j, pl.ds(i * STEP + 8, STEP), :]
                acc[0] += fold(g_re * d_re + g_im * d_im)
                acc[1] += fold(w * (d_re * d_re + d_im * d_im))
                acc[2] += fold(g_re * s_re + g_im * s_im)
                acc[3] += fold(w * (s_re * s_re + s_im * s_im))
                g.append((g_re, g_im))
            for ch in range(2):
                a, b = turn(g[0][ch], shift_g), turn(g[1][ch], shift_g)
                grad[ch, tile_g, dst, :] += jnp.where(keep, a, 0.0)
                grad[ch, tile_g + 1, dst, :] += jnp.where(keep, b, a)
                grad[ch, tile_g + 2, dst, :] += jnp.where(keep, 0.0, b)
            return tuple(acc)

        acc = lax.fori_loop(0, WIN // STEP, finish, (zero,) * 4, unroll=2)
        total = [jnp.sum(acc[k], axis=(0, 1), keepdims=True) for k in range(4)]
        at_row = lax.broadcasted_iota(jnp.int32, (8, 128), 0) == slot
        for k in range(2):
            value = total[2 * k] * lax.rsqrt(total[2 * k + 1] + 1e-6)
            raw[...] += jnp.where(at_row & (lane == k), value, 0.0)
        return 0

    lax.fori_loop(0, where[4, 0, 2 * CAP], visit, 0)


def slots(where, ext, probe, spat, tables):
    v = pl.BlockSpec(memory_space=VMEM)
    return pl.pallas_call(
        slots_kernel,
        out_shape=(
            jax.ShapeDtypeStruct((2, 5, EXT_ROWS, 128), f32),
            jax.ShapeDtypeStruct((TILE, TILE), f32),
            jax.ShapeDtypeStruct((5, 2, WIN, 128), f32),
            jax.ShapeDtypeStruct((8, 128), f32),
        ),
        in_specs=[pl.BlockSpec(memory_space=pltpu.SMEM), v, v, v, v],
        out_specs=[v, v, v, v],
        scratch_shapes=[
            VMEM((2, 2, 272, 128), f32),
            VMEM((2, 2, 272, 128), f32),
            VMEM((2, 4, WIN, WIN), bf16),
            VMEM((2, 4, WIN, WIN), bf16),
            VMEM((2, 2, WIN, WIN), f32),
            VMEM((2, 2, WIN, WIN), f32),
            VMEM((2, WIN, 128), f32),
            VMEM((8, 904, 128), f32),
        ],
        compiler_params=pltpu.CompilerParams(vmem_limit_bytes=24 * 2**20),
        name="slots",
    )(where, ext, probe, spat, tables)


SHARDS = 32
SHARD = 80
PIECE = SHARD + 8


def plane(dx, dy):
    r, c = lax.axis_index("row"), lax.axis_index("col")
    return (lax.rem(r + 4 * dx, 16), lax.rem(c + 4 * dy, 16))


def depth_of():
    r, c = lax.axis_index("row"), lax.axis_index("col")
    return 4 * lax.rem(r // 2, 2) + lax.rem(c, 4)


def along(dz):
    r, c = lax.axis_index("row"), lax.axis_index("col")
    z = lax.rem(depth_of() + dz, 8)
    return (r // 4 * 4 + z // 4 * 2 + lax.rem(r, 2), c // 4 * 4 + lax.rem(z, 4))


def sums_kernel(
    grad,
    weight,
    obj,
    probe,
    part,
    raw,
    obj_new,
    probe_new,
    step,
    mate_rows,
    corner_in,
    row_out,
    row_in,
    side_out,
    side_in,
    mine,
    mate_part,
    plane_part,
    deep,
    deep_part,
    deep_all,
    all_sum,
    flat,
    hsend,
    hrecv,
    csend,
    crecv,
    psend,
    precv,
    zsend,
    zrecv,
):
    r, c = lax.axis_index("row"), lax.axis_index("col")
    n_row, n_col = lax.axis_size("row"), lax.axis_size("col")
    core = lax.rem(r, 2)
    own = r // 4 * 4 + c // 4
    z = depth_of()
    mate = (r + 1 - 2 * core, c)
    beyond = (lax.rem(r - 1 + 2 * core + n_row, n_row), c)
    left, right = neighbour((0, -1)), neighbour((0, 1))
    planes = [(dx, dy) for dx in range(4) for dy in range(4) if (dx, dy) != (0, 0)]

    barrier = pltpu.get_barrier_semaphore()
    partners = [left, right, mate, beyond]
    partners += [plane(*p) for p in planes] + [along(d) for d in range(1, 8)]
    for partner in partners:
        pl.semaphore_signal(barrier, inc=1, device_id=partner, device_id_type=MESH)

    def gather(i, _):
        mine[i, 0:SHARD, :] = part[pl.ds(pl.multiple_of(i * SHARD, SHARD), SHARD), :]
        mine[i, SHARD:PIECE, :] = raw[...]
        return 0

    lax.fori_loop(0, SHARDS, gather, 0)
    pl.semaphore_wait(barrier, len(partners))

    outer_from = pl.multiple_of(8 + 512 * core, 8)
    inner_from = pl.multiple_of(520 - 512 * core, 8)
    outer_to = pl.multiple_of(256 * core, 8)
    inner_to = pl.multiple_of(256 - 256 * core, 8)
    col_ok = [c > 0, c < n_col - 1]
    outer_ok = jnp.where(core == 0, r, n_row - 1 - r) > 0

    rows_to_mate = send(
        grad.at[:, :, pl.ds(inner_from, 128), :], mate_rows, csend.at[2], crecv.at[2], mate
    )
    half = SHARDS // 2
    to_mate = send(
        mine.at[pl.ds(half * (1 - core), half)], mate_part, csend.at[0], crecv.at[0], mate
    )
    edge = pl.ds(outer_from, 128)
    corners = [
        send(grad.at[:, 4, edge, :], corner_in.at[0], hsend.at[0], hrecv.at[0], right),
        send(grad.at[:, 0, edge, :], corner_in.at[1], hsend.at[1], hrecv.at[1], left),
    ]

    rows_to_mate.wait()
    for k, tile in enumerate((4, 0)):
        for ch in range(2):
            side_out[k, ch] = grad[ch, tile, 136:520, :]
            side_out[k, ch, pl.ds(inner_to, 128), :] += mate_rows[ch, tile]

    def send_sides(ch):
        return [
            send(side_out.at[k, ch], side_in.at[k, ch], hsend.at[2 + 2 * k + ch], hrecv.at[2 + 2 * k + ch], to)
            for k, to in enumerate((right, left))
        ]

    sides = send_sides(0)
    to_mate.wait()

    def add_mate(i, _):
        mine[half * core + i] += mate_part[i]
        return 0

    lax.fori_loop(0, half, add_mate, 0)
    copies = []
    for i, (dx, dy) in enumerate(planes):
        to = plane(dx, dy)
        owner = to[0] // 4 * 4 + to[1] // 4
        copies.append(
            send(mine.at[half * core + owner], plane_part.at[i], psend.at[i], precv.at[i], to)
        )
    for copy in corners:
        copy.wait()
    for ch in range(2):
        for t in range(3):
            v = grad[ch, 1 + t, edge, :]
            if t == 0:
                v = v + jnp.where(col_ok[0], corner_in[0, ch], 0.0)
            if t == 2:
                v = v + jnp.where(col_ok[1], corner_in[1, ch], 0.0)
            row_out[ch, t] = v
    for copy in copies:
        copy.wait()
    total = mine[half * core + own]
    for i in range(15):
        total = total + plane_part[i]
    deep[0:PIECE, :] = total
    deep[PIECE:128, :] = jnp.zeros((128 - PIECE, 128), f32)
    copies = []
    for d in range(1, 8):
        there = lax.rem(z + d, 8)
        copies.append(
            send(
                deep.at[pl.ds(pl.multiple_of(there * 16, 16), 16)],
                deep_part.at[d - 1],
                zsend.at[d - 1],
                zrecv.at[d - 1],
                along(d),
            )
        )
    for copy in copies:
        copy.wait()
    total = deep[pl.ds(pl.multiple_of(z * 16, 16), 16), :]
    for d in range(7):
        total = total + deep_part[d]
    here = deep_all.at[pl.ds(pl.multiple_of(z * 16, 16), 16)]
    deep_all[pl.ds(pl.multiple_of(z * 16, 16), 16), :] = total
    copies = [send(here, here, zsend.at[6 + d], zrecv.at[6 + d], along(d)) for d in range(1, 8)]
    strip = send(row_out, row_in, hsend.at[6], hrecv.at[6], beyond)
    sides += send_sides(1)
    for copy in copies:
        copy.wait()
    all_sum[half * core + own] = deep_all[0:PIECE, :]
    block = all_sum.at[half * core + own]
    copies = [
        send(block, block, psend.at[15 + i], precv.at[15 + i], plane(*p)) for i, p in enumerate(planes)
    ]
    for copy in copies:
        copy.wait()
    block = all_sum.at[pl.ds(half * core, half)]
    to_mate = send(block, block, csend.at[1], crecv.at[1], mate)

    def peak(i, top):
        rows = pl.ds(pl.multiple_of(i * 8, 8), 8)
        power = probe[0, 0, rows, :] ** 2 + probe[0, 1, rows, :] ** 2
        power = power + probe[1, 0, rows, :] ** 2 + probe[1, 1, rows, :] ** 2
        return jnp.maximum(top, power)

    top = lax.fori_loop(0, WIN // 8, peak, jnp.zeros((8, WIN), f32))
    floor = 0.1 * jnp.max(top, axis=(0, 1), keepdims=True)

    to_mate.wait()

    def spread(i, _):
        flat[pl.ds(pl.multiple_of(i * SHARD, SHARD), SHARD), :] = all_sum[i, 0:SHARD, :]
        return 0

    lax.fori_loop(0, SHARDS, spread, 0)

    def peak_sum(i, top):
        return jnp.maximum(top, flat[pl.ds(pl.multiple_of(2048 + i * 8, 8), 8), :])

    top = lax.fori_loop(0, 64, peak_sum, jnp.zeros((8, 128), f32))
    floor_p = 0.1 * jnp.max(top, axis=(0, 1), keepdims=True)

    def renew(i, _):
        rows = pl.ds(pl.multiple_of(i * 8, 8), 8)
        for j in range(2):
            cols = slice(128 * j, 128 * (j + 1))

            def at(k):
                return flat[pl.ds(pl.multiple_of((2 * k + j) * WIN + i * 8, 8), 8), :]

            wp = at(4)
            scale = 1.0 / (wp + floor_p)
            for m in range(2):
                for ch in range(2):
                    old = probe[m, ch, rows, cols]
                    probe_new[m, ch, rows, cols] = old + (at(2 * m + ch) - old * wp) * scale
        return 0

    lax.fori_loop(0, WIN // 8, renew, 0)

    rows8 = lax.broadcasted_iota(jnp.int32, (8, 128), 0)
    lanes8 = lax.broadcasted_iota(jnp.int32, (8, 128), 1)
    is_count = (rows8 == 7) & (lanes8 == 2)
    sums = all_sum[0, SHARD:PIECE, :]
    count = jnp.sum(jnp.where(is_count, sums, 0.0), axis=(0, 1), keepdims=True)
    mine_count = jnp.sum(jnp.where(is_count, raw[...], 0.0), axis=(0, 1), keepdims=True)
    mean = jnp.sum(sums, axis=0, keepdims=True) / count
    step[...] = jnp.where(rows8.astype(f32) < mine_count, raw[...] - mean, 0.0)

    for copy in sides:
        copy.wait()
    strip.wait()
    for band, start in ((0, outer_to), (1, 128), (2, inner_to)):

        def update(i, _, band=band, start=start):
            rows = pl.ds(pl.multiple_of(start + i * 8, 8), 8)
            thin = pl.ds(pl.multiple_of(i * 8, 8), 8)
            for t in range(3):
                cols = slice(128 * t, 128 * (t + 1))
                down = weight[rows, cols] + floor
                for ch in range(2):
                    g = grad[ch, 1 + t, pl.ds(pl.multiple_of(136 + start + i * 8, 8), 8), :]
                    if band == 0:
                        g = g + jnp.where(outer_ok, row_in[ch, t, thin, :], 0.0)
                    if band == 2:
                        g = g + mate_rows[ch, 1 + t, thin, :]
                    if t == 0:
                        g = g + jnp.where(col_ok[0], side_in[0, ch, rows, :], 0.0)
                    if t == 2:
                        g = g + jnp.where(col_ok[1], side_in[1, ch, rows, :], 0.0)
                    obj_new[ch, rows, cols] = obj[ch, rows, cols] + g / down
            return 0

        lax.fori_loop(0, 16, update, 0, unroll=2)


def sums(grad, weight, obj, probe, part, raw):
    v = pl.BlockSpec(memory_space=VMEM)
    dma = pltpu.SemaphoreType.DMA
    return pl.pallas_call(
        sums_kernel,
        out_shape=(
            jax.ShapeDtypeStruct((2, TILE, TILE), f32),
            jax.ShapeDtypeStruct((2, 2, WIN, WIN), f32),
            jax.ShapeDtypeStruct((8, 128), f32),
        ),
        in_specs=[v] * 6,
        out_specs=[v] * 3,
        scratch_shapes=[
            VMEM((2, 5, 128, 128), f32),
            VMEM((2, 2, 128, 128), f32),
            VMEM((2, 3, 128, 128), f32),
            VMEM((2, 3, 128, 128), f32),
            VMEM((2, 2, TILE, 128), f32),
            VMEM((2, 2, TILE, 128), f32),
            VMEM((SHARDS, PIECE, 128), f32),
            VMEM((SHARDS // 2, PIECE, 128), f32),
            VMEM((15, PIECE, 128), f32),
            VMEM((128, 128), f32),
            VMEM((7, 16, 128), f32),
            VMEM((128, 128), f32),
            VMEM((SHARDS, PIECE, 128), f32),
            VMEM((SHARDS * SHARD, 128), f32),
            dma((7,)),
            dma((7,)),
            dma((3,)),
            dma((3,)),
            dma((30,)),
            dma((30,)),
            dma((14,)),
            dma((14,)),
        ],
        compiler_params=pltpu.CompilerParams(
            collective_id=1, has_side_effects=True, vmem_limit_bytes=28 * 2**20
        ),
        name="sums",
    )(grad, weight, obj, probe, part, raw)


def on_device(object_field, probe, patterns, positions, counts):
    meta = jnp.concatenate([positions.reshape(1, 2 * CAP), counts.reshape(1, 1)], axis=1)
    meta = jnp.pad(meta, ((0, 7), (0, 128 - 2 * CAP - 1)))
    ext, spat, where = halo(object_field, patterns[0, 0], meta, jnp.asarray(order_table()))
    grad, weight, part, raw = slots(where, ext, probe, spat, jnp.asarray(dft_tables()))
    object_new, probe_new, step = sums(
        grad, weight, object_field, probe, part.reshape(SHARDS * SHARD, 128), raw
    )
    return object_new, probe_new, step[:CAP, :2].reshape(1, 1, CAP, 2)


def solution(mesh):
    placed = (
        P(None, "row", "col"),
        P(),
        P("row", "col", None, None, None),
        P("row", "col", None, None),
        P("row", "col"),
    )
    return jax.shard_map(
        on_device,
        mesh=mesh,
        in_specs=placed,
        out_specs=(P(None, "row", "col"), P(), P("row", "col", None, None)),
        check_vma=False,
    )
```

```python
import functools

import jax
import jax.numpy as jnp
import ml_dtypes
import numpy as np
from jax import lax
from jax.experimental import pallas as pl
from jax.experimental.pallas import tpu as pltpu
from jax.sharding import PartitionSpec as P

MESH = pl.DeviceIdType.MESH
VMEM = pltpu.VMEM
f32 = jnp.float32
bf16 = jnp.bfloat16

WIN = 256
HALF = 128
TILE = 384
CAP = 6
STEP = 32
EXT_ROWS = 8 + HALF + TILE + HALF + 8
OFFSETS = [(-1, 0), (1, 0), (0, -1), (0, 1), (-1, -1), (-1, 1), (1, -1), (1, 1)]


def dft_tables():
    k = np.arange(HALF)
    even = np.exp(-2j * np.pi * np.outer(2 * k, k) / WIN) / np.sqrt(WIN)
    odd = np.exp(-2j * np.pi * np.outer(2 * k + 1, k) / WIN) / np.sqrt(WIN)

    def block(z):
        return np.block([[z.real, -z.imag], [z.imag, z.real]])

    out = []
    for mat in (block(even), block(odd), block(even).T, block(odd).T):
        high = mat.astype(np.float32).astype(ml_dtypes.bfloat16)
        low = (mat - high.astype(np.float64)).astype(np.float32).astype(ml_dtypes.bfloat16)
        out += [high, low]
    return np.stack(out)


def order_table():
    table = np.zeros((WIN, WIN), np.float32)
    k = np.arange(HALF)
    table[2 * k, k] = 1
    table[2 * k + 1, HALF + k] = 1
    return table.astype(ml_dtypes.bfloat16)


def split(x):
    high = x.astype(bf16)
    return high, (x - high.astype(f32)).astype(bf16)


def mm(a, b):
    return jnp.dot(a, b, preferred_element_type=f32)


def neighbour(step):
    n_row, n_col = lax.axis_size("row"), lax.axis_size("col")
    r, c = lax.axis_index("row"), lax.axis_index("col")
    return (lax.rem(r + step[0] + n_row, n_row), lax.rem(c + step[1] + n_col, n_col))


def greet():
    barrier = pltpu.get_barrier_semaphore()
    for step in OFFSETS:
        pl.semaphore_signal(barrier, inc=1, device_id=neighbour(step), device_id_type=MESH)
    pl.semaphore_wait(barrier, len(OFFSETS))


def send(src, dst, ssem, rsem, to):
    copy = pltpu.make_async_remote_copy(
        src_ref=src, dst_ref=dst, send_sem=ssem, recv_sem=rsem, device_id=to, device_id_type=MESH
    )
    copy.start()
    return copy


def halo_kernel(
    obj, pats_far, meta, order, ext, spat, metas, pats, turned, lsem, ssem, rsem, msend, mrecv
):
    core = lax.rem(lax.axis_index("row"), 2)
    load = pltpu.make_async_copy(pats_far, pats, lsem)
    load.start()
    greet()
    for t in range(3):
        for ch in range(2):
            ext[ch, 1 + t, 136:520, :] = obj[ch, :, 128 * t : 128 * (t + 1)]
    metas[4] = meta[...]

    def strip(tile, tiles, row, rows):
        return ext.at[:, pl.ds(tile, tiles), pl.ds(row, rows), :]

    tops = [
        send(strip(1, 3, 136, 128), strip(1, 3, 520, 128), ssem.at[0], rsem.at[0], neighbour((-1, 0))),
        send(strip(1, 3, 392, 128), strip(1, 3, 8, 128), ssem.at[1], rsem.at[1], neighbour((1, 0))),
    ]
    left, right = neighbour((0, -1)), neighbour((0, 1))
    sides = [
        send(strip(1, 1, 136, 384), strip(4, 1, 136, 384), ssem.at[4], rsem.at[4], left),
        send(strip(3, 1, 136, 384), strip(0, 1, 136, 384), ssem.at[5], rsem.at[5], right),
    ]
    small = [
        send(
            metas.at[4],
            metas.at[(1 - dr) * 3 + 1 - dc],
            msend.at[i],
            mrecv.at[i],
            neighbour((dr, dc)),
        )
        for i, (dr, dc) in enumerate(OFFSETS)
    ]

    load.wait()

    def reorder(slot, _):
        high, low = split(jnp.sqrt(pats[slot]))
        sorted_cols = mm(high, order[...]) + mm(low, order[...])
        for j in range(2):
            turned[j] = sorted_cols[:, 128 * j : 128 * (j + 1)]
        for parity in range(2):
            for j in range(2):
                spat[slot, 128 * parity : 128 * (parity + 1), 128 * j : 128 * (j + 1)] = turned[
                    j, pl.ds(parity, 128, stride=2), :
                ]
        return 0

    lax.fori_loop(0, CAP, reorder, 0)
    for copy in tops:
        copy.wait()
    outer = pl.multiple_of(8 + 512 * core, 8)
    far = [
        send(strip(1, 1, outer, 128), strip(4, 1, outer, 128), ssem.at[2], rsem.at[2], left),
        send(strip(3, 1, outer, 128), strip(0, 1, outer, 128), ssem.at[3], rsem.at[3], right),
    ]
    mate = (lax.axis_index("row") + 1 - 2 * core, lax.axis_index("col"))
    near = pl.multiple_of(392 - 256 * core, 8)
    for k, tile in enumerate((4, 0)):
        sides[k].wait()
        far.append(
            send(strip(tile, 1, near, 128), strip(tile, 1, outer, 128), ssem.at[6 + k], rsem.at[6 + k], mate)
        )
    for copy in far + small:
        copy.wait()
    r, c = lax.axis_index("row"), lax.axis_index("col")
    for ch in range(2):
        for t in range(5):
            ext[ch, t, 0:8, :] = jnp.zeros((8, 128), f32)
            ext[ch, t, 648:656, :] = jnp.zeros((8, 128), f32)

    @pl.when(r == 0)
    def _():
        ext[:, :, 8:136, :] = jnp.zeros((2, 5, 128, 128), f32)

    @pl.when(r == lax.axis_size("row") - 1)
    def _():
        ext[:, :, 520:648, :] = jnp.zeros((2, 5, 128, 128), f32)

    @pl.when(c == 0)
    def _():
        ext[:, 0, 8:648, :] = jnp.zeros((2, 640, 128), f32)

    @pl.when(c == lax.axis_size("col") - 1)
    def _():
        ext[:, 4, 8:648, :] = jnp.zeros((2, 640, 128), f32)


def halo(obj, pats, meta, order):
    return pl.pallas_call(
        halo_kernel,
        out_shape=(
            jax.ShapeDtypeStruct((2, 5, EXT_ROWS, 128), f32),
            jax.ShapeDtypeStruct((CAP, WIN, WIN), f32),
            jax.ShapeDtypeStruct((9, 8, 128), jnp.int32),
        ),
        in_specs=[
            pl.BlockSpec(memory_space=VMEM),
            pl.BlockSpec(memory_space=pl.ANY),
            pl.BlockSpec(memory_space=VMEM),
            pl.BlockSpec(memory_space=VMEM),
        ],
        out_specs=[pl.BlockSpec(memory_space=VMEM)] * 3,
        scratch_shapes=[
            VMEM((CAP, WIN, WIN), f32),
            VMEM((2, WIN, 128), f32),
            pltpu.SemaphoreType.DMA,
            pltpu.SemaphoreType.DMA((8,)),
            pltpu.SemaphoreType.DMA((8,)),
            pltpu.SemaphoreType.DMA((8,)),
            pltpu.SemaphoreType.DMA((8,)),
        ],
        compiler_params=pltpu.CompilerParams(
            collective_id=0, has_side_effects=True, vmem_limit_bytes=20 * 2**20
        ),
        name="halo_in",
    )(obj, pats, meta, order)


def turn(x, shift):
    return pltpu.roll(x, shift, 1)


def slots_kernel(
    where,
    ext,
    probe,
    spat,
    tables_far,
    grad,
    weight,
    probe_out,
    raw,
    patch,
    slope,
    xs,
    ts,
    zs,
    rev,
    power,
    canvas,
    tables,
    lsem,
):
    load = pltpu.make_async_copy(tables_far, tables, lsem)
    load.start()
    r, c = lax.axis_index("row"), lax.axis_index("col")
    row_start, col_start = r * TILE, c * TILE
    lane = lax.broadcasted_iota(jnp.int32, (8, 128), 1)
    zero = jnp.zeros((8, 128), f32)

    def clear(ref, lead, rows):
        def step(i, _):
            for ix in lead:
                ref[(*ix, pl.ds(pl.multiple_of(i * 8, 8), 8), slice(None))] = zero
            return 0

        lax.fori_loop(0, rows // 8, step, 0, unroll=2)

    clear(grad, [(ch, t) for ch in range(2) for t in range(5)], EXT_ROWS)
    clear(probe_out, [(i, t) for i in range(5) for t in range(2)], WIN)
    for t in range(3):
        canvas[2 + t, WIN : WIN + TILE, :] = jnp.zeros((TILE, 128), f32)
    raw[...] = jnp.where(
        (lax.broadcasted_iota(jnp.int32, (8, 128), 0) == 7) & (lane == 2),
        where[4, 0, 2 * CAP].astype(f32),
        0.0,
    )

    def fill_power(i, _):
        rows = pl.ds(pl.multiple_of(i * 8, 8), 8)
        for j in range(2):
            cols = slice(128 * j, 128 * (j + 1))
            power[j, rows, :] = (
                probe[0, 0, rows, cols] ** 2
                + probe[0, 1, rows, cols] ** 2
                + probe[1, 0, rows, cols] ** 2
                + probe[1, 1, rows, cols] ** 2
            )
        return 0

    lax.fori_loop(0, WIN // 8, fill_power, 0, unroll=4)

    for j in range(9):
        jr, jc = j // 3 - 1, j % 3 - 1
        inside = (r + jr >= 0) & (r + jr < lax.axis_size("row")) & (c + jc >= 0) & (c + jc < lax.axis_size("col"))
        live = jnp.where(inside, where[j, 0, 2 * CAP], 0)

        def place(slot, _, j=j):
            top = where[j, 0, 2 * slot] - row_start
            left = where[j, 0, 2 * slot + 1] - col_start

            @pl.when((top > -WIN) & (top < TILE) & (left > -WIN) & (left < TILE))
            def _():
                at = left + WIN
                tile, shift = at // 128, lax.rem(at, 128)
                keep = lax.broadcasted_iota(jnp.int32, (32, 128), 1) >= shift

                def rows_step(i, _):
                    src = pl.ds(pl.multiple_of(i * 32, 32), 32)
                    dst = pl.ds(top + WIN + i * 32, 32)
                    a, b = turn(power[0, src, :], shift), turn(power[1, src, :], shift)
                    canvas[tile, dst, :] += jnp.where(keep, a, 0.0)
                    canvas[tile + 1, dst, :] += jnp.where(keep, b, a)
                    canvas[tile + 2, dst, :] += jnp.where(keep, 0.0, b)
                    return 0

                lax.fori_loop(jnp.maximum(-top, 0) // 32, (jnp.minimum(TILE - top, WIN) + 31) // 32, rows_step, 0)

            return 0

        lax.fori_loop(0, live, place, 0)

    for t in range(3):
        weight[:, 128 * t : 128 * (t + 1)] = canvas[2 + t, pl.ds(WIN, TILE), :]

    load.wait()

    def visit(slot, _):
        top = where[4, 0, 2 * slot] - row_start + HALF
        left = where[4, 0, 2 * slot + 1] - col_start + HALF

        base = left - 1
        tile, shift = base // 128, lax.rem(base, 128)
        last = jnp.minimum(tile + 3, 4)
        apart = lax.broadcasted_iota(jnp.int32, (512, 256), 0) - lax.broadcasted_iota(
            jnp.int32, (512, 256), 1
        )
        move = jnp.where(apart == shift + 1, 1.0, 0.0).astype(bf16)
        differ = jnp.where(apart == shift + 2, 0.5, jnp.where(apart == shift, -0.5, 0.0)).astype(bf16)
        shifter = jnp.concatenate([move, differ], axis=1)
        for ch in range(2):
            x = [ext[ch, t, pl.ds(top, 272), :] for t in (tile, tile + 1, tile + 2, last)]
            high, low = split(jnp.concatenate(x, axis=1))
            y = mm(high, shifter) + mm(low, shifter)
            for j in range(2):
                patch[ch, j] = y[:, 128 * j : 128 * (j + 1)]
                slope[ch, j] = y[:, 256 + 128 * j : 256 + 128 * (j + 1)]

        def leave(i, _):
            rows = [pl.multiple_of(i * 16 + 128 * h, 16) for h in range(2)]
            for j in range(2):
                cols = slice(128 * j, 128 * (j + 1))
                o = [[patch[ch, j, pl.ds(rw + 8, 16), :] for ch in range(2)] for rw in rows]
                for m in range(2):
                    e = []
                    for h in range(2):
                        pr = probe[m, 0, pl.ds(rows[h], 16), cols]
                        pi = probe[m, 1, pl.ds(rows[h], 16), cols]
                        e.append((pr * o[h][0] - pi * o[h][1], pr * o[h][1] + pi * o[h][0]))
                    for ch in range(2):
                        at = pl.ds(pl.multiple_of(i * 16 + 128 * ch, 16), 16)
                        for k, v in enumerate((e[0][ch] + e[1][ch], e[0][ch] - e[1][ch])):
                            high, low = split(v)
                            xs[m, 2 * k, at, cols] = high
                            xs[m, 2 * k + 1, at, cols] = low
            return 0

        lax.fori_loop(0, 8, leave, 0, unroll=True)

        def left_mm(k, high, low):
            return mm(tables[2 * k], high) + mm(tables[2 * k], low) + mm(tables[2 * k + 1], high)

        def right_mm(k, high, low):
            return mm(high, tables[2 * k]) + mm(low, tables[2 * k]) + mm(high, tables[2 * k + 1])

        for m in range(2):
            for k in range(2):
                y = left_mm(k, xs[m, 2 * k], xs[m, 2 * k + 1])
                for ch in range(2):
                    a, b = y[128 * ch : 128 * (ch + 1), :128], y[128 * ch : 128 * (ch + 1), 128:]
                    for q, v in enumerate((a + b, a - b)):
                        high, low = split(v)
                        at = (slice(128 * k, 128 * (k + 1)), slice(128 * ch, 128 * (ch + 1)))
                        ts[m, 2 * q, *at] = high
                        ts[m, 2 * q + 1, *at] = low
        for q in range(2):
            y = right_mm(2 + q, ts[:, 2 * q].reshape(512, 256), ts[:, 2 * q + 1].reshape(512, 256))
            for m in range(2):
                zs[m, q] = y[256 * m : 256 * (m + 1)]

        def project(i, _):
            at = pl.ds(pl.multiple_of(i * 16, 16), 16)
            for q in range(2):
                z = [[zs[m, q, at, 128 * ch : 128 * (ch + 1)] for ch in range(2)] for m in range(2)]
                amp = z[0][0] ** 2 + z[0][1] ** 2 + z[1][0] ** 2 + z[1][1] ** 2
                factor = spat[slot, at, 128 * q : 128 * (q + 1)] * lax.rsqrt(jnp.maximum(amp, 0.0625))
                for m in range(2):
                    for ch in range(2):
                        high, low = split(z[m][ch] * factor)
                        ts[m, 2 * q, at, 128 * ch : 128 * (ch + 1)] = high
                        ts[m, 2 * q + 1, at, 128 * ch : 128 * (ch + 1)] = low
            return 0

        lax.fori_loop(0, 16, project, 0, unroll=True)

        both_a = right_mm(0, ts[:, 0].reshape(512, 256), ts[:, 1].reshape(512, 256))
        both_b = right_mm(1, ts[:, 2].reshape(512, 256), ts[:, 3].reshape(512, 256))
        for m in range(2):
            a = both_a[256 * m : 256 * (m + 1)]
            b = both_b[256 * m : 256 * (m + 1)]
            for half, v in enumerate((a + b, a - b)):
                high, low = split(v)
                for k in range(2):
                    for ch in range(2):
                        at = (slice(128 * ch, 128 * (ch + 1)), slice(128 * half, 128 * (half + 1)))
                        pick = (slice(128 * k, 128 * (k + 1)), slice(128 * ch, 128 * (ch + 1)))
                        xs[m, 2 * k, *at] = high[pick]
                        xs[m, 2 * k + 1, *at] = low[pick]
            u = left_mm(2, xs[m, 0], xs[m, 1])
            v = left_mm(3, xs[m, 2], xs[m, 3])
            for ch in range(2):
                at = slice(128 * ch, 128 * (ch + 1))
                rev[m, ch, 0:128, :] = u[at] + v[at]
                rev[m, ch, 128:256, :] = u[at] - v[at]

        tile_g, shift_g = left // 128, lax.rem(left, 128)
        keep = lax.broadcasted_iota(jnp.int32, (STEP, 128), 1) >= shift_g

        def fold(x):
            return sum(x[8 * k : 8 * (k + 1)] for k in range(STEP // 8))

        def finish(i, acc):
            at = pl.ds(pl.multiple_of(i * STEP, STEP), STEP)
            dst = pl.ds(top + 8 + i * STEP, STEP)
            g = []
            acc = list(acc)
            for j in range(2):
                cols = slice(128 * j, 128 * (j + 1))
                o_re = patch[0, j, pl.ds(i * STEP + 8, STEP), :]
                o_im = patch[1, j, pl.ds(i * STEP + 8, STEP), :]
                w = power[j, at, :]
                g_re, g_im = -w * o_re, -w * o_im
                for m in range(2):
                    p_re, p_im = probe[m, 0, at, cols], probe[m, 1, at, cols]
                    v_re, v_im = rev[m, 0, at, cols], rev[m, 1, at, cols]
                    g_re += p_re * v_re + p_im * v_im
                    g_im += p_re * v_im - p_im * v_re
                    probe_out[2 * m, j, at, :] += o_re * v_re + o_im * v_im
                    probe_out[2 * m + 1, j, at, :] += o_re * v_im - o_im * v_re
                probe_out[4, j, at, :] += o_re * o_re + o_im * o_im
                d_re = 0.5 * (
                    patch[0, j, pl.ds(i * STEP + 9, STEP), :] - patch[0, j, pl.ds(i * STEP + 7, STEP), :]
                )
                d_im = 0.5 * (
                    patch[1, j, pl.ds(i * STEP + 9, STEP), :] - patch[1, j, pl.ds(i * STEP + 7, STEP), :]
                )
                s_re = slope[0, j, pl.ds(i * STEP + 8, STEP), :]
                s_im = slope[1, j, pl.ds(i * STEP + 8, STEP), :]
                acc[0] += fold(g_re * d_re + g_im * d_im)
                acc[1] += fold(w * (d_re * d_re + d_im * d_im))
                acc[2] += fold(g_re * s_re + g_im * s_im)
                acc[3] += fold(w * (s_re * s_re + s_im * s_im))
                g.append((g_re, g_im))
            for ch in range(2):
                a, b = turn(g[0][ch], shift_g), turn(g[1][ch], shift_g)
                grad[ch, tile_g, dst, :] += jnp.where(keep, a, 0.0)
                grad[ch, tile_g + 1, dst, :] += jnp.where(keep, b, a)
                grad[ch, tile_g + 2, dst, :] += jnp.where(keep, 0.0, b)
            return tuple(acc)

        acc = lax.fori_loop(0, WIN // STEP, finish, (zero,) * 4, unroll=True)
        total = [jnp.sum(acc[k], axis=(0, 1), keepdims=True) for k in range(4)]
        at_row = lax.broadcasted_iota(jnp.int32, (8, 128), 0) == slot
        for k in range(2):
            value = total[2 * k] * lax.rsqrt(total[2 * k + 1] + 1e-6)
            raw[...] += jnp.where(at_row & (lane == k), value, 0.0)
        return 0

    lax.fori_loop(0, where[4, 0, 2 * CAP], visit, 0)


def slots(where, ext, probe, spat, tables):
    v = pl.BlockSpec(memory_space=VMEM)
    return pl.pallas_call(
        slots_kernel,
        out_shape=(
            jax.ShapeDtypeStruct((2, 5, EXT_ROWS, 128), f32),
            jax.ShapeDtypeStruct((TILE, TILE), f32),
            jax.ShapeDtypeStruct((5, 2, WIN, 128), f32),
            jax.ShapeDtypeStruct((8, 128), f32),
        ),
        in_specs=[pl.BlockSpec(memory_space=pltpu.SMEM), v, v, v, pl.BlockSpec(memory_space=pl.ANY)],
        out_specs=[v, v, v, v],
        scratch_shapes=[
            VMEM((2, 2, 272, 128), f32),
            VMEM((2, 2, 272, 128), f32),
            VMEM((2, 4, WIN, WIN), bf16),
            VMEM((2, 4, WIN, WIN), bf16),
            VMEM((2, 2, WIN, WIN), f32),
            VMEM((2, 2, WIN, WIN), f32),
            VMEM((2, WIN, 128), f32),
            VMEM((8, 904, 128), f32),
            VMEM((8, WIN, WIN), bf16),
            pltpu.SemaphoreType.DMA,
        ],
        compiler_params=pltpu.CompilerParams(vmem_limit_bytes=24 * 2**20),
        name="slots",
    )(where, ext, probe, spat, tables)


SHARDS = 32
SHARD = 80
PIECE = SHARD + 8


def plane(dx, dy):
    r, c = lax.axis_index("row"), lax.axis_index("col")
    return (lax.rem(r + 4 * dx, 16), lax.rem(c + 4 * dy, 16))


def depth_of():
    r, c = lax.axis_index("row"), lax.axis_index("col")
    return 4 * lax.rem(r // 2, 2) + lax.rem(c, 4)


def along(dz):
    r, c = lax.axis_index("row"), lax.axis_index("col")
    z = lax.rem(depth_of() + dz, 8)
    return (r // 4 * 4 + z // 4 * 2 + lax.rem(r, 2), c // 4 * 4 + lax.rem(z, 4))


def sums_kernel(
    grad,
    weight,
    obj,
    probe,
    part,
    raw,
    obj_new,
    probe_new,
    step,
    mate_rows,
    corner_in,
    row_out,
    row_in,
    side_out,
    side_in,
    mine,
    mate_part,
    plane_part,
    deep,
    deep_part,
    deep_all,
    all_sum,
    flat,
    hsend,
    hrecv,
    csend,
    crecv,
    psend,
    precv,
    zsend,
    zrecv,
):
    r, c = lax.axis_index("row"), lax.axis_index("col")
    n_row, n_col = lax.axis_size("row"), lax.axis_size("col")
    core = lax.rem(r, 2)
    own = r // 4 * 4 + c // 4
    z = depth_of()
    mate = (r + 1 - 2 * core, c)
    beyond = (lax.rem(r - 1 + 2 * core + n_row, n_row), c)
    left, right = neighbour((0, -1)), neighbour((0, 1))
    planes = [(dx, dy) for dx in range(4) for dy in range(4) if (dx, dy) != (0, 0)]

    barrier = pltpu.get_barrier_semaphore()
    partners = [left, right, mate, beyond]
    partners += [plane(*p) for p in planes] + [along(d) for d in range(1, 8)]
    for partner in partners:
        pl.semaphore_signal(barrier, inc=1, device_id=partner, device_id_type=MESH)

    def gather(i, _):
        mine[i, 0:SHARD, :] = part[pl.ds(pl.multiple_of(i * SHARD, SHARD), SHARD), :]
        mine[i, SHARD:PIECE, :] = raw[...]
        return 0

    lax.fori_loop(0, SHARDS, gather, 0)
    pl.semaphore_wait(barrier, len(partners))

    outer_from = pl.multiple_of(8 + 512 * core, 8)
    inner_from = pl.multiple_of(520 - 512 * core, 8)
    outer_to = pl.multiple_of(256 * core, 8)
    inner_to = pl.multiple_of(256 - 256 * core, 8)
    col_ok = [c > 0, c < n_col - 1]
    outer_ok = jnp.where(core == 0, r, n_row - 1 - r) > 0

    rows_to_mate = send(
        grad.at[:, :, pl.ds(inner_from, 128), :], mate_rows, csend.at[2], crecv.at[2], mate
    )
    half = SHARDS // 2
    to_mate = send(
        mine.at[pl.ds(half * (1 - core), half)], mate_part, csend.at[0], crecv.at[0], mate
    )
    edge = pl.ds(outer_from, 128)
    corners = [
        send(grad.at[:, 4, edge, :], corner_in.at[0], hsend.at[0], hrecv.at[0], right),
        send(grad.at[:, 0, edge, :], corner_in.at[1], hsend.at[1], hrecv.at[1], left),
    ]

    rows_to_mate.wait()
    def fill_sides(ch):
        for k, tile in enumerate((4, 0)):
            side_out[k, ch] = grad[ch, tile, 136:520, :]
            side_out[k, ch, pl.ds(inner_to, 128), :] += mate_rows[ch, tile]

    def send_side(ch, k):
        i = 2 + 2 * k + ch
        return send(side_out.at[k, ch], side_in.at[k, ch], hsend.at[i], hrecv.at[i], (right, left)[k])

    fill_sides(0)
    sides = [send_side(0, 0), send_side(0, 1)]
    to_mate.wait()

    def add_mate(i, _):
        mine[half * core + i] += mate_part[i]
        return 0

    lax.fori_loop(0, half, add_mate, 0)
    copies = []
    for i, (dx, dy) in enumerate(planes):
        to = plane(dx, dy)
        owner = to[0] // 4 * 4 + to[1] // 4
        copies.append(
            send(mine.at[half * core + owner], plane_part.at[i], psend.at[i], precv.at[i], to)
        )
    fill_sides(1)
    for copy in corners:
        copy.wait()
    for ch in range(2):
        for t in range(3):
            v = grad[ch, 1 + t, edge, :]
            if t == 0:
                v = v + jnp.where(col_ok[0], corner_in[0, ch], 0.0)
            if t == 2:
                v = v + jnp.where(col_ok[1], corner_in[1, ch], 0.0)
            row_out[ch, t] = v
    for copy in copies:
        copy.wait()
    total = mine[half * core + own]
    for i in range(15):
        total = total + plane_part[i]
    deep[0:PIECE, :] = total
    deep[PIECE:128, :] = jnp.zeros((128 - PIECE, 128), f32)
    copies = []
    for d in range(1, 8):
        there = lax.rem(z + d, 8)
        copies.append(
            send(
                deep.at[pl.ds(pl.multiple_of(there * 16, 16), 16)],
                deep_part.at[d - 1],
                zsend.at[d - 1],
                zrecv.at[d - 1],
                along(d),
            )
        )
    sides.append(send_side(1, 0))
    for copy in copies:
        copy.wait()
    total = deep[pl.ds(pl.multiple_of(z * 16, 16), 16), :]
    for d in range(7):
        total = total + deep_part[d]
    here = deep_all.at[pl.ds(pl.multiple_of(z * 16, 16), 16)]
    deep_all[pl.ds(pl.multiple_of(z * 16, 16), 16), :] = total
    copies = [send(here, here, zsend.at[6 + d], zrecv.at[6 + d], along(d)) for d in range(1, 8)]
    sides.append(send_side(1, 1))
    strip = send(row_out, row_in, hsend.at[6], hrecv.at[6], beyond)
    for copy in copies:
        copy.wait()
    all_sum[half * core + own] = deep_all[0:PIECE, :]
    block = all_sum.at[half * core + own]
    copies = [
        send(block, block, psend.at[15 + i], precv.at[15 + i], plane(*p)) for i, p in enumerate(planes)
    ]
    for copy in copies:
        copy.wait()
    block = all_sum.at[pl.ds(half * core, half)]
    to_mate = send(block, block, csend.at[1], crecv.at[1], mate)

    def peak(i, top):
        rows = pl.ds(pl.multiple_of(i * 8, 8), 8)
        power = probe[0, 0, rows, :] ** 2 + probe[0, 1, rows, :] ** 2
        power = power + probe[1, 0, rows, :] ** 2 + probe[1, 1, rows, :] ** 2
        return jnp.maximum(top, power)

    top = lax.fori_loop(0, WIN // 8, peak, jnp.zeros((8, WIN), f32))
    floor = 0.1 * jnp.max(top, axis=(0, 1), keepdims=True)

    to_mate.wait()

    def spread(i, _):
        flat[pl.ds(pl.multiple_of(i * SHARD, SHARD), SHARD), :] = all_sum[i, 0:SHARD, :]
        return 0

    lax.fori_loop(0, SHARDS, spread, 0)

    def peak_sum(i, top):
        return jnp.maximum(top, flat[pl.ds(pl.multiple_of(2048 + i * 8, 8), 8), :])

    top = lax.fori_loop(0, 64, peak_sum, jnp.zeros((8, 128), f32))
    floor_p = 0.1 * jnp.max(top, axis=(0, 1), keepdims=True)

    def renew(i, _):
        rows = pl.ds(pl.multiple_of(i * 8, 8), 8)
        for j in range(2):
            cols = slice(128 * j, 128 * (j + 1))

            def at(k):
                return flat[pl.ds(pl.multiple_of((2 * k + j) * WIN + i * 8, 8), 8), :]

            wp = at(4)
            scale = 1.0 / (wp + floor_p)
            for m in range(2):
                for ch in range(2):
                    old = probe[m, ch, rows, cols]
                    probe_new[m, ch, rows, cols] = old + (at(2 * m + ch) - old * wp) * scale
        return 0

    lax.fori_loop(0, WIN // 8, renew, 0)

    rows8 = lax.broadcasted_iota(jnp.int32, (8, 128), 0)
    lanes8 = lax.broadcasted_iota(jnp.int32, (8, 128), 1)
    is_count = (rows8 == 7) & (lanes8 == 2)
    sums = all_sum[0, SHARD:PIECE, :]
    count = jnp.sum(jnp.where(is_count, sums, 0.0), axis=(0, 1), keepdims=True)
    mine_count = jnp.sum(jnp.where(is_count, raw[...], 0.0), axis=(0, 1), keepdims=True)
    mean = jnp.sum(sums, axis=0, keepdims=True) / count
    step[...] = jnp.where(rows8.astype(f32) < mine_count, raw[...] - mean, 0.0)

    for copy in sides:
        copy.wait()
    for band, start in ((1, 128), (2, inner_to), (0, outer_to)):
        if band == 0:
            strip.wait()

        def update(i, _, band=band, start=start):
            rows = pl.ds(pl.multiple_of(start + i * 8, 8), 8)
            thin = pl.ds(pl.multiple_of(i * 8, 8), 8)
            for t in range(3):
                cols = slice(128 * t, 128 * (t + 1))
                down = weight[rows, cols] + floor
                for ch in range(2):
                    g = grad[ch, 1 + t, pl.ds(pl.multiple_of(136 + start + i * 8, 8), 8), :]
                    if band == 0:
                        g = g + jnp.where(outer_ok, row_in[ch, t, thin, :], 0.0)
                    if band == 2:
                        g = g + mate_rows[ch, 1 + t, thin, :]
                    if t == 0:
                        g = g + jnp.where(col_ok[0], side_in[0, ch, rows, :], 0.0)
                    if t == 2:
                        g = g + jnp.where(col_ok[1], side_in[1, ch, rows, :], 0.0)
                    obj_new[ch, rows, cols] = obj[ch, rows, cols] + g / down
            return 0

        lax.fori_loop(0, 16, update, 0, unroll=2)


def sums(grad, weight, obj, probe, part, raw):
    v = pl.BlockSpec(memory_space=VMEM)
    dma = pltpu.SemaphoreType.DMA
    return pl.pallas_call(
        sums_kernel,
        out_shape=(
            jax.ShapeDtypeStruct((2, TILE, TILE), f32),
            jax.ShapeDtypeStruct((2, 2, WIN, WIN), f32),
            jax.ShapeDtypeStruct((8, 128), f32),
        ),
        in_specs=[v] * 6,
        out_specs=[v] * 3,
        scratch_shapes=[
            VMEM((2, 5, 128, 128), f32),
            VMEM((2, 2, 128, 128), f32),
            VMEM((2, 3, 128, 128), f32),
            VMEM((2, 3, 128, 128), f32),
            VMEM((2, 2, TILE, 128), f32),
            VMEM((2, 2, TILE, 128), f32),
            VMEM((SHARDS, PIECE, 128), f32),
            VMEM((SHARDS // 2, PIECE, 128), f32),
            VMEM((15, PIECE, 128), f32),
            VMEM((128, 128), f32),
            VMEM((7, 16, 128), f32),
            VMEM((128, 128), f32),
            VMEM((SHARDS, PIECE, 128), f32),
            VMEM((SHARDS * SHARD, 128), f32),
            dma((7,)),
            dma((7,)),
            dma((3,)),
            dma((3,)),
            dma((30,)),
            dma((30,)),
            dma((14,)),
            dma((14,)),
        ],
        compiler_params=pltpu.CompilerParams(
            collective_id=1, has_side_effects=True, vmem_limit_bytes=28 * 2**20
        ),
        name="sums",
    )(grad, weight, obj, probe, part, raw)


def on_device(object_field, probe, patterns, positions, counts):
    meta = jnp.concatenate([positions.reshape(1, 2 * CAP), counts.reshape(1, 1)], axis=1)
    meta = jnp.pad(meta, ((0, 7), (0, 128 - 2 * CAP - 1)))
    ext, spat, where = halo(object_field, patterns[0, 0], meta, jnp.asarray(order_table()))
    grad, weight, part, raw = slots(where, ext, probe, spat, jnp.asarray(dft_tables()))
    object_new, probe_new, step = sums(
        grad, weight, object_field, probe, part.reshape(SHARDS * SHARD, 128), raw
    )
    return object_new, probe_new, step[:CAP, :2].reshape(1, 1, CAP, 2)


def solution(mesh):
    placed = (
        P(None, "row", "col"),
        P(),
        P("row", "col", None, None, None),
        P("row", "col", None, None),
        P("row", "col"),
    )
    return jax.shard_map(
        on_device,
        mesh=mesh,
        in_specs=placed,
        out_specs=(P(None, "row", "col"), P(), P("row", "col", None, None)),
        check_vma=False,
    )
```

```python
import functools

import jax
import jax.numpy as jnp
import ml_dtypes
import numpy as np
from jax import lax
from jax.experimental import pallas as pl
from jax.experimental.pallas import tpu as pltpu
from jax.sharding import PartitionSpec as P

MESH = pl.DeviceIdType.MESH
VMEM = pltpu.VMEM
f32 = jnp.float32
bf16 = jnp.bfloat16

WIN = 256
HALF = 128
TILE = 384
CAP = 6
STEP = 32
EXT_ROWS = 8 + HALF + TILE + HALF + 8
OFFSETS = [(-1, 0), (1, 0), (0, -1), (0, 1), (-1, -1), (-1, 1), (1, -1), (1, 1)]


def dft_tables():
    k = np.arange(HALF)
    even = np.exp(-2j * np.pi * np.outer(2 * k, k) / WIN) / np.sqrt(WIN)
    odd = np.exp(-2j * np.pi * np.outer(2 * k + 1, k) / WIN) / np.sqrt(WIN)

    def block(z):
        return np.block([[z.real, -z.imag], [z.imag, z.real]])

    out = []
    for mat in (block(even), block(odd), block(even).T, block(odd).T):
        high = mat.astype(np.float32).astype(ml_dtypes.bfloat16)
        low = (mat - high.astype(np.float64)).astype(np.float32).astype(ml_dtypes.bfloat16)
        out += [high, low]
    return np.stack(out)


def order_table():
    table = np.zeros((WIN, WIN), np.float32)
    k = np.arange(HALF)
    table[2 * k, k] = 1
    table[2 * k + 1, HALF + k] = 1
    return table.astype(ml_dtypes.bfloat16)


def split(x):
    high = x.astype(bf16)
    return high, (x - high.astype(f32)).astype(bf16)


def mm(a, b):
    return jnp.dot(a, b, preferred_element_type=f32)


def neighbour(step):
    n_row, n_col = lax.axis_size("row"), lax.axis_size("col")
    r, c = lax.axis_index("row"), lax.axis_index("col")
    return (lax.rem(r + step[0] + n_row, n_row), lax.rem(c + step[1] + n_col, n_col))


def greet():
    barrier = pltpu.get_barrier_semaphore()
    for step in OFFSETS:
        pl.semaphore_signal(barrier, inc=1, device_id=neighbour(step), device_id_type=MESH)
    pl.semaphore_wait(barrier, len(OFFSETS))


def send(src, dst, ssem, rsem, to):
    copy = pltpu.make_async_remote_copy(
        src_ref=src, dst_ref=dst, send_sem=ssem, recv_sem=rsem, device_id=to, device_id_type=MESH
    )
    copy.start()
    return copy


def halo_kernel(
    obj, pats_far, meta, order, ext, spat, metas, pats, turned, lsem, ssem, rsem, msend, mrecv
):
    core = lax.rem(lax.axis_index("row"), 2)
    load = pltpu.make_async_copy(pats_far, pats, lsem)
    load.start()
    greet()
    for t in range(3):
        for ch in range(2):
            ext[ch, 1 + t, 136:520, :] = obj[ch, :, 128 * t : 128 * (t + 1)]
    metas[4] = meta[...]

    def strip(tile, tiles, row, rows):
        return ext.at[:, pl.ds(tile, tiles), pl.ds(row, rows), :]

    tops = [
        send(strip(1, 3, 136, 128), strip(1, 3, 520, 128), ssem.at[0], rsem.at[0], neighbour((-1, 0))),
        send(strip(1, 3, 392, 128), strip(1, 3, 8, 128), ssem.at[1], rsem.at[1], neighbour((1, 0))),
    ]
    left, right = neighbour((0, -1)), neighbour((0, 1))
    sides = [
        send(strip(1, 1, 136, 384), strip(4, 1, 136, 384), ssem.at[4], rsem.at[4], left),
        send(strip(3, 1, 136, 384), strip(0, 1, 136, 384), ssem.at[5], rsem.at[5], right),
    ]
    small = [
        send(
            metas.at[4],
            metas.at[(1 - dr) * 3 + 1 - dc],
            msend.at[i],
            mrecv.at[i],
            neighbour((dr, dc)),
        )
        for i, (dr, dc) in enumerate(OFFSETS)
    ]

    load.wait()

    def reorder(slot, _):
        high, low = split(jnp.sqrt(pats[slot]))
        sorted_cols = mm(high, order[...]) + mm(low, order[...])
        for j in range(2):
            turned[j] = sorted_cols[:, 128 * j : 128 * (j + 1)]
        for parity in range(2):
            for j in range(2):
                spat[slot, 128 * parity : 128 * (parity + 1), 128 * j : 128 * (j + 1)] = turned[
                    j, pl.ds(parity, 128, stride=2), :
                ]
        return 0

    lax.fori_loop(0, CAP, reorder, 0)
    for copy in tops:
        copy.wait()
    outer = pl.multiple_of(8 + 512 * core, 8)
    far = [
        send(strip(1, 1, outer, 128), strip(4, 1, outer, 128), ssem.at[2], rsem.at[2], left),
        send(strip(3, 1, outer, 128), strip(0, 1, outer, 128), ssem.at[3], rsem.at[3], right),
    ]
    mate = (lax.axis_index("row") + 1 - 2 * core, lax.axis_index("col"))
    near = pl.multiple_of(392 - 256 * core, 8)
    for k, tile in enumerate((4, 0)):
        sides[k].wait()
        far.append(
            send(strip(tile, 1, near, 128), strip(tile, 1, outer, 128), ssem.at[6 + k], rsem.at[6 + k], mate)
        )
    for copy in far + small:
        copy.wait()
    r, c = lax.axis_index("row"), lax.axis_index("col")
    for ch in range(2):
        for t in range(5):
            ext[ch, t, 0:8, :] = jnp.zeros((8, 128), f32)
            ext[ch, t, 648:656, :] = jnp.zeros((8, 128), f32)

    @pl.when(r == 0)
    def _():
        ext[:, :, 8:136, :] = jnp.zeros((2, 5, 128, 128), f32)

    @pl.when(r == lax.axis_size("row") - 1)
    def _():
        ext[:, :, 520:648, :] = jnp.zeros((2, 5, 128, 128), f32)

    @pl.when(c == 0)
    def _():
        ext[:, 0, 8:648, :] = jnp.zeros((2, 640, 128), f32)

    @pl.when(c == lax.axis_size("col") - 1)
    def _():
        ext[:, 4, 8:648, :] = jnp.zeros((2, 640, 128), f32)


def halo(obj, pats, meta, order):
    return pl.pallas_call(
        halo_kernel,
        out_shape=(
            jax.ShapeDtypeStruct((2, 5, EXT_ROWS, 128), f32),
            jax.ShapeDtypeStruct((CAP, WIN, WIN), f32),
            jax.ShapeDtypeStruct((9, 8, 128), jnp.int32),
        ),
        in_specs=[
            pl.BlockSpec(memory_space=VMEM),
            pl.BlockSpec(memory_space=pltpu.HBM),
            pl.BlockSpec(memory_space=VMEM),
            pl.BlockSpec(memory_space=VMEM),
        ],
        out_specs=[pl.BlockSpec(memory_space=VMEM)] * 3,
        scratch_shapes=[
            VMEM((CAP, WIN, WIN), f32),
            VMEM((2, WIN, 128), f32),
            pltpu.SemaphoreType.DMA,
            pltpu.SemaphoreType.DMA((8,)),
            pltpu.SemaphoreType.DMA((8,)),
            pltpu.SemaphoreType.DMA((8,)),
            pltpu.SemaphoreType.DMA((8,)),
        ],
        compiler_params=pltpu.CompilerParams(
            collective_id=0, has_side_effects=True, vmem_limit_bytes=20 * 2**20
        ),
        name="halo_in",
    )(obj, pats, meta, order)


def turn(x, shift):
    return pltpu.roll(x, shift, 1)


def slots_kernel(
    where,
    ext,
    probe,
    spat,
    tables_far,
    grad,
    weight,
    probe_out,
    raw,
    patch,
    slope,
    xs,
    ts,
    zs,
    rev,
    power,
    canvas,
    tables,
    lsem,
):
    load = pltpu.make_async_copy(tables_far, tables, lsem)
    load.start()
    r, c = lax.axis_index("row"), lax.axis_index("col")
    row_start, col_start = r * TILE, c * TILE
    lane = lax.broadcasted_iota(jnp.int32, (8, 128), 1)
    zero = jnp.zeros((8, 128), f32)

    def clear(ref, lead, rows):
        def step(i, _):
            for ix in lead:
                ref[(*ix, pl.ds(pl.multiple_of(i * 8, 8), 8), slice(None))] = zero
            return 0

        lax.fori_loop(0, rows // 8, step, 0, unroll=2)

    clear(grad, [(ch, t) for ch in range(2) for t in range(5)], EXT_ROWS)
    clear(probe_out, [(i, t) for i in range(5) for t in range(2)], WIN)
    for t in range(3):
        canvas[2 + t, WIN : WIN + TILE, :] = jnp.zeros((TILE, 128), f32)
    raw[...] = jnp.where(
        (lax.broadcasted_iota(jnp.int32, (8, 128), 0) == 7) & (lane == 2),
        where[4, 0, 2 * CAP].astype(f32),
        0.0,
    )

    def fill_power(i, _):
        rows = pl.ds(pl.multiple_of(i * 8, 8), 8)
        for j in range(2):
            cols = slice(128 * j, 128 * (j + 1))
            power[j, rows, :] = (
                probe[0, 0, rows, cols] ** 2
                + probe[0, 1, rows, cols] ** 2
                + probe[1, 0, rows, cols] ** 2
                + probe[1, 1, rows, cols] ** 2
            )
        return 0

    lax.fori_loop(0, WIN // 8, fill_power, 0, unroll=4)

    for j in (0, 1, 2, 3, 5, 6, 7, 8):
        jr, jc = j // 3 - 1, j % 3 - 1
        inside = (r + jr >= 0) & (r + jr < lax.axis_size("row")) & (c + jc >= 0) & (c + jc < lax.axis_size("col"))
        live = jnp.where(inside, where[j, 0, 2 * CAP], 0)

        def place(slot, _, j=j):
            top = where[j, 0, 2 * slot] - row_start
            left = where[j, 0, 2 * slot + 1] - col_start

            @pl.when((top > -WIN) & (top < TILE) & (left > -WIN) & (left < TILE))
            def _():
                at = left + WIN
                tile, shift = at // 128, lax.rem(at, 128)
                keep = lax.broadcasted_iota(jnp.int32, (32, 128), 1) >= shift
                begin = jnp.maximum(-top, 0) // 32
                end = (jnp.minimum(TILE - top, WIN) + 31) // 32
                for t in range(3):

                    @pl.when((tile + t >= 2) & (tile + t < 5))
                    def _(t=t):
                        def rows_step(i, _):
                            src = pl.ds(pl.multiple_of(i * 32, 32), 32)
                            a = turn(power[max(t - 1, 0), src, :], shift)
                            if t == 0:
                                v = jnp.where(keep, a, 0.0)
                            elif t == 1:
                                v = jnp.where(keep, turn(power[1, src, :], shift), a)
                            else:
                                v = jnp.where(keep, 0.0, a)
                            canvas[tile + t, pl.ds(top + WIN + i * 32, 32), :] += v
                            return 0

                        lax.fori_loop(begin, end, rows_step, 0)

            return 0

        lax.fori_loop(0, live, place, 0)

    load.wait()

    def visit(slot, _):
        top = where[4, 0, 2 * slot] - row_start + HALF
        left = where[4, 0, 2 * slot + 1] - col_start + HALF

        tile, shift = left // 128, lax.rem(left, 128)
        apart = lax.broadcasted_iota(jnp.int32, (256, 128), 0) - lax.broadcasted_iota(
            jnp.int32, (256, 128), 1
        )
        move = jnp.where(apart == shift, 1.0, 0.0).astype(bf16)
        differ = jnp.where(apart == shift + 1, 0.5, jnp.where(apart == shift - 1, -0.5, 0.0)).astype(bf16)
        shifter = jnp.concatenate([move, differ], axis=1)
        for ch in range(2):
            x = [split(ext[ch, tile + t, pl.ds(top, 272), :]) for t in range(3)]
            high, low = (
                jnp.concatenate(
                    [jnp.concatenate([x[j][p], x[j + 1][p]], axis=1) for j in range(2)], axis=0
                )
                for p in range(2)
            )
            y = mm(high, shifter) + mm(low, shifter)
            for j in range(2):
                patch[ch, j] = y[272 * j : 272 * (j + 1), :128]
                slope[ch, j] = y[272 * j : 272 * (j + 1), 128:]

        @pl.when(shift == 0)
        def _():
            first = lax.broadcasted_iota(jnp.int32, (272, 128), 1) == 0
            for ch in range(2):
                for j in range(2):
                    before = turn(ext[ch, tile + j - 1, pl.ds(top, 272), :], 1)
                    slope[ch, j] += jnp.where(first, -0.5 * before, 0.0)

        def leave(i, _):
            rows = [pl.multiple_of(i * 16 + 128 * h, 16) for h in range(2)]
            for j in range(2):
                cols = slice(128 * j, 128 * (j + 1))
                o = [[patch[ch, j, pl.ds(rw + 8, 16), :] for ch in range(2)] for rw in rows]
                for m in range(2):
                    e = []
                    for h in range(2):
                        pr = probe[m, 0, pl.ds(rows[h], 16), cols]
                        pi = probe[m, 1, pl.ds(rows[h], 16), cols]
                        e.append((pr * o[h][0] - pi * o[h][1], pr * o[h][1] + pi * o[h][0]))
                    for ch in range(2):
                        at = pl.ds(pl.multiple_of(i * 16 + 128 * ch, 16), 16)
                        for k, v in enumerate((e[0][ch] + e[1][ch], e[0][ch] - e[1][ch])):
                            high, low = split(v)
                            xs[m, 2 * k, at, cols] = high
                            xs[m, 2 * k + 1, at, cols] = low
            return 0

        lax.fori_loop(0, 8, leave, 0, unroll=True)

        def left_mm(k, high, low):
            return mm(tables[2 * k], high) + mm(tables[2 * k], low) + mm(tables[2 * k + 1], high)

        def right_mm(k, high, low):
            return mm(high, tables[2 * k]) + mm(low, tables[2 * k]) + mm(high, tables[2 * k + 1])

        for m in range(2):
            for k in range(2):
                y = left_mm(k, xs[m, 2 * k], xs[m, 2 * k + 1])
                for ch in range(2):
                    a, b = y[128 * ch : 128 * (ch + 1), :128], y[128 * ch : 128 * (ch + 1), 128:]
                    for q, v in enumerate((a + b, a - b)):
                        high, low = split(v)
                        at = (slice(128 * k, 128 * (k + 1)), slice(128 * ch, 128 * (ch + 1)))
                        ts[m, 2 * q, *at] = high
                        ts[m, 2 * q + 1, *at] = low
        for q in range(2):
            y = right_mm(2 + q, ts[:, 2 * q].reshape(512, 256), ts[:, 2 * q + 1].reshape(512, 256))
            for m in range(2):
                zs[m, q] = y[256 * m : 256 * (m + 1)]

        def project(i, _):
            at = pl.ds(pl.multiple_of(i * 16, 16), 16)
            for q in range(2):
                z = [[zs[m, q, at, 128 * ch : 128 * (ch + 1)] for ch in range(2)] for m in range(2)]
                amp = z[0][0] ** 2 + z[0][1] ** 2 + z[1][0] ** 2 + z[1][1] ** 2
                factor = spat[slot, at, 128 * q : 128 * (q + 1)] * lax.rsqrt(jnp.maximum(amp, 0.0625))
                for m in range(2):
                    for ch in range(2):
                        high, low = split(z[m][ch] * factor)
                        ts[m, 2 * q, at, 128 * ch : 128 * (ch + 1)] = high
                        ts[m, 2 * q + 1, at, 128 * ch : 128 * (ch + 1)] = low
            return 0

        lax.fori_loop(0, 16, project, 0, unroll=True)

        both_a = right_mm(0, ts[:, 0].reshape(512, 256), ts[:, 1].reshape(512, 256))
        both_b = right_mm(1, ts[:, 2].reshape(512, 256), ts[:, 3].reshape(512, 256))
        for m in range(2):
            a = both_a[256 * m : 256 * (m + 1)]
            b = both_b[256 * m : 256 * (m + 1)]
            for half, v in enumerate((a + b, a - b)):
                high, low = split(v)
                for k in range(2):
                    for ch in range(2):
                        at = (slice(128 * ch, 128 * (ch + 1)), slice(128 * half, 128 * (half + 1)))
                        pick = (slice(128 * k, 128 * (k + 1)), slice(128 * ch, 128 * (ch + 1)))
                        xs[m, 2 * k, *at] = high[pick]
                        xs[m, 2 * k + 1, *at] = low[pick]
            u = left_mm(2, xs[m, 0], xs[m, 1])
            v = left_mm(3, xs[m, 2], xs[m, 3])
            for ch in range(2):
                at = slice(128 * ch, 128 * (ch + 1))
                rev[m, ch, 0:128, :] = u[at] + v[at]
                rev[m, ch, 128:256, :] = u[at] - v[at]

        tile_g, shift_g = left // 128, lax.rem(left, 128)
        keep = lax.broadcasted_iota(jnp.int32, (STEP, 128), 1) >= shift_g

        def fold(x):
            return sum(x[8 * k : 8 * (k + 1)] for k in range(STEP // 8))

        def finish(i, acc):
            at = pl.ds(pl.multiple_of(i * STEP, STEP), STEP)
            dst = pl.ds(top + 8 + i * STEP, STEP)
            g = []
            acc = list(acc)
            for j in range(2):
                cols = slice(128 * j, 128 * (j + 1))
                o_re = patch[0, j, pl.ds(i * STEP + 8, STEP), :]
                o_im = patch[1, j, pl.ds(i * STEP + 8, STEP), :]
                w = power[j, at, :]
                g_re, g_im = -w * o_re, -w * o_im
                for m in range(2):
                    p_re, p_im = probe[m, 0, at, cols], probe[m, 1, at, cols]
                    v_re, v_im = rev[m, 0, at, cols], rev[m, 1, at, cols]
                    g_re += p_re * v_re + p_im * v_im
                    g_im += p_re * v_im - p_im * v_re
                    probe_out[2 * m, j, at, :] += o_re * v_re + o_im * v_im
                    probe_out[2 * m + 1, j, at, :] += o_re * v_im - o_im * v_re
                probe_out[4, j, at, :] += o_re * o_re + o_im * o_im
                d_re = 0.5 * (
                    patch[0, j, pl.ds(i * STEP + 9, STEP), :] - patch[0, j, pl.ds(i * STEP + 7, STEP), :]
                )
                d_im = 0.5 * (
                    patch[1, j, pl.ds(i * STEP + 9, STEP), :] - patch[1, j, pl.ds(i * STEP + 7, STEP), :]
                )
                s_re = slope[0, j, pl.ds(i * STEP + 8, STEP), :]
                s_im = slope[1, j, pl.ds(i * STEP + 8, STEP), :]
                acc[0] += fold(g_re * d_re + g_im * d_im)
                acc[1] += fold(w * (d_re * d_re + d_im * d_im))
                acc[2] += fold(g_re * s_re + g_im * s_im)
                acc[3] += fold(w * (s_re * s_re + s_im * s_im))
                g.append((g_re, g_im))
            for ch in range(2):
                a, b = turn(g[0][ch], shift_g), turn(g[1][ch], shift_g)
                grad[ch, tile_g, dst, :] += jnp.where(keep, a, 0.0)
                grad[ch, tile_g + 1, dst, :] += jnp.where(keep, b, a)
                grad[ch, tile_g + 2, dst, :] += jnp.where(keep, 0.0, b)
            a, b = turn(power[0, at, :], shift_g), turn(power[1, at, :], shift_g)
            dst = pl.ds(top + HALF + i * STEP, STEP)
            canvas[tile_g + 1, dst, :] += jnp.where(keep, a, 0.0)
            canvas[tile_g + 2, dst, :] += jnp.where(keep, b, a)
            canvas[tile_g + 3, dst, :] += jnp.where(keep, 0.0, b)
            return tuple(acc)

        acc = lax.fori_loop(0, WIN // STEP, finish, (zero,) * 4, unroll=True)
        total = [jnp.sum(acc[k], axis=(0, 1), keepdims=True) for k in range(4)]
        at_row = lax.broadcasted_iota(jnp.int32, (8, 128), 0) == slot
        for k in range(2):
            value = total[2 * k] * lax.rsqrt(total[2 * k + 1] + 1e-6)
            raw[...] += jnp.where(at_row & (lane == k), value, 0.0)
        return 0

    lax.fori_loop(0, where[4, 0, 2 * CAP], visit, 0)
    for t in range(3):
        weight[:, 128 * t : 128 * (t + 1)] = canvas[2 + t, pl.ds(WIN, TILE), :]


def slots(where, ext, probe, spat, tables):
    v = pl.BlockSpec(memory_space=VMEM)
    return pl.pallas_call(
        slots_kernel,
        out_shape=(
            jax.ShapeDtypeStruct((2, 5, EXT_ROWS, 128), f32),
            jax.ShapeDtypeStruct((TILE, TILE), f32),
            jax.ShapeDtypeStruct((5, 2, WIN, 128), f32),
            jax.ShapeDtypeStruct((8, 128), f32),
        ),
        in_specs=[pl.BlockSpec(memory_space=pltpu.SMEM), v, v, v, pl.BlockSpec(memory_space=pltpu.HBM)],
        out_specs=[v, v, v, v],
        scratch_shapes=[
            VMEM((2, 2, 272, 128), f32),
            VMEM((2, 2, 272, 128), f32),
            VMEM((2, 4, WIN, WIN), bf16),
            VMEM((2, 4, WIN, WIN), bf16),
            VMEM((2, 2, WIN, WIN), f32),
            VMEM((2, 2, WIN, WIN), f32),
            VMEM((2, WIN, 128), f32),
            VMEM((8, 904, 128), f32),
            VMEM((8, WIN, WIN), bf16),
            pltpu.SemaphoreType.DMA,
        ],
        compiler_params=pltpu.CompilerParams(vmem_limit_bytes=24 * 2**20),
        name="slots",
    )(where, ext, probe, spat, tables)


SHARDS = 32
SHARD = 80
PIECE = SHARD + 8


def plane(dx, dy):
    r, c = lax.axis_index("row"), lax.axis_index("col")
    return (lax.rem(r + 4 * dx, 16), lax.rem(c + 4 * dy, 16))


def depth_of():
    r, c = lax.axis_index("row"), lax.axis_index("col")
    return 4 * lax.rem(r // 2, 2) + lax.rem(c, 4)


def along(dz):
    r, c = lax.axis_index("row"), lax.axis_index("col")
    z = lax.rem(depth_of() + dz, 8)
    return (r // 4 * 4 + z // 4 * 2 + lax.rem(r, 2), c // 4 * 4 + lax.rem(z, 4))


def sums_kernel(
    grad,
    weight,
    obj,
    probe,
    part,
    raw,
    obj_new,
    probe_new,
    step,
    mate_rows,
    corner_in,
    row_out,
    row_in,
    side_out,
    side_in,
    mine,
    mate_part,
    plane_part,
    deep,
    deep_part,
    deep_all,
    all_sum,
    flat,
    hsend,
    hrecv,
    csend,
    crecv,
    psend,
    precv,
    zsend,
    zrecv,
):
    r, c = lax.axis_index("row"), lax.axis_index("col")
    n_row, n_col = lax.axis_size("row"), lax.axis_size("col")
    core = lax.rem(r, 2)
    own = r // 4 * 4 + c // 4
    z = depth_of()
    mate = (r + 1 - 2 * core, c)
    beyond = (lax.rem(r - 1 + 2 * core + n_row, n_row), c)
    left, right = neighbour((0, -1)), neighbour((0, 1))
    planes = [(dx, dy) for dx in range(4) for dy in range(4) if (dx, dy) != (0, 0)]

    barrier = pltpu.get_barrier_semaphore()
    partners = [left, right, mate, beyond]
    partners += [plane(*p) for p in planes] + [along(d) for d in range(1, 8)]
    for partner in partners:
        pl.semaphore_signal(barrier, inc=1, device_id=partner, device_id_type=MESH)

    def gather(i, _):
        mine[i, 0:SHARD, :] = part[pl.ds(pl.multiple_of(i * SHARD, SHARD), SHARD), :]
        mine[i, SHARD:PIECE, :] = raw[...]
        return 0

    lax.fori_loop(0, SHARDS, gather, 0)
    pl.semaphore_wait(barrier, len(partners))

    outer_from = pl.multiple_of(8 + 512 * core, 8)
    inner_from = pl.multiple_of(520 - 512 * core, 8)
    outer_to = pl.multiple_of(256 * core, 8)
    inner_to = pl.multiple_of(256 - 256 * core, 8)
    col_ok = [c > 0, c < n_col - 1]
    outer_ok = jnp.where(core == 0, r, n_row - 1 - r) > 0

    half = SHARDS // 2
    to_mate = send(
        mine.at[pl.ds(half * (1 - core), half)], mate_part, csend.at[0], crecv.at[0], mate
    )
    rows_to_mate = send(
        grad.at[:, :, pl.ds(inner_from, 128), :], mate_rows, csend.at[2], crecv.at[2], mate
    )
    edge = pl.ds(outer_from, 128)
    corners = [
        send(grad.at[:, 4, edge, :], corner_in.at[0], hsend.at[0], hrecv.at[0], right),
        send(grad.at[:, 0, edge, :], corner_in.at[1], hsend.at[1], hrecv.at[1], left),
    ]

    rows_to_mate.wait()
    def fill_sides(ch):
        for k, tile in enumerate((4, 0)):
            side_out[k, ch] = grad[ch, tile, 136:520, :]
            side_out[k, ch, pl.ds(inner_to, 128), :] += mate_rows[ch, tile]

    def send_side(ch, k):
        i = 2 + 2 * k + ch
        return send(side_out.at[k, ch], side_in.at[k, ch], hsend.at[i], hrecv.at[i], (right, left)[k])

    fill_sides(0)
    sides = [send_side(0, 0), send_side(0, 1)]
    to_mate.wait()

    def add_mate(i, _):
        mine[half * core + i] += mate_part[i]
        return 0

    lax.fori_loop(0, half, add_mate, 0)
    copies = []
    for i, (dx, dy) in enumerate(planes):
        to = plane(dx, dy)
        owner = to[0] // 4 * 4 + to[1] // 4
        copies.append(
            send(mine.at[half * core + owner], plane_part.at[i], psend.at[i], precv.at[i], to)
        )
    fill_sides(1)
    for copy in corners:
        copy.wait()
    for ch in range(2):
        for t in range(3):
            v = grad[ch, 1 + t, edge, :]
            if t == 0:
                v = v + jnp.where(col_ok[0], corner_in[0, ch], 0.0)
            if t == 2:
                v = v + jnp.where(col_ok[1], corner_in[1, ch], 0.0)
            row_out[ch, t] = v
    for copy in copies:
        copy.wait()
    total = mine[half * core + own]
    for i in range(15):
        total = total + plane_part[i]
    deep[0:PIECE, :] = total
    deep[PIECE:128, :] = jnp.zeros((128 - PIECE, 128), f32)
    copies = []
    for d in range(1, 8):
        there = lax.rem(z + d, 8)
        copies.append(
            send(
                deep.at[pl.ds(pl.multiple_of(there * 16, 16), 16)],
                deep_part.at[d - 1],
                zsend.at[d - 1],
                zrecv.at[d - 1],
                along(d),
            )
        )
    sides.append(send_side(1, 0))
    for copy in copies:
        copy.wait()
    total = deep[pl.ds(pl.multiple_of(z * 16, 16), 16), :]
    for d in range(7):
        total = total + deep_part[d]
    here = deep_all.at[pl.ds(pl.multiple_of(z * 16, 16), 16)]
    deep_all[pl.ds(pl.multiple_of(z * 16, 16), 16), :] = total
    copies = [send(here, here, zsend.at[6 + d], zrecv.at[6 + d], along(d)) for d in range(1, 8)]
    sides.append(send_side(1, 1))
    strip = send(row_out, row_in, hsend.at[6], hrecv.at[6], beyond)
    for copy in copies:
        copy.wait()
    all_sum[half * core + own] = deep_all[0:PIECE, :]
    block = all_sum.at[half * core + own]
    copies = [
        send(block, block, psend.at[15 + i], precv.at[15 + i], plane(*p)) for i, p in enumerate(planes)
    ]
    for copy in copies:
        copy.wait()
    block = all_sum.at[pl.ds(half * core, half)]
    to_mate = send(block, block, csend.at[1], crecv.at[1], mate)

    def peak(i, top):
        rows = pl.ds(pl.multiple_of(i * 8, 8), 8)
        power = probe[0, 0, rows, :] ** 2 + probe[0, 1, rows, :] ** 2
        power = power + probe[1, 0, rows, :] ** 2 + probe[1, 1, rows, :] ** 2
        return jnp.maximum(top, power)

    top = lax.fori_loop(0, WIN // 8, peak, jnp.zeros((8, WIN), f32))
    floor = 0.1 * jnp.max(top, axis=(0, 1), keepdims=True)

    to_mate.wait()

    def spread(i, _):
        flat[pl.ds(pl.multiple_of(i * SHARD, SHARD), SHARD), :] = all_sum[i, 0:SHARD, :]
        return 0

    lax.fori_loop(0, SHARDS, spread, 0)

    def peak_sum(i, top):
        return jnp.maximum(top, flat[pl.ds(pl.multiple_of(2048 + i * 8, 8), 8), :])

    top = lax.fori_loop(0, 64, peak_sum, jnp.zeros((8, 128), f32))
    floor_p = 0.1 * jnp.max(top, axis=(0, 1), keepdims=True)

    def renew(i, _):
        rows = pl.ds(pl.multiple_of(i * 8, 8), 8)
        for j in range(2):
            cols = slice(128 * j, 128 * (j + 1))

            def at(k):
                return flat[pl.ds(pl.multiple_of((2 * k + j) * WIN + i * 8, 8), 8), :]

            wp = at(4)
            scale = 1.0 / (wp + floor_p)
            for m in range(2):
                for ch in range(2):
                    old = probe[m, ch, rows, cols]
                    probe_new[m, ch, rows, cols] = old + (at(2 * m + ch) - old * wp) * scale
        return 0

    lax.fori_loop(0, WIN // 8, renew, 0)

    rows8 = lax.broadcasted_iota(jnp.int32, (8, 128), 0)
    lanes8 = lax.broadcasted_iota(jnp.int32, (8, 128), 1)
    is_count = (rows8 == 7) & (lanes8 == 2)
    sums = all_sum[0, SHARD:PIECE, :]
    count = jnp.sum(jnp.where(is_count, sums, 0.0), axis=(0, 1), keepdims=True)
    mine_count = jnp.sum(jnp.where(is_count, raw[...], 0.0), axis=(0, 1), keepdims=True)
    mean = jnp.sum(sums, axis=0, keepdims=True) / count
    step[...] = jnp.where(rows8.astype(f32) < mine_count, raw[...] - mean, 0.0)

    for copy in sides:
        copy.wait()
    for band, start in ((1, 128), (2, inner_to), (0, outer_to)):
        if band == 0:
            strip.wait()

        def update(i, _, band=band, start=start):
            rows = pl.ds(pl.multiple_of(start + i * 8, 8), 8)
            thin = pl.ds(pl.multiple_of(i * 8, 8), 8)
            for t in range(3):
                cols = slice(128 * t, 128 * (t + 1))
                down = weight[rows, cols] + floor
                for ch in range(2):
                    g = grad[ch, 1 + t, pl.ds(pl.multiple_of(136 + start + i * 8, 8), 8), :]
                    if band == 0:
                        g = g + jnp.where(outer_ok, row_in[ch, t, thin, :], 0.0)
                    if band == 2:
                        g = g + mate_rows[ch, 1 + t, thin, :]
                    if t == 0:
                        g = g + jnp.where(col_ok[0], side_in[0, ch, rows, :], 0.0)
                    if t == 2:
                        g = g + jnp.where(col_ok[1], side_in[1, ch, rows, :], 0.0)
                    obj_new[ch, rows, cols] = obj[ch, rows, cols] + g / down
            return 0

        lax.fori_loop(0, 16, update, 0, unroll=2)


def sums(grad, weight, obj, probe, part, raw):
    v = pl.BlockSpec(memory_space=VMEM)
    dma = pltpu.SemaphoreType.DMA
    return pl.pallas_call(
        sums_kernel,
        out_shape=(
            jax.ShapeDtypeStruct((2, TILE, TILE), f32),
            jax.ShapeDtypeStruct((2, 2, WIN, WIN), f32),
            jax.ShapeDtypeStruct((8, 128), f32),
        ),
        in_specs=[v] * 6,
        out_specs=[v] * 3,
        scratch_shapes=[
            VMEM((2, 5, 128, 128), f32),
            VMEM((2, 2, 128, 128), f32),
            VMEM((2, 3, 128, 128), f32),
            VMEM((2, 3, 128, 128), f32),
            VMEM((2, 2, TILE, 128), f32),
            VMEM((2, 2, TILE, 128), f32),
            VMEM((SHARDS, PIECE, 128), f32),
            VMEM((SHARDS // 2, PIECE, 128), f32),
            VMEM((15, PIECE, 128), f32),
            VMEM((128, 128), f32),
            VMEM((7, 16, 128), f32),
            VMEM((128, 128), f32),
            VMEM((SHARDS, PIECE, 128), f32),
            VMEM((SHARDS * SHARD, 128), f32),
            dma((7,)),
            dma((7,)),
            dma((3,)),
            dma((3,)),
            dma((30,)),
            dma((30,)),
            dma((14,)),
            dma((14,)),
        ],
        compiler_params=pltpu.CompilerParams(
            collective_id=1, has_side_effects=True, vmem_limit_bytes=28 * 2**20
        ),
        name="sums",
    )(grad, weight, obj, probe, part, raw)


def on_device(object_field, probe, patterns, positions, counts):
    meta = jnp.concatenate([positions.reshape(1, 2 * CAP), counts.reshape(1, 1)], axis=1)
    meta = jnp.pad(meta, ((0, 7), (0, 128 - 2 * CAP - 1)))
    ext, spat, where = halo(object_field, patterns[0, 0], meta, jnp.asarray(order_table()))
    grad, weight, part, raw = slots(where, ext, probe, spat, jnp.asarray(dft_tables()))
    object_new, probe_new, step = sums(
        grad, weight, object_field, probe, part.reshape(SHARDS * SHARD, 128), raw
    )
    return object_new, probe_new, step[:CAP, :2].reshape(1, 1, CAP, 2)


def solution(mesh):
    placed = (
        P(None, "row", "col"),
        P(),
        P("row", "col", None, None, None),
        P("row", "col", None, None),
        P("row", "col"),
    )
    return jax.shard_map(
        on_device,
        mesh=mesh,
        in_specs=placed,
        out_specs=(P(None, "row", "col"), P(), P("row", "col", None, None)),
        check_vma=False,
    )
```

```python
import functools

import jax
import jax.numpy as jnp
import ml_dtypes
import numpy as np
from jax import lax
from jax.experimental import pallas as pl
from jax.experimental.pallas import tpu as pltpu
from jax.sharding import PartitionSpec as P

MESH = pl.DeviceIdType.MESH
VMEM = pltpu.VMEM
f32 = jnp.float32
bf16 = jnp.bfloat16

WIN = 256
HALF = 128
TILE = 384
CAP = 6
STEP = 32
EXT_ROWS = 8 + HALF + TILE + HALF + 8
OFFSETS = [(-1, 0), (1, 0), (0, -1), (0, 1), (-1, -1), (-1, 1), (1, -1), (1, 1)]


def dft_tables():
    k = np.arange(HALF)
    even = np.exp(-2j * np.pi * np.outer(2 * k, k) / WIN) / np.sqrt(WIN)
    odd = np.exp(-2j * np.pi * np.outer(2 * k + 1, k) / WIN) / np.sqrt(WIN)

    def block(z):
        return np.block([[z.real, -z.imag], [z.imag, z.real]])

    out = []
    for mat in (block(even), block(odd), block(even).T, block(odd).T):
        high = mat.astype(np.float32).astype(ml_dtypes.bfloat16)
        low = (mat - high.astype(np.float64)).astype(np.float32).astype(ml_dtypes.bfloat16)
        out += [high, low]
    return np.stack(out)


def split(x):
    high = x.astype(bf16)
    return high, (x - high.astype(f32)).astype(bf16)


def mm(a, b):
    return jnp.dot(a, b, preferred_element_type=f32)


def neighbour(step):
    n_row, n_col = lax.axis_size("row"), lax.axis_size("col")
    r, c = lax.axis_index("row"), lax.axis_index("col")
    return (lax.rem(r + step[0] + n_row, n_row), lax.rem(c + step[1] + n_col, n_col))


def greet():
    barrier = pltpu.get_barrier_semaphore()
    for step in OFFSETS:
        pl.semaphore_signal(barrier, inc=1, device_id=neighbour(step), device_id_type=MESH)
    pl.semaphore_wait(barrier, len(OFFSETS))


def send(src, dst, ssem, rsem, to):
    copy = pltpu.make_async_remote_copy(
        src_ref=src, dst_ref=dst, send_sem=ssem, recv_sem=rsem, device_id=to, device_id_type=MESH
    )
    copy.start()
    return copy


def when(condition, act):
    @pl.when(condition)
    def _():
        act()


def finish_copy(copy, sent, received):
    when(sent, copy.wait_send)
    when(received, copy.wait_recv)


def make(src, dst, ssem, rsem, to):
    return pltpu.make_async_remote_copy(
        src_ref=src, dst_ref=dst, send_sem=ssem, recv_sem=rsem, device_id=to, device_id_type=MESH
    )


def halo_kernel(
    obj, pats_far, meta, ext, spat, metas, pats, turned, lsem, ssem, rsem, msend, mrecv
):
    r, c = lax.axis_index("row"), lax.axis_index("col")
    core = lax.rem(r, 2)
    load = pltpu.make_async_copy(pats_far, pats, lsem)
    load.start()
    has_up, has_down = r > 0, r < lax.axis_size("row") - 1
    has_left, has_right = c > 0, c < lax.axis_size("col") - 1

    for ch in range(2):
        for t in range(5):
            ext[ch, t, 0:8, :] = jnp.zeros((8, 128), f32)
            ext[ch, t, 648:656, :] = jnp.zeros((8, 128), f32)

    def blank(tiles, rows):
        ext[:, tiles, rows, :] = jnp.zeros((2, tiles.stop - tiles.start, rows.stop - rows.start, 128), f32)

    when(r == 0, lambda: blank(slice(0, 5), slice(8, 136)))
    when(jnp.logical_not(has_down), lambda: blank(slice(0, 5), slice(520, 648)))
    when(c == 0, lambda: blank(slice(0, 1), slice(8, 648)))
    when(jnp.logical_not(has_right), lambda: blank(slice(4, 5), slice(8, 648)))
    greet()
    for t in range(3):
        for ch in range(2):
            ext[ch, 1 + t, 136:520, :] = obj[ch, :, 128 * t : 128 * (t + 1)]
    metas[4] = meta[...]

    def strip(tile, tiles, row, rows):
        return ext.at[:, pl.ds(tile, tiles), pl.ds(row, rows), :]

    left, right = neighbour((0, -1)), neighbour((0, 1))
    outer = pl.multiple_of(8 + 512 * core, 8)
    up = make(strip(1, 3, 136, 128), strip(1, 3, 520, 128), ssem.at[0], rsem.at[0], neighbour((-1, 0)))
    down = make(strip(1, 3, 392, 128), strip(1, 3, 8, 128), ssem.at[1], rsem.at[1], neighbour((1, 0)))
    to_left = make(strip(1, 1, 136, 384), strip(4, 1, 136, 384), ssem.at[4], rsem.at[4], left)
    to_right = make(strip(3, 1, 136, 384), strip(0, 1, 136, 384), ssem.at[5], rsem.at[5], right)
    when(has_up, up.start)
    when(has_down, down.start)
    far_left, far_right = lax.rem(c, 4) == 0, lax.rem(c, 4) == 3
    when(has_left & far_left, to_left.start)
    when(has_right & far_right, to_right.start)
    small = [
        send(
            metas.at[4],
            metas.at[(1 - dr) * 3 + 1 - dc],
            msend.at[i],
            mrecv.at[i],
            neighbour((dr, dc)),
        )
        for i, (dr, dc) in enumerate(OFFSETS)
    ]
    when(has_left & jnp.logical_not(far_left), to_left.start)
    when(has_right & jnp.logical_not(far_right), to_right.start)
    load.wait()
    order = []
    for parity in range(2):
        index = lax.broadcasted_iota(jnp.int32, (WIN, HALF), 0)
        wanted = 2 * lax.broadcasted_iota(jnp.int32, (WIN, HALF), 1) + parity
        order.append(jnp.where(index == wanted, 1.0, 0.0).astype(bf16))
    order = jnp.concatenate(order, axis=1)

    def reorder(slot, _):
        high, low = split(jnp.sqrt(pats[slot]))
        sorted_cols = mm(high, order) + mm(low, order)
        for j in range(2):
            turned[j] = sorted_cols[:, 128 * j : 128 * (j + 1)]
        for parity in range(2):
            for j in range(2):
                spat[slot, 128 * parity : 128 * (parity + 1), 128 * j : 128 * (j + 1)] = turned[
                    j, pl.ds(parity, 128, stride=2), :
                ]
        return 0

    lax.fori_loop(0, CAP, reorder, 0)
    finish_copy(up, has_up, has_down)
    finish_copy(down, has_down, has_up)
    far_l = make(strip(1, 1, outer, 128), strip(4, 1, outer, 128), ssem.at[2], rsem.at[2], left)
    far_r = make(strip(3, 1, outer, 128), strip(0, 1, outer, 128), ssem.at[3], rsem.at[3], right)
    when(has_left, far_l.start)
    when(has_right, far_r.start)
    mate = (r + 1 - 2 * core, c)
    near = pl.multiple_of(392 - 256 * core, 8)
    relays = []
    for k, (tile, copy, sent, received) in enumerate(
        ((4, to_left, has_left, has_right), (0, to_right, has_right, has_left))
    ):
        finish_copy(copy, sent, received)
        relays.append(
            send(strip(tile, 1, near, 128), strip(tile, 1, outer, 128), ssem.at[6 + k], rsem.at[6 + k], mate)
        )
    finish_copy(far_l, has_left, has_right)
    finish_copy(far_r, has_right, has_left)
    for copy in relays + small:
        copy.wait()


def halo(obj, pats, meta):
    return pl.pallas_call(
        halo_kernel,
        out_shape=(
            jax.ShapeDtypeStruct((2, 5, EXT_ROWS, 128), f32),
            jax.ShapeDtypeStruct((CAP, WIN, WIN), f32),
            jax.ShapeDtypeStruct((9, 8, 128), jnp.int32),
        ),
        in_specs=[
            pl.BlockSpec(memory_space=VMEM),
            pl.BlockSpec(memory_space=pltpu.HBM),
            pl.BlockSpec(memory_space=VMEM),
        ],
        out_specs=[pl.BlockSpec(memory_space=VMEM)] * 3,
        scratch_shapes=[
            VMEM((CAP, WIN, WIN), f32),
            VMEM((2, WIN, 128), f32),
            pltpu.SemaphoreType.DMA,
            pltpu.SemaphoreType.DMA((8,)),
            pltpu.SemaphoreType.DMA((8,)),
            pltpu.SemaphoreType.DMA((8,)),
            pltpu.SemaphoreType.DMA((8,)),
        ],
        compiler_params=pltpu.CompilerParams(
            collective_id=0, has_side_effects=True, vmem_limit_bytes=20 * 2**20
        ),
        name="halo_in",
    )(obj, pats, meta)


def turn(x, shift):
    return pltpu.roll(x, shift, 1)


def slots_kernel(
    where,
    ext,
    probe,
    spat,
    tables_far,
    grad,
    weight,
    probe_out,
    raw,
    patch,
    slope,
    xs,
    ts,
    zs,
    rev,
    power,
    canvas,
    tables,
    lsem,
):
    load = pltpu.make_async_copy(tables_far, tables, lsem)
    load.start()
    r, c = lax.axis_index("row"), lax.axis_index("col")
    row_start, col_start = r * TILE, c * TILE
    lane = lax.broadcasted_iota(jnp.int32, (8, 128), 1)
    zero = jnp.zeros((8, 128), f32)

    def clear(ref, lead, rows):
        def step(i, _):
            for ix in lead:
                ref[(*ix, pl.ds(pl.multiple_of(i * 8, 8), 8), slice(None))] = zero
            return 0

        lax.fori_loop(0, rows // 8, step, 0, unroll=2)

    clear(grad, [(ch, t) for ch in range(2) for t in range(5)], EXT_ROWS)
    clear(probe_out, [(i, t) for i in range(5) for t in range(2)], WIN)
    for t in range(3):
        canvas[2 + t, WIN : WIN + TILE, :] = jnp.zeros((TILE, 128), f32)
    raw[...] = jnp.where(
        (lax.broadcasted_iota(jnp.int32, (8, 128), 0) == 7) & (lane == 2),
        where[4, 0, 2 * CAP].astype(f32),
        0.0,
    )

    def fill_power(i, _):
        rows = pl.ds(pl.multiple_of(i * 8, 8), 8)
        for j in range(2):
            cols = slice(128 * j, 128 * (j + 1))
            power[j, rows, :] = (
                probe[0, 0, rows, cols] ** 2
                + probe[0, 1, rows, cols] ** 2
                + probe[1, 0, rows, cols] ** 2
                + probe[1, 1, rows, cols] ** 2
            )
        return 0

    lax.fori_loop(0, WIN // 8, fill_power, 0, unroll=4)

    for j in (0, 1, 2, 3, 5, 6, 7, 8):
        jr, jc = j // 3 - 1, j % 3 - 1
        inside = (r + jr >= 0) & (r + jr < lax.axis_size("row")) & (c + jc >= 0) & (c + jc < lax.axis_size("col"))
        live = jnp.where(inside, where[j, 0, 2 * CAP], 0)

        def place(slot, _, j=j, jr=jr, jc=jc):
            top = where[j, 0, 2 * slot] - row_start
            left = where[j, 0, 2 * slot + 1] - col_start

            @pl.when((top > -WIN) & (top < TILE) & (left > -WIN) & (left < TILE))
            def _():
                at = left + WIN
                tile, shift = at // 128, lax.rem(at, 128)
                begin, rows = {-1: (HALF, HALF), 0: (0, WIN), 1: (0, HALF)}[jr]
                for start in range(begin, begin + rows, 64):
                    keep = lax.broadcasted_iota(jnp.int32, (64, 128), 1) >= shift
                    dst = pl.ds(top + WIN + start, 64)
                    if jc <= 0:
                        b = turn(power[1, start : start + 64, :], shift)
                        canvas[tile + 2, dst, :] += jnp.where(keep, 0.0, b)
                    if jc >= 0:
                        a = turn(power[0, start : start + 64, :], shift)
                        canvas[tile, dst, :] += jnp.where(keep, a, 0.0)
                    if jc == 0:
                        canvas[tile + 1, dst, :] += jnp.where(keep, b, a)

            return 0

        lax.fori_loop(0, live, place, 0)

    load.wait()

    def visit(slot, _):
        top = where[4, 0, 2 * slot] - row_start + HALF
        left = where[4, 0, 2 * slot + 1] - col_start + HALF

        tile, shift = left // 128, lax.rem(left, 128)
        apart = lax.broadcasted_iota(jnp.int32, (256, 128), 0) - lax.broadcasted_iota(
            jnp.int32, (256, 128), 1
        )
        move = jnp.where(apart == shift, 1.0, 0.0).astype(bf16)
        differ = jnp.where(apart == shift + 1, 0.5, jnp.where(apart == shift - 1, -0.5, 0.0)).astype(bf16)
        shifter = jnp.concatenate([move, differ], axis=1)
        for ch in range(2):
            x = [split(ext[ch, tile + t, pl.ds(top, 272), :]) for t in range(3)]
            high, low = (
                jnp.concatenate(
                    [jnp.concatenate([x[j][p], x[j + 1][p]], axis=1) for j in range(2)], axis=0
                )
                for p in range(2)
            )
            y = mm(high, shifter) + mm(low, shifter)
            for j in range(2):
                patch[ch, j] = y[272 * j : 272 * (j + 1), :128]
                slope[ch, j] = y[272 * j : 272 * (j + 1), 128:]

        @pl.when(shift == 0)
        def _():
            first = lax.broadcasted_iota(jnp.int32, (272, 128), 1) == 0
            for ch in range(2):
                for j in range(2):
                    before = turn(ext[ch, tile + j - 1, pl.ds(top, 272), :], 1)
                    slope[ch, j] += jnp.where(first, -0.5 * before, 0.0)

        def leave(i, _):
            rows = [pl.multiple_of(i * 16 + 128 * h, 16) for h in range(2)]
            for j in range(2):
                cols = slice(128 * j, 128 * (j + 1))
                o = [[patch[ch, j, pl.ds(rw + 8, 16), :] for ch in range(2)] for rw in rows]
                for m in range(2):
                    e = []
                    for h in range(2):
                        pr = probe[m, 0, pl.ds(rows[h], 16), cols]
                        pi = probe[m, 1, pl.ds(rows[h], 16), cols]
                        e.append((pr * o[h][0] - pi * o[h][1], pr * o[h][1] + pi * o[h][0]))
                    for ch in range(2):
                        at = pl.ds(pl.multiple_of(i * 16 + 128 * ch, 16), 16)
                        for k, v in enumerate((e[0][ch] + e[1][ch], e[0][ch] - e[1][ch])):
                            high, low = split(v)
                            xs[m, 2 * k, at, cols] = high
                            xs[m, 2 * k + 1, at, cols] = low
            return 0

        lax.fori_loop(0, 8, leave, 0, unroll=True)

        def left_mm(k, high, low):
            return mm(tables[2 * k], high) + mm(tables[2 * k], low) + mm(tables[2 * k + 1], high)

        def right_mm(k, high, low):
            return mm(high, tables[2 * k]) + mm(low, tables[2 * k]) + mm(high, tables[2 * k + 1])

        for m in range(2):
            for k in range(2):
                y = left_mm(k, xs[m, 2 * k], xs[m, 2 * k + 1])
                for ch in range(2):
                    a, b = y[128 * ch : 128 * (ch + 1), :128], y[128 * ch : 128 * (ch + 1), 128:]
                    for q, v in enumerate((a + b, a - b)):
                        high, low = split(v)
                        at = (slice(128 * k, 128 * (k + 1)), slice(128 * ch, 128 * (ch + 1)))
                        ts[m, 2 * q, *at] = high
                        ts[m, 2 * q + 1, *at] = low
        for q in range(2):
            y = right_mm(2 + q, ts[:, 2 * q].reshape(512, 256), ts[:, 2 * q + 1].reshape(512, 256))
            for m in range(2):
                zs[m, q] = y[256 * m : 256 * (m + 1)]

        def project(i, _):
            at = pl.ds(pl.multiple_of(i * 16, 16), 16)
            for q in range(2):
                z = [[zs[m, q, at, 128 * ch : 128 * (ch + 1)] for ch in range(2)] for m in range(2)]
                amp = z[0][0] ** 2 + z[0][1] ** 2 + z[1][0] ** 2 + z[1][1] ** 2
                factor = spat[slot, at, 128 * q : 128 * (q + 1)] * lax.rsqrt(jnp.maximum(amp, 0.0625))
                for m in range(2):
                    for ch in range(2):
                        high, low = split(z[m][ch] * factor)
                        ts[m, 2 * q, at, 128 * ch : 128 * (ch + 1)] = high
                        ts[m, 2 * q + 1, at, 128 * ch : 128 * (ch + 1)] = low
            return 0

        lax.fori_loop(0, 16, project, 0, unroll=True)

        both_a = right_mm(0, ts[:, 0].reshape(512, 256), ts[:, 1].reshape(512, 256))
        both_b = right_mm(1, ts[:, 2].reshape(512, 256), ts[:, 3].reshape(512, 256))
        for m in range(2):
            a = both_a[256 * m : 256 * (m + 1)]
            b = both_b[256 * m : 256 * (m + 1)]
            for half, v in enumerate((a + b, a - b)):
                high, low = split(v)
                for k in range(2):
                    for ch in range(2):
                        at = (slice(128 * ch, 128 * (ch + 1)), slice(128 * half, 128 * (half + 1)))
                        pick = (slice(128 * k, 128 * (k + 1)), slice(128 * ch, 128 * (ch + 1)))
                        xs[m, 2 * k, *at] = high[pick]
                        xs[m, 2 * k + 1, *at] = low[pick]
            u = left_mm(2, xs[m, 0], xs[m, 1])
            v = left_mm(3, xs[m, 2], xs[m, 3])
            for ch in range(2):
                at = slice(128 * ch, 128 * (ch + 1))
                rev[m, ch, 0:128, :] = u[at] + v[at]
                rev[m, ch, 128:256, :] = u[at] - v[at]

        tile_g, shift_g = left // 128, lax.rem(left, 128)
        keep = lax.broadcasted_iota(jnp.int32, (STEP, 128), 1) >= shift_g

        def fold(x):
            return sum(x[8 * k : 8 * (k + 1)] for k in range(STEP // 8))

        def finish(i, acc):
            at = pl.ds(pl.multiple_of(i * STEP, STEP), STEP)
            dst = pl.ds(top + 8 + i * STEP, STEP)
            g = []
            acc = list(acc)
            for j in range(2):
                cols = slice(128 * j, 128 * (j + 1))
                o_re = patch[0, j, pl.ds(i * STEP + 8, STEP), :]
                o_im = patch[1, j, pl.ds(i * STEP + 8, STEP), :]
                w = power[j, at, :]
                g_re, g_im = -w * o_re, -w * o_im
                for m in range(2):
                    p_re, p_im = probe[m, 0, at, cols], probe[m, 1, at, cols]
                    v_re, v_im = rev[m, 0, at, cols], rev[m, 1, at, cols]
                    g_re += p_re * v_re + p_im * v_im
                    g_im += p_re * v_im - p_im * v_re
                    probe_out[2 * m, j, at, :] += o_re * v_re + o_im * v_im
                    probe_out[2 * m + 1, j, at, :] += o_re * v_im - o_im * v_re
                probe_out[4, j, at, :] += o_re * o_re + o_im * o_im
                d_re = 0.5 * (
                    patch[0, j, pl.ds(i * STEP + 9, STEP), :] - patch[0, j, pl.ds(i * STEP + 7, STEP), :]
                )
                d_im = 0.5 * (
                    patch[1, j, pl.ds(i * STEP + 9, STEP), :] - patch[1, j, pl.ds(i * STEP + 7, STEP), :]
                )
                s_re = slope[0, j, pl.ds(i * STEP + 8, STEP), :]
                s_im = slope[1, j, pl.ds(i * STEP + 8, STEP), :]
                acc[0] += fold(g_re * d_re + g_im * d_im)
                acc[1] += fold(w * (d_re * d_re + d_im * d_im))
                acc[2] += fold(g_re * s_re + g_im * s_im)
                acc[3] += fold(w * (s_re * s_re + s_im * s_im))
                g.append((g_re, g_im))
            for ch in range(2):
                a, b = turn(g[0][ch], shift_g), turn(g[1][ch], shift_g)
                grad[ch, tile_g, dst, :] += jnp.where(keep, a, 0.0)
                grad[ch, tile_g + 1, dst, :] += jnp.where(keep, b, a)
                grad[ch, tile_g + 2, dst, :] += jnp.where(keep, 0.0, b)
            a, b = turn(power[0, at, :], shift_g), turn(power[1, at, :], shift_g)
            dst = pl.ds(top + HALF + i * STEP, STEP)
            canvas[tile_g + 1, dst, :] += jnp.where(keep, a, 0.0)
            canvas[tile_g + 2, dst, :] += jnp.where(keep, b, a)
            canvas[tile_g + 3, dst, :] += jnp.where(keep, 0.0, b)
            return tuple(acc)

        acc = lax.fori_loop(0, WIN // STEP, finish, (zero,) * 4, unroll=True)
        total = [jnp.sum(acc[k], axis=(0, 1), keepdims=True) for k in range(4)]
        at_row = lax.broadcasted_iota(jnp.int32, (8, 128), 0) == slot
        for k in range(2):
            value = total[2 * k] * lax.rsqrt(total[2 * k + 1] + 1e-6)
            raw[...] += jnp.where(at_row & (lane == k), value, 0.0)
        return 0

    lax.fori_loop(0, where[4, 0, 2 * CAP], visit, 0)
    for t in range(3):
        weight[:, 128 * t : 128 * (t + 1)] = canvas[2 + t, pl.ds(WIN, TILE), :]


def slots(where, ext, probe, spat, tables):
    v = pl.BlockSpec(memory_space=VMEM)
    return pl.pallas_call(
        slots_kernel,
        out_shape=(
            jax.ShapeDtypeStruct((2, 5, EXT_ROWS, 128), f32),
            jax.ShapeDtypeStruct((TILE, TILE), f32),
            jax.ShapeDtypeStruct((5, 2, WIN, 128), f32),
            jax.ShapeDtypeStruct((8, 128), f32),
        ),
        in_specs=[pl.BlockSpec(memory_space=pltpu.SMEM), v, v, v, pl.BlockSpec(memory_space=pltpu.HBM)],
        out_specs=[v, v, v, v],
        scratch_shapes=[
            VMEM((2, 2, 272, 128), f32),
            VMEM((2, 2, 272, 128), f32),
            VMEM((2, 4, WIN, WIN), bf16),
            VMEM((2, 4, WIN, WIN), bf16),
            VMEM((2, 2, WIN, WIN), f32),
            VMEM((2, 2, WIN, WIN), f32),
            VMEM((2, WIN, 128), f32),
            VMEM((8, 904, 128), f32),
            VMEM((8, WIN, WIN), bf16),
            pltpu.SemaphoreType.DMA,
        ],
        compiler_params=pltpu.CompilerParams(vmem_limit_bytes=24 * 2**20),
        name="slots",
    )(where, ext, probe, spat, tables)


SHARDS = 32
SHARD = 80
PIECE = SHARD + 8


def plane(dx, dy):
    r, c = lax.axis_index("row"), lax.axis_index("col")
    return (lax.rem(r + 4 * dx, 16), lax.rem(c + 4 * dy, 16))


def depth_of():
    r, c = lax.axis_index("row"), lax.axis_index("col")
    return 4 * lax.rem(r // 2, 2) + lax.rem(c, 4)


def along(dz):
    r, c = lax.axis_index("row"), lax.axis_index("col")
    z = lax.rem(depth_of() + dz, 8)
    return (r // 4 * 4 + z // 4 * 2 + lax.rem(r, 2), c // 4 * 4 + lax.rem(z, 4))


def sums_kernel(
    grad,
    weight,
    obj,
    probe,
    part,
    raw,
    obj_new,
    probe_new,
    step,
    mate_rows,
    corner_in,
    row_out,
    row_in,
    side_out,
    side_in,
    mine,
    mate_part,
    plane_part,
    deep,
    deep_part,
    deep_all,
    all_sum,
    flat,
    hsend,
    hrecv,
    csend,
    crecv,
    psend,
    precv,
    zsend,
    zrecv,
):
    r, c = lax.axis_index("row"), lax.axis_index("col")
    n_row, n_col = lax.axis_size("row"), lax.axis_size("col")
    core = lax.rem(r, 2)
    own = r // 4 * 4 + c // 4
    z = depth_of()
    mate = (r + 1 - 2 * core, c)
    beyond = (lax.rem(r - 1 + 2 * core + n_row, n_row), c)
    left, right = neighbour((0, -1)), neighbour((0, 1))
    planes = [(dx, dy) for dx in range(4) for dy in range(4) if (dx, dy) != (0, 0)]

    barrier = pltpu.get_barrier_semaphore()
    partners = [left, right, mate, beyond]
    partners += [plane(*p) for p in planes] + [along(d) for d in range(1, 8)]
    for partner in partners:
        pl.semaphore_signal(barrier, inc=1, device_id=partner, device_id_type=MESH)

    def gather(i, _):
        mine[i, 0:SHARD, :] = part[pl.ds(pl.multiple_of(i * SHARD, SHARD), SHARD), :]
        mine[i, SHARD:PIECE, :] = raw[...]
        return 0

    lax.fori_loop(0, SHARDS, gather, 0)
    pl.semaphore_wait(barrier, len(partners))

    outer_from = pl.multiple_of(8 + 512 * core, 8)
    inner_from = pl.multiple_of(520 - 512 * core, 8)
    outer_to = pl.multiple_of(256 * core, 8)
    inner_to = pl.multiple_of(256 - 256 * core, 8)
    col_ok = [c > 0, c < n_col - 1]
    outer_ok = jnp.where(core == 0, r, n_row - 1 - r) > 0

    half = SHARDS // 2
    to_mate = send(
        mine.at[pl.ds(half * (1 - core), half)], mate_part, csend.at[0], crecv.at[0], mate
    )
    rows_to_mate = send(
        grad.at[:, :, pl.ds(inner_from, 128), :], mate_rows, csend.at[2], crecv.at[2], mate
    )
    edge = pl.ds(outer_from, 128)
    has_left, has_right = col_ok
    corner_r = make(grad.at[:, 4, edge, :], corner_in.at[0], hsend.at[0], hrecv.at[0], right)
    corner_l = make(grad.at[:, 0, edge, :], corner_in.at[1], hsend.at[1], hrecv.at[1], left)
    when(has_right, corner_r.start)
    when(has_left, corner_l.start)

    rows_to_mate.wait()
    def fill_sides(ch):
        for k, tile in enumerate((4, 0)):
            side_out[k, ch] = grad[ch, tile, 136:520, :]
            side_out[k, ch, pl.ds(inner_to, 128), :] += mate_rows[ch, tile]

    def side(ch, k):
        i = 2 + 2 * k + ch
        return make(side_out.at[k, ch], side_in.at[k, ch], hsend.at[i], hrecv.at[i], (right, left)[k])

    sides = [[side(ch, k) for k in range(2)] for ch in range(2)]

    fill_sides(0)
    fill_sides(1)
    to_mate.wait()

    def add_mate(i, _):
        mine[half * core + i] += mate_part[i]
        return 0

    lax.fori_loop(0, half, add_mate, 0)
    copies = []
    for i, (dx, dy) in enumerate(planes):
        to = plane(dx, dy)
        owner = to[0] // 4 * 4 + to[1] // 4
        copies.append(
            send(mine.at[half * core + owner], plane_part.at[i], psend.at[i], precv.at[i], to)
        )
    finish_copy(corner_r, has_right, has_left)
    finish_copy(corner_l, has_left, has_right)
    for ch in range(2):
        for t in range(3):
            v = grad[ch, 1 + t, edge, :]
            if t == 0:
                v = v + jnp.where(col_ok[0], corner_in[0, ch], 0.0)
            if t == 2:
                v = v + jnp.where(col_ok[1], corner_in[1, ch], 0.0)
            row_out[ch, t] = v
    strip = make(row_out, row_in, hsend.at[6], hrecv.at[6], beyond)
    when(outer_ok, strip.start)
    for copy in copies:
        copy.wait()
    total = mine[half * core + own]
    for i in range(15):
        total = total + plane_part[i]
    deep[0:PIECE, :] = total
    deep[PIECE:128, :] = jnp.zeros((128 - PIECE, 128), f32)
    copies = []
    for d in range(1, 8):
        there = lax.rem(z + d, 8)
        copies.append(
            send(
                deep.at[pl.ds(pl.multiple_of(there * 16, 16), 16)],
                deep_part.at[d - 1],
                zsend.at[d - 1],
                zrecv.at[d - 1],
                along(d),
            )
        )
    for copy in copies:
        copy.wait()
    total = deep[pl.ds(pl.multiple_of(z * 16, 16), 16), :]
    for d in range(7):
        total = total + deep_part[d]
    here = deep_all.at[pl.ds(pl.multiple_of(z * 16, 16), 16)]
    deep_all[pl.ds(pl.multiple_of(z * 16, 16), 16), :] = total
    copies = [send(here, here, zsend.at[6 + d], zrecv.at[6 + d], along(d)) for d in range(1, 8)]
    for ch in range(2):
        when(has_right, sides[ch][0].start)
        when(has_left, sides[ch][1].start)
    for copy in copies:
        copy.wait()
    all_sum[half * core + own] = deep_all[0:PIECE, :]
    block = all_sum.at[half * core + own]
    copies = [
        send(block, block, psend.at[15 + i], precv.at[15 + i], plane(*p)) for i, p in enumerate(planes)
    ]
    for copy in copies:
        copy.wait()
    block = all_sum.at[pl.ds(half * core, half)]
    to_mate = send(block, block, csend.at[1], crecv.at[1], mate)

    def peak(i, top):
        rows = pl.ds(pl.multiple_of(i * 8, 8), 8)
        power = probe[0, 0, rows, :] ** 2 + probe[0, 1, rows, :] ** 2
        power = power + probe[1, 0, rows, :] ** 2 + probe[1, 1, rows, :] ** 2
        return jnp.maximum(top, power)

    top = lax.fori_loop(0, WIN // 8, peak, jnp.zeros((8, WIN), f32))
    floor = 0.1 * jnp.max(top, axis=(0, 1), keepdims=True)

    to_mate.wait()

    def spread(i, _):
        flat[pl.ds(pl.multiple_of(i * SHARD, SHARD), SHARD), :] = all_sum[i, 0:SHARD, :]
        return 0

    lax.fori_loop(0, SHARDS, spread, 0)

    def peak_sum(i, top):
        return jnp.maximum(top, flat[pl.ds(pl.multiple_of(2048 + i * 8, 8), 8), :])

    top = lax.fori_loop(0, 64, peak_sum, jnp.zeros((8, 128), f32))
    floor_p = 0.1 * jnp.max(top, axis=(0, 1), keepdims=True)

    def renew(i, _):
        rows = pl.ds(pl.multiple_of(i * 8, 8), 8)
        for j in range(2):
            cols = slice(128 * j, 128 * (j + 1))

            def at(k):
                return flat[pl.ds(pl.multiple_of((2 * k + j) * WIN + i * 8, 8), 8), :]

            wp = at(4)
            scale = 1.0 / (wp + floor_p)
            for m in range(2):
                for ch in range(2):
                    old = probe[m, ch, rows, cols]
                    probe_new[m, ch, rows, cols] = old + (at(2 * m + ch) - old * wp) * scale
        return 0

    lax.fori_loop(0, WIN // 8, renew, 0)

    rows8 = lax.broadcasted_iota(jnp.int32, (8, 128), 0)
    lanes8 = lax.broadcasted_iota(jnp.int32, (8, 128), 1)
    is_count = (rows8 == 7) & (lanes8 == 2)
    sums = all_sum[0, SHARD:PIECE, :]
    count = jnp.sum(jnp.where(is_count, sums, 0.0), axis=(0, 1), keepdims=True)
    mine_count = jnp.sum(jnp.where(is_count, raw[...], 0.0), axis=(0, 1), keepdims=True)
    mean = jnp.sum(sums, axis=0, keepdims=True) / count
    step[...] = jnp.where(rows8.astype(f32) < mine_count, raw[...] - mean, 0.0)

    for ch in range(2):
        finish_copy(sides[ch][0], has_right, has_left)
        finish_copy(sides[ch][1], has_left, has_right)
    for band, start in ((1, 128), (2, inner_to), (0, outer_to)):
        if band == 0:
            finish_copy(strip, outer_ok, outer_ok)

        def update(i, _, band=band, start=start):
            rows = pl.ds(pl.multiple_of(start + i * 8, 8), 8)
            thin = pl.ds(pl.multiple_of(i * 8, 8), 8)
            for t in range(3):
                cols = slice(128 * t, 128 * (t + 1))
                down = weight[rows, cols] + floor
                for ch in range(2):
                    g = grad[ch, 1 + t, pl.ds(pl.multiple_of(136 + start + i * 8, 8), 8), :]
                    if band == 0:
                        g = g + jnp.where(outer_ok, row_in[ch, t, thin, :], 0.0)
                    if band == 2:
                        g = g + mate_rows[ch, 1 + t, thin, :]
                    if t == 0:
                        g = g + jnp.where(col_ok[0], side_in[0, ch, rows, :], 0.0)
                    if t == 2:
                        g = g + jnp.where(col_ok[1], side_in[1, ch, rows, :], 0.0)
                    obj_new[ch, rows, cols] = obj[ch, rows, cols] + g / down
            return 0

        lax.fori_loop(0, 16, update, 0, unroll=2)


def sums(grad, weight, obj, probe, part, raw):
    v = pl.BlockSpec(memory_space=VMEM)
    dma = pltpu.SemaphoreType.DMA
    return pl.pallas_call(
        sums_kernel,
        out_shape=(
            jax.ShapeDtypeStruct((2, TILE, TILE), f32),
            jax.ShapeDtypeStruct((2, 2, WIN, WIN), f32),
            jax.ShapeDtypeStruct((8, 128), f32),
        ),
        in_specs=[v] * 6,
        out_specs=[v] * 3,
        scratch_shapes=[
            VMEM((2, 5, 128, 128), f32),
            VMEM((2, 2, 128, 128), f32),
            VMEM((2, 3, 128, 128), f32),
            VMEM((2, 3, 128, 128), f32),
            VMEM((2, 2, TILE, 128), f32),
            VMEM((2, 2, TILE, 128), f32),
            VMEM((SHARDS, PIECE, 128), f32),
            VMEM((SHARDS // 2, PIECE, 128), f32),
            VMEM((15, PIECE, 128), f32),
            VMEM((128, 128), f32),
            VMEM((7, 16, 128), f32),
            VMEM((128, 128), f32),
            VMEM((SHARDS, PIECE, 128), f32),
            VMEM((SHARDS * SHARD, 128), f32),
            dma((7,)),
            dma((7,)),
            dma((3,)),
            dma((3,)),
            dma((30,)),
            dma((30,)),
            dma((14,)),
            dma((14,)),
        ],
        compiler_params=pltpu.CompilerParams(
            collective_id=1, has_side_effects=True, vmem_limit_bytes=28 * 2**20
        ),
        name="sums",
    )(grad, weight, obj, probe, part, raw)


def on_device(object_field, probe, patterns, positions, counts):
    meta = jnp.concatenate([positions.reshape(1, 2 * CAP), counts.reshape(1, 1)], axis=1)
    meta = jnp.pad(meta, ((0, 7), (0, 128 - 2 * CAP - 1)))
    ext, spat, where = halo(object_field, patterns[0, 0], meta)
    grad, weight, part, raw = slots(where, ext, probe, spat, jnp.asarray(dft_tables()))
    object_new, probe_new, step = sums(
        grad, weight, object_field, probe, part.reshape(SHARDS * SHARD, 128), raw
    )
    return object_new, probe_new, step[:CAP, :2].reshape(1, 1, CAP, 2)


def solution(mesh):
    placed = (
        P(None, "row", "col"),
        P(),
        P("row", "col", None, None, None),
        P("row", "col", None, None),
        P("row", "col"),
    )
    return jax.shard_map(
        on_device,
        mesh=mesh,
        in_specs=placed,
        out_specs=(P(None, "row", "col"), P(), P("row", "col", None, None)),
        check_vma=False,
    )
```

```python
import functools

import jax
import jax.numpy as jnp
import ml_dtypes
import numpy as np
from jax import lax
from jax.experimental import pallas as pl
from jax.experimental.pallas import tpu as pltpu
from jax.sharding import PartitionSpec as P

MESH = pl.DeviceIdType.MESH
VMEM = pltpu.VMEM
f32 = jnp.float32
bf16 = jnp.bfloat16

WIN = 256
HALF = 128
TILE = 384
CAP = 6
STEP = 32
EXT_ROWS = 8 + HALF + TILE + HALF + 8
OFFSETS = [(-1, 0), (1, 0), (0, -1), (0, 1), (-1, -1), (-1, 1), (1, -1), (1, 1)]


def dft_tables():
    k = np.arange(HALF)
    even = np.exp(-2j * np.pi * np.outer(2 * k, k) / WIN) / np.sqrt(WIN)
    odd = np.exp(-2j * np.pi * np.outer(2 * k + 1, k) / WIN) / np.sqrt(WIN)

    def block(z):
        return np.block([[z.real, -z.imag], [z.imag, z.real]])

    out = []
    for mat in (block(even), block(odd), block(even).T, block(odd).T):
        high = mat.astype(np.float32).astype(ml_dtypes.bfloat16)
        low = (mat - high.astype(np.float64)).astype(np.float32).astype(ml_dtypes.bfloat16)
        out += [high, low]
    return np.stack(out)


def split(x):
    high = x.astype(bf16)
    return high, (x - high.astype(f32)).astype(bf16)


def mm(a, b):
    return jnp.dot(a, b, preferred_element_type=f32)


def neighbour(step):
    n_row, n_col = lax.axis_size("row"), lax.axis_size("col")
    r, c = lax.axis_index("row"), lax.axis_index("col")
    return (lax.rem(r + step[0] + n_row, n_row), lax.rem(c + step[1] + n_col, n_col))


def greet():
    barrier = pltpu.get_barrier_semaphore()
    for step in OFFSETS:
        pl.semaphore_signal(barrier, inc=1, device_id=neighbour(step), device_id_type=MESH)
    pl.semaphore_wait(barrier, len(OFFSETS))


def send(src, dst, ssem, rsem, to):
    copy = pltpu.make_async_remote_copy(
        src_ref=src, dst_ref=dst, send_sem=ssem, recv_sem=rsem, device_id=to, device_id_type=MESH
    )
    copy.start()
    return copy


def when(condition, act):
    @pl.when(condition)
    def _():
        act()


def finish_copy(copy, sent, received):
    when(sent, copy.wait_send)
    when(received, copy.wait_recv)


def make(src, dst, ssem, rsem, to):
    return pltpu.make_async_remote_copy(
        src_ref=src, dst_ref=dst, send_sem=ssem, recv_sem=rsem, device_id=to, device_id_type=MESH
    )


def halo_kernel(
    obj, pats_far, meta, ext, spat, metas, pats, turned, lsem, ssem, rsem, msend, mrecv
):
    r, c = lax.axis_index("row"), lax.axis_index("col")
    core = lax.rem(r, 2)
    load = pltpu.make_async_copy(pats_far, pats, lsem)
    load.start()
    has_up, has_down = r > 0, r < lax.axis_size("row") - 1
    has_left, has_right = c > 0, c < lax.axis_size("col") - 1

    for ch in range(2):
        for t in range(5):
            ext[ch, t, 0:8, :] = jnp.zeros((8, 128), f32)
            ext[ch, t, 648:656, :] = jnp.zeros((8, 128), f32)

    def blank(tiles, rows):
        ext[:, tiles, rows, :] = jnp.zeros((2, tiles.stop - tiles.start, rows.stop - rows.start, 128), f32)

    when(r == 0, lambda: blank(slice(0, 5), slice(8, 136)))
    when(jnp.logical_not(has_down), lambda: blank(slice(0, 5), slice(520, 648)))
    when(c == 0, lambda: blank(slice(0, 1), slice(8, 648)))
    when(jnp.logical_not(has_right), lambda: blank(slice(4, 5), slice(8, 648)))
    greet()
    for t in range(3):
        for ch in range(2):
            ext[ch, 1 + t, 136:520, :] = obj[ch, :, 128 * t : 128 * (t + 1)]
    metas[4] = meta[...]

    def strip(tile, tiles, row, rows):
        return ext.at[:, pl.ds(tile, tiles), pl.ds(row, rows), :]

    left, right = neighbour((0, -1)), neighbour((0, 1))
    outer = pl.multiple_of(8 + 512 * core, 8)
    up = make(strip(1, 3, 136, 128), strip(1, 3, 520, 128), ssem.at[0], rsem.at[0], neighbour((-1, 0)))
    down = make(strip(1, 3, 392, 128), strip(1, 3, 8, 128), ssem.at[1], rsem.at[1], neighbour((1, 0)))
    to_left = make(strip(1, 1, 136, 384), strip(4, 1, 136, 384), ssem.at[4], rsem.at[4], left)
    to_right = make(strip(3, 1, 136, 384), strip(0, 1, 136, 384), ssem.at[5], rsem.at[5], right)
    when(has_up, up.start)
    when(has_down, down.start)
    far_left, far_right = lax.rem(c, 4) == 0, lax.rem(c, 4) == 3
    when(has_left & far_left, to_left.start)
    when(has_right & far_right, to_right.start)
    beyond = lax.rem(r - 1 + 2 * core + lax.axis_size("row"), lax.axis_size("row"))
    outer_ok = jnp.where(core == 0, r, lax.axis_size("row") - 1 - r) > 0
    own_edge, its_edge = pl.multiple_of(136 + 256 * core, 8), pl.multiple_of(520 - 512 * core, 8)
    jump_l = make(
        strip(1, 1, own_edge, 128), strip(4, 1, its_edge, 128), ssem.at[2], rsem.at[2], (beyond, left[1])
    )
    jump_r = make(
        strip(3, 1, own_edge, 128), strip(0, 1, its_edge, 128), ssem.at[3], rsem.at[3], (beyond, right[1])
    )
    when(has_left & far_left & outer_ok, jump_l.start)
    when(has_right & far_right & outer_ok, jump_r.start)
    small = [
        send(
            metas.at[4],
            metas.at[(1 - dr) * 3 + 1 - dc],
            msend.at[i],
            mrecv.at[i],
            neighbour((dr, dc)),
        )
        for i, (dr, dc) in enumerate(OFFSETS)
    ]
    when(has_left & jnp.logical_not(far_left), to_left.start)
    when(has_right & jnp.logical_not(far_right), to_right.start)
    load.wait()
    order = []
    for parity in range(2):
        index = lax.broadcasted_iota(jnp.int32, (WIN, HALF), 0)
        wanted = 2 * lax.broadcasted_iota(jnp.int32, (WIN, HALF), 1) + parity
        order.append(jnp.where(index == wanted, 1.0, 0.0).astype(bf16))
    order = jnp.concatenate(order, axis=1)

    def reorder(slot, _):
        high, low = split(jnp.sqrt(pats[slot]))
        sorted_cols = mm(high, order) + mm(low, order)
        for j in range(2):
            turned[j] = sorted_cols[:, 128 * j : 128 * (j + 1)]
        for parity in range(2):
            for j in range(2):
                spat[slot, 128 * parity : 128 * (parity + 1), 128 * j : 128 * (j + 1)] = turned[
                    j, pl.ds(parity, 128, stride=2), :
                ]
        return 0

    lax.fori_loop(0, CAP, reorder, 0)
    finish_copy(up, has_up, has_down)
    finish_copy(down, has_down, has_up)
    far_l = make(strip(1, 1, outer, 128), strip(4, 1, outer, 128), ssem.at[2], rsem.at[2], left)
    far_r = make(strip(3, 1, outer, 128), strip(0, 1, outer, 128), ssem.at[3], rsem.at[3], right)
    when(has_left & jnp.logical_not(far_left), far_l.start)
    when(has_right & jnp.logical_not(far_right), far_r.start)
    mate = (r + 1 - 2 * core, c)
    near = pl.multiple_of(392 - 256 * core, 8)
    relays = []
    for k, (tile, copy, sent, received) in enumerate(
        ((4, to_left, has_left, has_right), (0, to_right, has_right, has_left))
    ):
        finish_copy(copy, sent, received)
        relays.append(
            send(strip(tile, 1, near, 128), strip(tile, 1, outer, 128), ssem.at[6 + k], rsem.at[6 + k], mate)
        )
    sent_left = has_left & (jnp.logical_not(far_left) | outer_ok)
    sent_right = has_right & (jnp.logical_not(far_right) | outer_ok)
    finish_copy(far_l, sent_left, sent_right)
    finish_copy(far_r, sent_right, sent_left)
    for copy in relays + small:
        copy.wait()


def halo(obj, pats, meta):
    return pl.pallas_call(
        halo_kernel,
        out_shape=(
            jax.ShapeDtypeStruct((2, 5, EXT_ROWS, 128), f32),
            jax.ShapeDtypeStruct((CAP, WIN, WIN), f32),
            jax.ShapeDtypeStruct((9, 8, 128), jnp.int32),
        ),
        in_specs=[
            pl.BlockSpec(memory_space=VMEM),
            pl.BlockSpec(memory_space=pltpu.HBM),
            pl.BlockSpec(memory_space=VMEM),
        ],
        out_specs=[pl.BlockSpec(memory_space=VMEM)] * 3,
        scratch_shapes=[
            VMEM((CAP, WIN, WIN), f32),
            VMEM((2, WIN, 128), f32),
            pltpu.SemaphoreType.DMA,
            pltpu.SemaphoreType.DMA((8,)),
            pltpu.SemaphoreType.DMA((8,)),
            pltpu.SemaphoreType.DMA((8,)),
            pltpu.SemaphoreType.DMA((8,)),
        ],
        compiler_params=pltpu.CompilerParams(
            collective_id=0, has_side_effects=True, vmem_limit_bytes=20 * 2**20
        ),
        name="halo_in",
    )(obj, pats, meta)


def turn(x, shift):
    return pltpu.roll(x, shift, 1)


def slots_kernel(
    where,
    ext,
    probe,
    spat,
    tables_far,
    grad,
    weight,
    probe_out,
    raw,
    patch,
    slope,
    xs,
    ts,
    zs,
    rev,
    power,
    canvas,
    tables,
    lsem,
):
    load = pltpu.make_async_copy(tables_far, tables, lsem)
    load.start()
    r, c = lax.axis_index("row"), lax.axis_index("col")
    row_start, col_start = r * TILE, c * TILE
    lane = lax.broadcasted_iota(jnp.int32, (8, 128), 1)
    zero = jnp.zeros((8, 128), f32)

    def clear(ref, lead, rows):
        def step(i, _):
            for ix in lead:
                ref[(*ix, pl.ds(pl.multiple_of(i * 8, 8), 8), slice(None))] = zero
            return 0

        lax.fori_loop(0, rows // 8, step, 0, unroll=2)

    clear(grad, [(ch, t) for ch in range(2) for t in range(5)], EXT_ROWS)
    clear(probe_out, [(i, t) for i in range(5) for t in range(2)], WIN)
    for t in range(3):
        canvas[2 + t, WIN : WIN + TILE, :] = jnp.zeros((TILE, 128), f32)
    raw[...] = jnp.where(
        (lax.broadcasted_iota(jnp.int32, (8, 128), 0) == 7) & (lane == 2),
        where[4, 0, 2 * CAP].astype(f32),
        0.0,
    )

    def fill_power(i, _):
        rows = pl.ds(pl.multiple_of(i * 8, 8), 8)
        for j in range(2):
            cols = slice(128 * j, 128 * (j + 1))
            power[j, rows, :] = (
                probe[0, 0, rows, cols] ** 2
                + probe[0, 1, rows, cols] ** 2
                + probe[1, 0, rows, cols] ** 2
                + probe[1, 1, rows, cols] ** 2
            )
        return 0

    lax.fori_loop(0, WIN // 8, fill_power, 0, unroll=4)

    for j in (0, 1, 2, 3, 5, 6, 7, 8):
        jr, jc = j // 3 - 1, j % 3 - 1
        inside = (r + jr >= 0) & (r + jr < lax.axis_size("row")) & (c + jc >= 0) & (c + jc < lax.axis_size("col"))
        live = jnp.where(inside, where[j, 0, 2 * CAP], 0)

        def place(slot, _, j=j, jr=jr, jc=jc):
            top = where[j, 0, 2 * slot] - row_start
            left = where[j, 0, 2 * slot + 1] - col_start

            @pl.when((top > -WIN) & (top < TILE) & (left > -WIN) & (left < TILE))
            def _():
                at = left + WIN
                tile, shift = at // 128, lax.rem(at, 128)
                begin, rows = {-1: (HALF, HALF), 0: (0, WIN), 1: (0, HALF)}[jr]
                for start in range(begin, begin + rows, 64):
                    keep = lax.broadcasted_iota(jnp.int32, (64, 128), 1) >= shift
                    dst = pl.ds(top + WIN + start, 64)
                    if jc <= 0:
                        b = turn(power[1, start : start + 64, :], shift)
                        canvas[tile + 2, dst, :] += jnp.where(keep, 0.0, b)
                    if jc >= 0:
                        a = turn(power[0, start : start + 64, :], shift)
                        canvas[tile, dst, :] += jnp.where(keep, a, 0.0)
                    if jc == 0:
                        canvas[tile + 1, dst, :] += jnp.where(keep, b, a)

            return 0

        lax.fori_loop(0, live, place, 0)

    load.wait()

    def visit(slot, _):
        top = where[4, 0, 2 * slot] - row_start + HALF
        left = where[4, 0, 2 * slot + 1] - col_start + HALF

        tile, shift = left // 128, lax.rem(left, 128)
        apart = lax.broadcasted_iota(jnp.int32, (256, 128), 0) - lax.broadcasted_iota(
            jnp.int32, (256, 128), 1
        )
        move = jnp.where(apart == shift, 1.0, 0.0).astype(bf16)
        differ = jnp.where(apart == shift + 1, 0.5, jnp.where(apart == shift - 1, -0.5, 0.0)).astype(bf16)
        shifter = jnp.concatenate([move, differ], axis=1)
        for ch in range(2):
            x = [split(ext[ch, tile + t, pl.ds(top, 272), :]) for t in range(3)]
            high, low = (
                jnp.concatenate(
                    [jnp.concatenate([x[j][p], x[j + 1][p]], axis=1) for j in range(2)], axis=0
                )
                for p in range(2)
            )
            y = mm(high, shifter) + mm(low, shifter)
            for j in range(2):
                patch[ch, j] = y[272 * j : 272 * (j + 1), :128]
                slope[ch, j] = y[272 * j : 272 * (j + 1), 128:]

        @pl.when(shift == 0)
        def _():
            first = lax.broadcasted_iota(jnp.int32, (272, 128), 1) == 0
            for ch in range(2):
                for j in range(2):
                    before = turn(ext[ch, tile + j - 1, pl.ds(top, 272), :], 1)
                    slope[ch, j] += jnp.where(first, -0.5 * before, 0.0)

        def leave(i, _):
            rows = [pl.multiple_of(i * 16 + 128 * h, 16) for h in range(2)]
            for j in range(2):
                cols = slice(128 * j, 128 * (j + 1))
                o = [[patch[ch, j, pl.ds(rw + 8, 16), :] for ch in range(2)] for rw in rows]
                for m in range(2):
                    e = []
                    for h in range(2):
                        pr = probe[m, 0, pl.ds(rows[h], 16), cols]
                        pi = probe[m, 1, pl.ds(rows[h], 16), cols]
                        e.append((pr * o[h][0] - pi * o[h][1], pr * o[h][1] + pi * o[h][0]))
                    for ch in range(2):
                        at = pl.ds(pl.multiple_of(i * 16 + 128 * ch, 16), 16)
                        for k, v in enumerate((e[0][ch] + e[1][ch], e[0][ch] - e[1][ch])):
                            high, low = split(v)
                            xs[m, 2 * k, at, cols] = high
                            xs[m, 2 * k + 1, at, cols] = low
            return 0

        lax.fori_loop(0, 8, leave, 0, unroll=True)

        def left_mm(k, high, low):
            return mm(tables[2 * k], high) + mm(tables[2 * k], low) + mm(tables[2 * k + 1], high)

        def right_mm(k, high, low):
            return mm(high, tables[2 * k]) + mm(low, tables[2 * k]) + mm(high, tables[2 * k + 1])

        for m in range(2):
            for k in range(2):
                y = left_mm(k, xs[m, 2 * k], xs[m, 2 * k + 1])
                for ch in range(2):
                    a, b = y[128 * ch : 128 * (ch + 1), :128], y[128 * ch : 128 * (ch + 1), 128:]
                    for q, v in enumerate((a + b, a - b)):
                        high, low = split(v)
                        at = (slice(128 * k, 128 * (k + 1)), slice(128 * ch, 128 * (ch + 1)))
                        ts[m, 2 * q, *at] = high
                        ts[m, 2 * q + 1, *at] = low
        for q in range(2):
            y = right_mm(2 + q, ts[:, 2 * q].reshape(512, 256), ts[:, 2 * q + 1].reshape(512, 256))
            for m in range(2):
                zs[m, q] = y[256 * m : 256 * (m + 1)]

        def project(i, _):
            at = pl.ds(pl.multiple_of(i * 16, 16), 16)
            for q in range(2):
                z = [[zs[m, q, at, 128 * ch : 128 * (ch + 1)] for ch in range(2)] for m in range(2)]
                amp = z[0][0] ** 2 + z[0][1] ** 2 + z[1][0] ** 2 + z[1][1] ** 2
                factor = spat[slot, at, 128 * q : 128 * (q + 1)] * lax.rsqrt(jnp.maximum(amp, 0.0625))
                for m in range(2):
                    for ch in range(2):
                        high, low = split(z[m][ch] * factor)
                        ts[m, 2 * q, at, 128 * ch : 128 * (ch + 1)] = high
                        ts[m, 2 * q + 1, at, 128 * ch : 128 * (ch + 1)] = low
            return 0

        lax.fori_loop(0, 16, project, 0, unroll=True)

        both_a = right_mm(0, ts[:, 0].reshape(512, 256), ts[:, 1].reshape(512, 256))
        both_b = right_mm(1, ts[:, 2].reshape(512, 256), ts[:, 3].reshape(512, 256))
        for m in range(2):
            a = both_a[256 * m : 256 * (m + 1)]
            b = both_b[256 * m : 256 * (m + 1)]
            for half, v in enumerate((a + b, a - b)):
                high, low = split(v)
                for k in range(2):
                    for ch in range(2):
                        at = (slice(128 * ch, 128 * (ch + 1)), slice(128 * half, 128 * (half + 1)))
                        pick = (slice(128 * k, 128 * (k + 1)), slice(128 * ch, 128 * (ch + 1)))
                        xs[m, 2 * k, *at] = high[pick]
                        xs[m, 2 * k + 1, *at] = low[pick]
            u = left_mm(2, xs[m, 0], xs[m, 1])
            v = left_mm(3, xs[m, 2], xs[m, 3])
            for ch in range(2):
                at = slice(128 * ch, 128 * (ch + 1))
                rev[m, ch, 0:128, :] = u[at] + v[at]
                rev[m, ch, 128:256, :] = u[at] - v[at]

        tile_g, shift_g = left // 128, lax.rem(left, 128)
        keep = lax.broadcasted_iota(jnp.int32, (STEP, 128), 1) >= shift_g

        def fold(x):
            return sum(x[8 * k : 8 * (k + 1)] for k in range(STEP // 8))

        def finish(i, acc):
            at = pl.ds(pl.multiple_of(i * STEP, STEP), STEP)
            dst = pl.ds(top + 8 + i * STEP, STEP)
            g = []
            acc = list(acc)
            for j in range(2):
                cols = slice(128 * j, 128 * (j + 1))
                o_re = patch[0, j, pl.ds(i * STEP + 8, STEP), :]
                o_im = patch[1, j, pl.ds(i * STEP + 8, STEP), :]
                w = power[j, at, :]
                g_re, g_im = -w * o_re, -w * o_im
                for m in range(2):
                    p_re, p_im = probe[m, 0, at, cols], probe[m, 1, at, cols]
                    v_re, v_im = rev[m, 0, at, cols], rev[m, 1, at, cols]
                    g_re += p_re * v_re + p_im * v_im
                    g_im += p_re * v_im - p_im * v_re
                    probe_out[2 * m, j, at, :] += o_re * v_re + o_im * v_im
                    probe_out[2 * m + 1, j, at, :] += o_re * v_im - o_im * v_re
                probe_out[4, j, at, :] += o_re * o_re + o_im * o_im
                d_re = 0.5 * (
                    patch[0, j, pl.ds(i * STEP + 9, STEP), :] - patch[0, j, pl.ds(i * STEP + 7, STEP), :]
                )
                d_im = 0.5 * (
                    patch[1, j, pl.ds(i * STEP + 9, STEP), :] - patch[1, j, pl.ds(i * STEP + 7, STEP), :]
                )
                s_re = slope[0, j, pl.ds(i * STEP + 8, STEP), :]
                s_im = slope[1, j, pl.ds(i * STEP + 8, STEP), :]
                acc[0] += fold(g_re * d_re + g_im * d_im)
                acc[1] += fold(w * (d_re * d_re + d_im * d_im))
                acc[2] += fold(g_re * s_re + g_im * s_im)
                acc[3] += fold(w * (s_re * s_re + s_im * s_im))
                g.append((g_re, g_im))
            for ch in range(2):
                a, b = turn(g[0][ch], shift_g), turn(g[1][ch], shift_g)
                grad[ch, tile_g, dst, :] += jnp.where(keep, a, 0.0)
                grad[ch, tile_g + 1, dst, :] += jnp.where(keep, b, a)
                grad[ch, tile_g + 2, dst, :] += jnp.where(keep, 0.0, b)
            a, b = turn(power[0, at, :], shift_g), turn(power[1, at, :], shift_g)
            dst = pl.ds(top + HALF + i * STEP, STEP)
            canvas[tile_g + 1, dst, :] += jnp.where(keep, a, 0.0)
            canvas[tile_g + 2, dst, :] += jnp.where(keep, b, a)
            canvas[tile_g + 3, dst, :] += jnp.where(keep, 0.0, b)
            return tuple(acc)

        acc = lax.fori_loop(0, WIN // STEP, finish, (zero,) * 4, unroll=True)
        total = [jnp.sum(acc[k], axis=(0, 1), keepdims=True) for k in range(4)]
        at_row = lax.broadcasted_iota(jnp.int32, (8, 128), 0) == slot
        for k in range(2):
            value = total[2 * k] * lax.rsqrt(total[2 * k + 1] + 1e-6)
            raw[...] += jnp.where(at_row & (lane == k), value, 0.0)
        return 0

    lax.fori_loop(0, where[4, 0, 2 * CAP], visit, 0)
    for t in range(3):
        weight[:, 128 * t : 128 * (t + 1)] = canvas[2 + t, pl.ds(WIN, TILE), :]


def slots(where, ext, probe, spat, tables):
    v = pl.BlockSpec(memory_space=VMEM)
    return pl.pallas_call(
        slots_kernel,
        out_shape=(
            jax.ShapeDtypeStruct((2, 5, EXT_ROWS, 128), f32),
            jax.ShapeDtypeStruct((TILE, TILE), f32),
            jax.ShapeDtypeStruct((5, 2, WIN, 128), f32),
            jax.ShapeDtypeStruct((8, 128), f32),
        ),
        in_specs=[pl.BlockSpec(memory_space=pltpu.SMEM), v, v, v, pl.BlockSpec(memory_space=pltpu.HBM)],
        out_specs=[v, v, v, v],
        scratch_shapes=[
            VMEM((2, 2, 272, 128), f32),
            VMEM((2, 2, 272, 128), f32),
            VMEM((2, 4, WIN, WIN), bf16),
            VMEM((2, 4, WIN, WIN), bf16),
            VMEM((2, 2, WIN, WIN), f32),
            VMEM((2, 2, WIN, WIN), f32),
            VMEM((2, WIN, 128), f32),
            VMEM((8, 904, 128), f32),
            VMEM((8, WIN, WIN), bf16),
            pltpu.SemaphoreType.DMA,
        ],
        compiler_params=pltpu.CompilerParams(vmem_limit_bytes=24 * 2**20),
        name="slots",
    )(where, ext, probe, spat, tables)


SHARDS = 32
SHARD = 80
PIECE = SHARD + 8


def plane(dx, dy):
    r, c = lax.axis_index("row"), lax.axis_index("col")
    return (lax.rem(r + 4 * dx, 16), lax.rem(c + 4 * dy, 16))


def depth_of():
    r, c = lax.axis_index("row"), lax.axis_index("col")
    return 4 * lax.rem(r // 2, 2) + lax.rem(c, 4)


def along(dz):
    r, c = lax.axis_index("row"), lax.axis_index("col")
    z = lax.rem(depth_of() + dz, 8)
    return (r // 4 * 4 + z // 4 * 2 + lax.rem(r, 2), c // 4 * 4 + lax.rem(z, 4))


def sums_kernel(
    grad,
    weight,
    obj,
    probe,
    part,
    raw,
    obj_new,
    probe_new,
    step,
    mate_rows,
    corner_in,
    row_out,
    row_in,
    side_out,
    side_in,
    mine,
    mate_part,
    plane_part,
    deep,
    deep_part,
    deep_all,
    all_sum,
    flat,
    hsend,
    hrecv,
    csend,
    crecv,
    psend,
    precv,
    zsend,
    zrecv,
):
    r, c = lax.axis_index("row"), lax.axis_index("col")
    n_row, n_col = lax.axis_size("row"), lax.axis_size("col")
    core = lax.rem(r, 2)
    own = r // 4 * 4 + c // 4
    z = depth_of()
    mate = (r + 1 - 2 * core, c)
    beyond = (lax.rem(r - 1 + 2 * core + n_row, n_row), c)
    left, right = neighbour((0, -1)), neighbour((0, 1))
    planes = [(dx, dy) for dx in range(4) for dy in range(4) if (dx, dy) != (0, 0)]

    barrier = pltpu.get_barrier_semaphore()
    partners = [left, right, mate, beyond, (beyond[0], left[1]), (beyond[0], right[1])]
    partners += [plane(*p) for p in planes] + [along(d) for d in range(1, 8)]
    for partner in partners:
        pl.semaphore_signal(barrier, inc=1, device_id=partner, device_id_type=MESH)

    def gather(i, _):
        mine[i, 0:SHARD, :] = part[pl.ds(pl.multiple_of(i * SHARD, SHARD), SHARD), :]
        mine[i, SHARD:PIECE, :] = raw[...]
        return 0

    lax.fori_loop(0, SHARDS, gather, 0)
    pl.semaphore_wait(barrier, len(partners))

    outer_from = pl.multiple_of(8 + 512 * core, 8)
    inner_from = pl.multiple_of(520 - 512 * core, 8)
    outer_to = pl.multiple_of(256 * core, 8)
    inner_to = pl.multiple_of(256 - 256 * core, 8)
    col_ok = [c > 0, c < n_col - 1]
    outer_ok = jnp.where(core == 0, r, n_row - 1 - r) > 0

    half = SHARDS // 2
    to_mate = send(
        mine.at[pl.ds(half * (1 - core), half)], mate_part, csend.at[0], crecv.at[0], mate
    )
    rows_to_mate = send(
        grad.at[:, :, pl.ds(inner_from, 128), :], mate_rows, csend.at[2], crecv.at[2], mate
    )
    edge = pl.ds(outer_from, 128)
    has_left, has_right = col_ok
    far_left, far_right = lax.rem(c, 4) == 0, lax.rem(c, 4) == 3

    def corner(tile, k, to):
        return make(grad.at[:, tile, edge, :], corner_in.at[k], hsend.at[k], hrecv.at[k], to)

    corner_r, corner_l = corner(4, 0, right), corner(0, 1, left)
    jump_r, jump_l = corner(4, 0, (beyond[0], right[1])), corner(0, 1, (beyond[0], left[1]))
    when(has_right & jnp.logical_not(far_right), corner_r.start)
    when(has_left & jnp.logical_not(far_left), corner_l.start)
    when(has_right & far_right & outer_ok, jump_r.start)
    when(has_left & far_left & outer_ok, jump_l.start)
    corner_left = has_left & (jnp.logical_not(far_left) | outer_ok)
    corner_right = has_right & (jnp.logical_not(far_right) | outer_ok)
    jumped = [has_left & far_left & outer_ok, has_right & far_right & outer_ok]

    rows_to_mate.wait()
    def fill_sides(ch):
        for k, tile in enumerate((4, 0)):
            side_out[k, ch] = grad[ch, tile, 136:520, :]
            side_out[k, ch, pl.ds(inner_to, 128), :] += mate_rows[ch, tile]

    def side(ch, k):
        i = 2 + 2 * k + ch
        return make(side_out.at[k, ch], side_in.at[k, ch], hsend.at[i], hrecv.at[i], (right, left)[k])

    sides = [[side(ch, k) for k in range(2)] for ch in range(2)]

    fill_sides(0)
    fill_sides(1)
    to_mate.wait()

    def add_mate(i, _):
        mine[half * core + i] += mate_part[i]
        return 0

    lax.fori_loop(0, half, add_mate, 0)
    copies = []
    for i, (dx, dy) in enumerate(planes):
        to = plane(dx, dy)
        owner = to[0] // 4 * 4 + to[1] // 4
        copies.append(
            send(mine.at[half * core + owner], plane_part.at[i], psend.at[i], precv.at[i], to)
        )
    finish_copy(corner_r, corner_right, corner_left)
    finish_copy(corner_l, corner_left, corner_right)
    for ch in range(2):
        for t in range(3):
            v = grad[ch, 1 + t, edge, :]
            if t == 0:
                v = v + jnp.where(has_left & jnp.logical_not(far_left), corner_in[0, ch], 0.0)
            if t == 2:
                v = v + jnp.where(has_right & jnp.logical_not(far_right), corner_in[1, ch], 0.0)
            row_out[ch, t] = v
    strip = make(row_out, row_in, hsend.at[6], hrecv.at[6], beyond)
    when(outer_ok, strip.start)
    for copy in copies:
        copy.wait()
    total = mine[half * core + own]
    for i in range(15):
        total = total + plane_part[i]
    deep[0:PIECE, :] = total
    deep[PIECE:128, :] = jnp.zeros((128 - PIECE, 128), f32)
    copies = []
    for d in range(1, 8):
        there = lax.rem(z + d, 8)
        copies.append(
            send(
                deep.at[pl.ds(pl.multiple_of(there * 16, 16), 16)],
                deep_part.at[d - 1],
                zsend.at[d - 1],
                zrecv.at[d - 1],
                along(d),
            )
        )
    for copy in copies:
        copy.wait()
    total = deep[pl.ds(pl.multiple_of(z * 16, 16), 16), :]
    for d in range(7):
        total = total + deep_part[d]
    here = deep_all.at[pl.ds(pl.multiple_of(z * 16, 16), 16)]
    deep_all[pl.ds(pl.multiple_of(z * 16, 16), 16), :] = total
    copies = [send(here, here, zsend.at[6 + d], zrecv.at[6 + d], along(d)) for d in range(1, 8)]
    for ch in range(2):
        when(has_right, sides[ch][0].start)
        when(has_left, sides[ch][1].start)
    for copy in copies:
        copy.wait()
    all_sum[half * core + own] = deep_all[0:PIECE, :]
    block = all_sum.at[half * core + own]
    copies = [
        send(block, block, psend.at[15 + i], precv.at[15 + i], plane(*p)) for i, p in enumerate(planes)
    ]
    for copy in copies:
        copy.wait()
    block = all_sum.at[pl.ds(half * core, half)]
    to_mate = send(block, block, csend.at[1], crecv.at[1], mate)

    def peak(i, top):
        rows = pl.ds(pl.multiple_of(i * 8, 8), 8)
        power = probe[0, 0, rows, :] ** 2 + probe[0, 1, rows, :] ** 2
        power = power + probe[1, 0, rows, :] ** 2 + probe[1, 1, rows, :] ** 2
        return jnp.maximum(top, power)

    top = lax.fori_loop(0, WIN // 8, peak, jnp.zeros((8, WIN), f32))
    floor = 0.1 * jnp.max(top, axis=(0, 1), keepdims=True)

    to_mate.wait()

    def spread(i, _):
        flat[pl.ds(pl.multiple_of(i * SHARD, SHARD), SHARD), :] = all_sum[i, 0:SHARD, :]
        return 0

    lax.fori_loop(0, SHARDS, spread, 0)

    def peak_sum(i, top):
        return jnp.maximum(top, flat[pl.ds(pl.multiple_of(2048 + i * 8, 8), 8), :])

    top = lax.fori_loop(0, 64, peak_sum, jnp.zeros((8, 128), f32))
    floor_p = 0.1 * jnp.max(top, axis=(0, 1), keepdims=True)

    def renew(i, _):
        rows = pl.ds(pl.multiple_of(i * 8, 8), 8)
        for j in range(2):
            cols = slice(128 * j, 128 * (j + 1))

            def at(k):
                return flat[pl.ds(pl.multiple_of((2 * k + j) * WIN + i * 8, 8), 8), :]

            wp = at(4)
            scale = 1.0 / (wp + floor_p)
            for m in range(2):
                for ch in range(2):
                    old = probe[m, ch, rows, cols]
                    probe_new[m, ch, rows, cols] = old + (at(2 * m + ch) - old * wp) * scale
        return 0

    lax.fori_loop(0, WIN // 8, renew, 0)

    rows8 = lax.broadcasted_iota(jnp.int32, (8, 128), 0)
    lanes8 = lax.broadcasted_iota(jnp.int32, (8, 128), 1)
    is_count = (rows8 == 7) & (lanes8 == 2)
    sums = all_sum[0, SHARD:PIECE, :]
    count = jnp.sum(jnp.where(is_count, sums, 0.0), axis=(0, 1), keepdims=True)
    mine_count = jnp.sum(jnp.where(is_count, raw[...], 0.0), axis=(0, 1), keepdims=True)
    mean = jnp.sum(sums, axis=0, keepdims=True) / count
    step[...] = jnp.where(rows8.astype(f32) < mine_count, raw[...] - mean, 0.0)

    for ch in range(2):
        finish_copy(sides[ch][0], has_right, has_left)
        finish_copy(sides[ch][1], has_left, has_right)
    for band, start in ((1, 128), (2, inner_to), (0, outer_to)):
        if band == 0:
            finish_copy(strip, outer_ok, outer_ok)

        def update(i, _, band=band, start=start):
            rows = pl.ds(pl.multiple_of(start + i * 8, 8), 8)
            thin = pl.ds(pl.multiple_of(i * 8, 8), 8)
            for t in range(3):
                cols = slice(128 * t, 128 * (t + 1))
                down = weight[rows, cols] + floor
                for ch in range(2):
                    g = grad[ch, 1 + t, pl.ds(pl.multiple_of(136 + start + i * 8, 8), 8), :]
                    if band == 0:
                        g = g + jnp.where(outer_ok, row_in[ch, t, thin, :], 0.0)
                        if t != 1:
                            g = g + jnp.where(jumped[t // 2], corner_in[t // 2, ch, thin, :], 0.0)
                    if band == 2:
                        g = g + mate_rows[ch, 1 + t, thin, :]
                    if t == 0:
                        g = g + jnp.where(col_ok[0], side_in[0, ch, rows, :], 0.0)
                    if t == 2:
                        g = g + jnp.where(col_ok[1], side_in[1, ch, rows, :], 0.0)
                    obj_new[ch, rows, cols] = obj[ch, rows, cols] + g / down
            return 0

        lax.fori_loop(0, 16, update, 0, unroll=2)


def sums(grad, weight, obj, probe, part, raw):
    v = pl.BlockSpec(memory_space=VMEM)
    dma = pltpu.SemaphoreType.DMA
    return pl.pallas_call(
        sums_kernel,
        out_shape=(
            jax.ShapeDtypeStruct((2, TILE, TILE), f32),
            jax.ShapeDtypeStruct((2, 2, WIN, WIN), f32),
            jax.ShapeDtypeStruct((8, 128), f32),
        ),
        in_specs=[v] * 6,
        out_specs=[v] * 3,
        scratch_shapes=[
            VMEM((2, 5, 128, 128), f32),
            VMEM((2, 2, 128, 128), f32),
            VMEM((2, 3, 128, 128), f32),
            VMEM((2, 3, 128, 128), f32),
            VMEM((2, 2, TILE, 128), f32),
            VMEM((2, 2, TILE, 128), f32),
            VMEM((SHARDS, PIECE, 128), f32),
            VMEM((SHARDS // 2, PIECE, 128), f32),
            VMEM((15, PIECE, 128), f32),
            VMEM((128, 128), f32),
            VMEM((7, 16, 128), f32),
            VMEM((128, 128), f32),
            VMEM((SHARDS, PIECE, 128), f32),
            VMEM((SHARDS * SHARD, 128), f32),
            dma((7,)),
            dma((7,)),
            dma((3,)),
            dma((3,)),
            dma((30,)),
            dma((30,)),
            dma((14,)),
            dma((14,)),
        ],
        compiler_params=pltpu.CompilerParams(
            collective_id=1, has_side_effects=True, vmem_limit_bytes=28 * 2**20
        ),
        name="sums",
    )(grad, weight, obj, probe, part, raw)


def on_device(object_field, probe, patterns, positions, counts):
    meta = jnp.concatenate([positions.reshape(1, 2 * CAP), counts.reshape(1, 1)], axis=1)
    meta = jnp.pad(meta, ((0, 7), (0, 128 - 2 * CAP - 1)))
    ext, spat, where = halo(object_field, patterns[0, 0], meta)
    grad, weight, part, raw = slots(where, ext, probe, spat, jnp.asarray(dft_tables()))
    object_new, probe_new, step = sums(
        grad, weight, object_field, probe, part.reshape(SHARDS * SHARD, 128), raw
    )
    return object_new, probe_new, step[:CAP, :2].reshape(1, 1, CAP, 2)


def solution(mesh):
    placed = (
        P(None, "row", "col"),
        P(),
        P("row", "col", None, None, None),
        P("row", "col", None, None),
        P("row", "col"),
    )
    return jax.shard_map(
        on_device,
        mesh=mesh,
        in_specs=placed,
        out_specs=(P(None, "row", "col"), P(), P("row", "col", None, None)),
        check_vma=False,
    )
```

```python
import functools

import jax
import jax.numpy as jnp
import ml_dtypes
import numpy as np
from jax import lax
from jax.experimental import pallas as pl
from jax.experimental.pallas import tpu as pltpu
from jax.sharding import PartitionSpec as P

MESH = pl.DeviceIdType.MESH
VMEM = pltpu.VMEM
f32 = jnp.float32
bf16 = jnp.bfloat16

WIN = 256
HALF = 128
TILE = 384
CAP = 6
STEP = 32
EXT_ROWS = 8 + HALF + TILE + HALF + 8
OFFSETS = [(-1, 0), (1, 0), (0, -1), (0, 1), (-1, -1), (-1, 1), (1, -1), (1, 1)]


def dft_tables():
    k = np.arange(HALF)
    even = np.exp(-2j * np.pi * np.outer(2 * k, k) / WIN) / np.sqrt(WIN)
    odd = np.exp(-2j * np.pi * np.outer(2 * k + 1, k) / WIN) / np.sqrt(WIN)

    def block(z):
        return np.block([[z.real, -z.imag], [z.imag, z.real]])

    out = []
    for mat in (block(even), block(odd), block(even).T, block(odd).T):
        high = mat.astype(np.float32).astype(ml_dtypes.bfloat16)
        low = (mat - high.astype(np.float64)).astype(np.float32).astype(ml_dtypes.bfloat16)
        out += [high, low]
    return np.stack(out)


def split(x):
    high = x.astype(bf16)
    return high, (x - high.astype(f32)).astype(bf16)


def mm(a, b):
    return jnp.dot(a, b, preferred_element_type=f32)


def neighbour(step):
    n_row, n_col = lax.axis_size("row"), lax.axis_size("col")
    r, c = lax.axis_index("row"), lax.axis_index("col")
    return (lax.rem(r + step[0] + n_row, n_row), lax.rem(c + step[1] + n_col, n_col))


def greet():
    barrier = pltpu.get_barrier_semaphore()
    for step in OFFSETS:
        pl.semaphore_signal(barrier, inc=1, device_id=neighbour(step), device_id_type=MESH)
    pl.semaphore_wait(barrier, len(OFFSETS))


def send(src, dst, ssem, rsem, to):
    copy = pltpu.make_async_remote_copy(
        src_ref=src, dst_ref=dst, send_sem=ssem, recv_sem=rsem, device_id=to, device_id_type=MESH
    )
    copy.start()
    return copy


def when(condition, act):
    @pl.when(condition)
    def _():
        act()


def finish_copy(copy, sent, received):
    when(sent, copy.wait_send)
    when(received, copy.wait_recv)


def make(src, dst, ssem, rsem, to):
    return pltpu.make_async_remote_copy(
        src_ref=src, dst_ref=dst, send_sem=ssem, recv_sem=rsem, device_id=to, device_id_type=MESH
    )


def halo_kernel(
    obj, pats_far, meta, ext, spat, metas, pats, turned, lsem, ssem, rsem, msend, mrecv
):
    r, c = lax.axis_index("row"), lax.axis_index("col")
    core = lax.rem(r, 2)
    load = pltpu.make_async_copy(pats_far, pats, lsem)
    load.start()
    has_up, has_down = r > 0, r < lax.axis_size("row") - 1
    has_left, has_right = c > 0, c < lax.axis_size("col") - 1

    for ch in range(2):
        for t in range(5):
            ext[ch, t, 0:8, :] = jnp.zeros((8, 128), f32)
            ext[ch, t, 648:656, :] = jnp.zeros((8, 128), f32)

    def blank(tiles, rows):
        ext[:, tiles, rows, :] = jnp.zeros((2, tiles.stop - tiles.start, rows.stop - rows.start, 128), f32)

    when(r == 0, lambda: blank(slice(0, 5), slice(8, 136)))
    when(jnp.logical_not(has_down), lambda: blank(slice(0, 5), slice(520, 648)))
    when(c == 0, lambda: blank(slice(0, 1), slice(8, 648)))
    when(jnp.logical_not(has_right), lambda: blank(slice(4, 5), slice(8, 648)))
    greet()
    for t in range(3):
        for ch in range(2):
            ext[ch, 1 + t, 136:520, :] = obj[ch, :, 128 * t : 128 * (t + 1)]
    metas[4] = meta[...]

    def strip(tile, tiles, row, rows):
        return ext.at[:, pl.ds(tile, tiles), pl.ds(row, rows), :]

    left, right = neighbour((0, -1)), neighbour((0, 1))
    outer = pl.multiple_of(8 + 512 * core, 8)
    up = make(strip(1, 3, 136, 128), strip(1, 3, 520, 128), ssem.at[0], rsem.at[0], neighbour((-1, 0)))
    down = make(strip(1, 3, 392, 128), strip(1, 3, 8, 128), ssem.at[1], rsem.at[1], neighbour((1, 0)))
    to_left = make(strip(1, 1, 136, 384), strip(4, 1, 136, 384), ssem.at[4], rsem.at[4], left)
    to_right = make(strip(3, 1, 136, 384), strip(0, 1, 136, 384), ssem.at[5], rsem.at[5], right)
    when(has_up, up.start)
    when(has_down, down.start)
    far_left, far_right = lax.rem(c, 4) == 0, lax.rem(c, 4) == 3
    when(has_left & far_left, to_left.start)
    when(has_right & far_right, to_right.start)
    beyond = lax.rem(r - 1 + 2 * core + lax.axis_size("row"), lax.axis_size("row"))
    outer_ok = jnp.where(core == 0, r, lax.axis_size("row") - 1 - r) > 0
    own_edge, its_edge = pl.multiple_of(136 + 256 * core, 8), pl.multiple_of(520 - 512 * core, 8)
    jump_l = make(
        strip(1, 1, own_edge, 128), strip(4, 1, its_edge, 128), ssem.at[2], rsem.at[2], (beyond, left[1])
    )
    jump_r = make(
        strip(3, 1, own_edge, 128), strip(0, 1, its_edge, 128), ssem.at[3], rsem.at[3], (beyond, right[1])
    )
    when(has_left & far_left & outer_ok, jump_l.start)
    when(has_right & far_right & outer_ok, jump_r.start)
    small = [
        send(
            metas.at[4],
            metas.at[(1 - dr) * 3 + 1 - dc],
            msend.at[i],
            mrecv.at[i],
            neighbour((dr, dc)),
        )
        for i, (dr, dc) in enumerate(OFFSETS)
    ]
    when(has_left & jnp.logical_not(far_left), to_left.start)
    when(has_right & jnp.logical_not(far_right), to_right.start)
    load.wait()
    order = []
    for parity in range(2):
        index = lax.broadcasted_iota(jnp.int32, (WIN, HALF), 0)
        wanted = 2 * lax.broadcasted_iota(jnp.int32, (WIN, HALF), 1) + parity
        order.append(jnp.where(index == wanted, 1.0, 0.0).astype(bf16))
    order = jnp.concatenate(order, axis=1)

    def reorder(slot, _):
        high, low = split(jnp.sqrt(pats[slot]))
        sorted_cols = mm(high, order) + mm(low, order)
        for j in range(2):
            turned[j] = sorted_cols[:, 128 * j : 128 * (j + 1)]
        for parity in range(2):
            for j in range(2):
                spat[slot, 128 * parity : 128 * (parity + 1), 128 * j : 128 * (j + 1)] = turned[
                    j, pl.ds(parity, 128, stride=2), :
                ]
        return 0

    lax.fori_loop(0, CAP, reorder, 0)
    finish_copy(up, has_up, has_down)
    finish_copy(down, has_down, has_up)
    far_l = make(strip(1, 1, outer, 128), strip(4, 1, outer, 128), ssem.at[2], rsem.at[2], left)
    far_r = make(strip(3, 1, outer, 128), strip(0, 1, outer, 128), ssem.at[3], rsem.at[3], right)
    when(has_left & jnp.logical_not(far_left), far_l.start)
    when(has_right & jnp.logical_not(far_right), far_r.start)
    mate = (r + 1 - 2 * core, c)
    near = pl.multiple_of(392 - 256 * core, 8)
    relays = []
    for k, (tile, copy, sent, received) in enumerate(
        ((4, to_left, has_left, has_right), (0, to_right, has_right, has_left))
    ):
        finish_copy(copy, sent, received)
        relays.append(
            send(strip(tile, 1, near, 128), strip(tile, 1, outer, 128), ssem.at[6 + k], rsem.at[6 + k], mate)
        )
    sent_left = has_left & (jnp.logical_not(far_left) | outer_ok)
    sent_right = has_right & (jnp.logical_not(far_right) | outer_ok)
    finish_copy(far_l, sent_left, sent_right)
    finish_copy(far_r, sent_right, sent_left)
    for copy in relays + small:
        copy.wait()


def halo(obj, pats, meta):
    return pl.pallas_call(
        halo_kernel,
        out_shape=(
            jax.ShapeDtypeStruct((2, 5, EXT_ROWS, 128), f32),
            jax.ShapeDtypeStruct((CAP, WIN, WIN), f32),
            jax.ShapeDtypeStruct((9, 8, 128), jnp.int32),
        ),
        in_specs=[
            pl.BlockSpec(memory_space=VMEM),
            pl.BlockSpec(memory_space=pltpu.HBM),
            pl.BlockSpec(memory_space=VMEM),
        ],
        out_specs=[pl.BlockSpec(memory_space=VMEM)] * 3,
        scratch_shapes=[
            VMEM((CAP, WIN, WIN), f32),
            VMEM((2, WIN, 128), f32),
            pltpu.SemaphoreType.DMA,
            pltpu.SemaphoreType.DMA((8,)),
            pltpu.SemaphoreType.DMA((8,)),
            pltpu.SemaphoreType.DMA((8,)),
            pltpu.SemaphoreType.DMA((8,)),
        ],
        compiler_params=pltpu.CompilerParams(
            collective_id=0, has_side_effects=True, vmem_limit_bytes=20 * 2**20
        ),
        name="halo_in",
    )(obj, pats, meta)


def turn(x, shift):
    return pltpu.roll(x, shift, 1)


def slots_kernel(
    where,
    ext,
    probe,
    spat,
    tables_far,
    grad,
    weight,
    probe_out,
    raw,
    patch,
    slope,
    xs,
    ts,
    zs,
    rev,
    power,
    canvas,
    tables,
    lsem,
):
    load = pltpu.make_async_copy(tables_far, tables, lsem)
    load.start()
    r, c = lax.axis_index("row"), lax.axis_index("col")
    row_start, col_start = r * TILE, c * TILE
    lane = lax.broadcasted_iota(jnp.int32, (8, 128), 1)
    zero = jnp.zeros((8, 128), f32)

    def clear(ref, lead, rows):
        def step(i, _):
            for ix in lead:
                ref[(*ix, pl.ds(pl.multiple_of(i * 8, 8), 8), slice(None))] = zero
            return 0

        lax.fori_loop(0, rows // 8, step, 0, unroll=2)

    clear(grad, [(ch, t) for ch in range(2) for t in range(5)], EXT_ROWS)
    clear(probe_out, [(i, t) for i in range(5) for t in range(2)], WIN)
    for t in range(3):
        canvas[2 + t, WIN : WIN + TILE, :] = jnp.zeros((TILE, 128), f32)
    raw[...] = jnp.where(
        (lax.broadcasted_iota(jnp.int32, (8, 128), 0) == 7) & (lane == 2),
        where[4, 0, 2 * CAP].astype(f32),
        0.0,
    )

    def fill_power(i, _):
        rows = pl.ds(pl.multiple_of(i * 8, 8), 8)
        for j in range(2):
            cols = slice(128 * j, 128 * (j + 1))
            power[j, rows, :] = (
                probe[0, 0, rows, cols] ** 2
                + probe[0, 1, rows, cols] ** 2
                + probe[1, 0, rows, cols] ** 2
                + probe[1, 1, rows, cols] ** 2
            )
        return 0

    lax.fori_loop(0, WIN // 8, fill_power, 0, unroll=4)

    for j in (0, 1, 2, 3, 5, 6, 7, 8):
        jr, jc = j // 3 - 1, j % 3 - 1
        inside = (r + jr >= 0) & (r + jr < lax.axis_size("row")) & (c + jc >= 0) & (c + jc < lax.axis_size("col"))
        live = jnp.where(inside, where[j, 0, 2 * CAP], 0)

        def place(slot, _, j=j, jr=jr, jc=jc):
            top = where[j, 0, 2 * slot] - row_start
            left = where[j, 0, 2 * slot + 1] - col_start

            @pl.when((top > -WIN) & (top < TILE) & (left > -WIN) & (left < TILE))
            def _():
                at = left + WIN
                tile, shift = at // 128, lax.rem(at, 128)
                begin, rows = {-1: (HALF, HALF), 0: (0, WIN), 1: (0, HALF)}[jr]
                for start in range(begin, begin + rows, 64):
                    keep = lax.broadcasted_iota(jnp.int32, (64, 128), 1) >= shift
                    dst = pl.ds(top + WIN + start, 64)
                    if jc <= 0:
                        b = turn(power[1, start : start + 64, :], shift)
                        canvas[tile + 2, dst, :] += jnp.where(keep, 0.0, b)
                    if jc >= 0:
                        a = turn(power[0, start : start + 64, :], shift)
                        canvas[tile, dst, :] += jnp.where(keep, a, 0.0)
                    if jc == 0:
                        canvas[tile + 1, dst, :] += jnp.where(keep, b, a)

            return 0

        lax.fori_loop(0, live, place, 0)

    load.wait()

    def visit(slot, _):
        top = where[4, 0, 2 * slot] - row_start + HALF
        left = where[4, 0, 2 * slot + 1] - col_start + HALF

        tile, shift = left // 128, lax.rem(left, 128)
        apart = lax.broadcasted_iota(jnp.int32, (256, 128), 0) - lax.broadcasted_iota(
            jnp.int32, (256, 128), 1
        )
        move = jnp.where(apart == shift, 1.0, 0.0).astype(bf16)
        differ = jnp.where(apart == shift + 1, 0.5, jnp.where(apart == shift - 1, -0.5, 0.0)).astype(bf16)
        shifter = jnp.concatenate([move, differ], axis=1)
        for ch in range(2):
            x = [split(ext[ch, tile + t, pl.ds(top, 272), :]) for t in range(3)]
            high, low = (
                jnp.concatenate(
                    [jnp.concatenate([x[j][p], x[j + 1][p]], axis=1) for j in range(2)], axis=0
                )
                for p in range(2)
            )
            y = mm(high, shifter) + mm(low, shifter)
            for j in range(2):
                patch[ch, j] = y[272 * j : 272 * (j + 1), :128]
                slope[ch, j] = y[272 * j : 272 * (j + 1), 128:]

        @pl.when(shift == 0)
        def _():
            first = lax.broadcasted_iota(jnp.int32, (272, 128), 1) == 0
            for ch in range(2):
                for j in range(2):
                    before = turn(ext[ch, tile + j - 1, pl.ds(top, 272), :], 1)
                    slope[ch, j] += jnp.where(first, -0.5 * before, 0.0)

        def leave(i, _):
            rows = [pl.multiple_of(i * 16 + 128 * h, 16) for h in range(2)]
            for j in range(2):
                cols = slice(128 * j, 128 * (j + 1))
                o = [[patch[ch, j, pl.ds(rw + 8, 16), :] for ch in range(2)] for rw in rows]
                for m in range(2):
                    e = []
                    for h in range(2):
                        pr = probe[m, 0, pl.ds(rows[h], 16), cols]
                        pi = probe[m, 1, pl.ds(rows[h], 16), cols]
                        e.append((pr * o[h][0] - pi * o[h][1], pr * o[h][1] + pi * o[h][0]))
                    for ch in range(2):
                        at = pl.ds(pl.multiple_of(i * 16 + 128 * ch, 16), 16)
                        for k, v in enumerate((e[0][ch] + e[1][ch], e[0][ch] - e[1][ch])):
                            high, low = split(v)
                            xs[m, 2 * k, at, cols] = high
                            xs[m, 2 * k + 1, at, cols] = low
            return 0

        lax.fori_loop(0, 8, leave, 0, unroll=True)

        def left_mm(k, high, low):
            return mm(tables[2 * k], high) + mm(tables[2 * k], low) + mm(tables[2 * k + 1], high)

        def right_mm(k, high, low):
            return mm(high, tables[2 * k]) + mm(low, tables[2 * k]) + mm(high, tables[2 * k + 1])

        for m in range(2):
            for k in range(2):
                y = left_mm(k, xs[m, 2 * k], xs[m, 2 * k + 1])
                for ch in range(2):
                    a, b = y[128 * ch : 128 * (ch + 1), :128], y[128 * ch : 128 * (ch + 1), 128:]
                    for q, v in enumerate((a + b, a - b)):
                        high, low = split(v)
                        at = (slice(128 * k, 128 * (k + 1)), slice(128 * ch, 128 * (ch + 1)))
                        ts[m, 2 * q, *at] = high
                        ts[m, 2 * q + 1, *at] = low
        for q in range(2):
            y = right_mm(2 + q, ts[:, 2 * q].reshape(512, 256), ts[:, 2 * q + 1].reshape(512, 256))
            for m in range(2):
                zs[m, q] = y[256 * m : 256 * (m + 1)]

        def project(i, _):
            at = pl.ds(pl.multiple_of(i * 16, 16), 16)
            for q in range(2):
                z = [[zs[m, q, at, 128 * ch : 128 * (ch + 1)] for ch in range(2)] for m in range(2)]
                amp = z[0][0] ** 2 + z[0][1] ** 2 + z[1][0] ** 2 + z[1][1] ** 2
                factor = spat[slot, at, 128 * q : 128 * (q + 1)] * lax.rsqrt(jnp.maximum(amp, 0.0625))
                for m in range(2):
                    for ch in range(2):
                        high, low = split(z[m][ch] * factor)
                        ts[m, 2 * q, at, 128 * ch : 128 * (ch + 1)] = high
                        ts[m, 2 * q + 1, at, 128 * ch : 128 * (ch + 1)] = low
            return 0

        lax.fori_loop(0, 16, project, 0, unroll=True)

        both_a = right_mm(0, ts[:, 0].reshape(512, 256), ts[:, 1].reshape(512, 256))
        both_b = right_mm(1, ts[:, 2].reshape(512, 256), ts[:, 3].reshape(512, 256))
        for m in range(2):
            a = both_a[256 * m : 256 * (m + 1)]
            b = both_b[256 * m : 256 * (m + 1)]
            for half, v in enumerate((a + b, a - b)):
                high, low = split(v)
                for k in range(2):
                    for ch in range(2):
                        at = (slice(128 * ch, 128 * (ch + 1)), slice(128 * half, 128 * (half + 1)))
                        pick = (slice(128 * k, 128 * (k + 1)), slice(128 * ch, 128 * (ch + 1)))
                        xs[m, 2 * k, *at] = high[pick]
                        xs[m, 2 * k + 1, *at] = low[pick]
            u = left_mm(2, xs[m, 0], xs[m, 1])
            v = left_mm(3, xs[m, 2], xs[m, 3])
            for ch in range(2):
                at = slice(128 * ch, 128 * (ch + 1))
                rev[m, ch, 0:128, :] = u[at] + v[at]
                rev[m, ch, 128:256, :] = u[at] - v[at]

        tile_g, shift_g = left // 128, lax.rem(left, 128)
        keep = lax.broadcasted_iota(jnp.int32, (STEP, 128), 1) >= shift_g

        def fold(x):
            return sum(x[8 * k : 8 * (k + 1)] for k in range(STEP // 8))

        def finish(i, acc):
            at = pl.ds(pl.multiple_of(i * STEP, STEP), STEP)
            dst = pl.ds(top + 8 + i * STEP, STEP)
            g = []
            acc = list(acc)
            for j in range(2):
                cols = slice(128 * j, 128 * (j + 1))
                o_re = patch[0, j, pl.ds(i * STEP + 8, STEP), :]
                o_im = patch[1, j, pl.ds(i * STEP + 8, STEP), :]
                w = power[j, at, :]
                g_re, g_im = -w * o_re, -w * o_im
                for m in range(2):
                    p_re, p_im = probe[m, 0, at, cols], probe[m, 1, at, cols]
                    v_re, v_im = rev[m, 0, at, cols], rev[m, 1, at, cols]
                    g_re += p_re * v_re + p_im * v_im
                    g_im += p_re * v_im - p_im * v_re
                    probe_out[2 * m, j, at, :] += o_re * v_re + o_im * v_im
                    probe_out[2 * m + 1, j, at, :] += o_re * v_im - o_im * v_re
                probe_out[4, j, at, :] += o_re * o_re + o_im * o_im
                d_re = 0.5 * (
                    patch[0, j, pl.ds(i * STEP + 9, STEP), :] - patch[0, j, pl.ds(i * STEP + 7, STEP), :]
                )
                d_im = 0.5 * (
                    patch[1, j, pl.ds(i * STEP + 9, STEP), :] - patch[1, j, pl.ds(i * STEP + 7, STEP), :]
                )
                s_re = slope[0, j, pl.ds(i * STEP + 8, STEP), :]
                s_im = slope[1, j, pl.ds(i * STEP + 8, STEP), :]
                acc[0] += fold(g_re * d_re + g_im * d_im)
                acc[1] += fold(w * (d_re * d_re + d_im * d_im))
                acc[2] += fold(g_re * s_re + g_im * s_im)
                acc[3] += fold(w * (s_re * s_re + s_im * s_im))
                g.append((g_re, g_im))
            for ch in range(2):
                a, b = turn(g[0][ch], shift_g), turn(g[1][ch], shift_g)
                grad[ch, tile_g, dst, :] += jnp.where(keep, a, 0.0)
                grad[ch, tile_g + 1, dst, :] += jnp.where(keep, b, a)
                grad[ch, tile_g + 2, dst, :] += jnp.where(keep, 0.0, b)
            a, b = turn(power[0, at, :], shift_g), turn(power[1, at, :], shift_g)
            dst = pl.ds(top + HALF + i * STEP, STEP)
            canvas[tile_g + 1, dst, :] += jnp.where(keep, a, 0.0)
            canvas[tile_g + 2, dst, :] += jnp.where(keep, b, a)
            canvas[tile_g + 3, dst, :] += jnp.where(keep, 0.0, b)
            return tuple(acc)

        acc = lax.fori_loop(0, WIN // STEP, finish, (zero,) * 4, unroll=True)
        total = [jnp.sum(acc[k], axis=(0, 1), keepdims=True) for k in range(4)]
        at_row = lax.broadcasted_iota(jnp.int32, (8, 128), 0) == slot
        for k in range(2):
            value = total[2 * k] * lax.rsqrt(total[2 * k + 1] + 1e-6)
            raw[...] += jnp.where(at_row & (lane == k), value, 0.0)
        return 0

    lax.fori_loop(0, where[4, 0, 2 * CAP], visit, 0)
    for t in range(3):
        weight[:, 128 * t : 128 * (t + 1)] = canvas[2 + t, pl.ds(WIN, TILE), :]


def slots(where, ext, probe, spat, tables):
    v = pl.BlockSpec(memory_space=VMEM)
    return pl.pallas_call(
        slots_kernel,
        out_shape=(
            jax.ShapeDtypeStruct((2, 5, EXT_ROWS, 128), f32),
            jax.ShapeDtypeStruct((TILE, TILE), f32),
            jax.ShapeDtypeStruct((5, 2, WIN, 128), f32),
            jax.ShapeDtypeStruct((8, 128), f32),
        ),
        in_specs=[pl.BlockSpec(memory_space=pltpu.SMEM), v, v, v, pl.BlockSpec(memory_space=pltpu.HBM)],
        out_specs=[v, v, v, v],
        scratch_shapes=[
            VMEM((2, 2, 272, 128), f32),
            VMEM((2, 2, 272, 128), f32),
            VMEM((2, 4, WIN, WIN), bf16),
            VMEM((2, 4, WIN, WIN), bf16),
            VMEM((2, 2, WIN, WIN), f32),
            VMEM((2, 2, WIN, WIN), f32),
            VMEM((2, WIN, 128), f32),
            VMEM((8, 904, 128), f32),
            VMEM((8, WIN, WIN), bf16),
            pltpu.SemaphoreType.DMA,
        ],
        compiler_params=pltpu.CompilerParams(vmem_limit_bytes=24 * 2**20),
        name="slots",
    )(where, ext, probe, spat, tables)


SHARDS = 32
SHARD = 80
PIECE = SHARD + 8


def plane(dx, dy):
    r, c = lax.axis_index("row"), lax.axis_index("col")
    return (lax.rem(r + 4 * dx, 16), lax.rem(c + 4 * dy, 16))


def depth_of():
    r, c = lax.axis_index("row"), lax.axis_index("col")
    return 4 * lax.rem(r // 2, 2) + lax.rem(c, 4)


def along(dz):
    r, c = lax.axis_index("row"), lax.axis_index("col")
    z = lax.rem(depth_of() + dz, 8)
    return (r // 4 * 4 + z // 4 * 2 + lax.rem(r, 2), c // 4 * 4 + lax.rem(z, 4))


def sums_kernel(
    grad,
    weight,
    obj,
    probe,
    part,
    raw,
    obj_new,
    probe_new,
    step,
    mate_rows,
    corner_in,
    row_out,
    row_in,
    middle_in,
    side_out,
    side_in,
    mine,
    mate_part,
    plane_part,
    deep,
    deep_part,
    deep_all,
    all_sum,
    flat,
    hsend,
    hrecv,
    csend,
    crecv,
    psend,
    precv,
    zsend,
    zrecv,
):
    r, c = lax.axis_index("row"), lax.axis_index("col")
    n_row, n_col = lax.axis_size("row"), lax.axis_size("col")
    core = lax.rem(r, 2)
    own = r // 4 * 4 + c // 4
    z = depth_of()
    mate = (r + 1 - 2 * core, c)
    beyond = (lax.rem(r - 1 + 2 * core + n_row, n_row), c)
    left, right = neighbour((0, -1)), neighbour((0, 1))
    planes = [(dx, dy) for dx in range(4) for dy in range(4) if (dx, dy) != (0, 0)]

    barrier = pltpu.get_barrier_semaphore()
    partners = [left, right, mate, beyond, (beyond[0], left[1]), (beyond[0], right[1])]
    partners += [plane(*p) for p in planes] + [along(d) for d in range(1, 8)]
    for partner in partners:
        pl.semaphore_signal(barrier, inc=1, device_id=partner, device_id_type=MESH)

    def gather(i, _):
        mine[i, 0:SHARD, :] = part[pl.ds(pl.multiple_of(i * SHARD, SHARD), SHARD), :]
        mine[i, SHARD:PIECE, :] = raw[...]
        return 0

    lax.fori_loop(0, SHARDS, gather, 0)
    pl.semaphore_wait(barrier, len(partners))

    outer_from = pl.multiple_of(8 + 512 * core, 8)
    inner_from = pl.multiple_of(520 - 512 * core, 8)
    outer_to = pl.multiple_of(256 * core, 8)
    inner_to = pl.multiple_of(256 - 256 * core, 8)
    col_ok = [c > 0, c < n_col - 1]
    outer_ok = jnp.where(core == 0, r, n_row - 1 - r) > 0

    edge = pl.ds(outer_from, 128)
    has_left, has_right = col_ok
    far_left, far_right = lax.rem(c, 4) == 0, lax.rem(c, 4) == 3

    def corner(tile, k, to):
        return make(grad.at[:, tile, edge, :], corner_in.at[k], hsend.at[k], hrecv.at[k], to)

    corner_r, corner_l = corner(4, 0, right), corner(0, 1, left)
    jump_r, jump_l = corner(4, 0, (beyond[0], right[1])), corner(0, 1, (beyond[0], left[1]))
    when(has_right & jnp.logical_not(far_right), corner_r.start)
    when(has_left & jnp.logical_not(far_left), corner_l.start)
    when(has_right & far_right & outer_ok, jump_r.start)
    when(has_left & far_left & outer_ok, jump_l.start)
    middle = make(grad.at[:, 2, edge, :], middle_in, hsend.at[7], hrecv.at[7], beyond)
    when(outer_ok, middle.start)
    corner_left = has_left & (jnp.logical_not(far_left) | outer_ok)
    corner_right = has_right & (jnp.logical_not(far_right) | outer_ok)
    jumped = [has_left & far_left & outer_ok, has_right & far_right & outer_ok]
    half = SHARDS // 2
    to_mate = send(
        mine.at[pl.ds(half * (1 - core), half)], mate_part, csend.at[0], crecv.at[0], mate
    )
    rows_to_mate = send(
        grad.at[:, :, pl.ds(inner_from, 128), :], mate_rows, csend.at[2], crecv.at[2], mate
    )

    rows_to_mate.wait()
    def fill_sides(ch):
        for k, tile in enumerate((4, 0)):
            side_out[k, ch] = grad[ch, tile, 136:520, :]
            side_out[k, ch, pl.ds(inner_to, 128), :] += mate_rows[ch, tile]

    def side(ch, k):
        i = 2 + 2 * k + ch
        return make(side_out.at[k, ch], side_in.at[k, ch], hsend.at[i], hrecv.at[i], (right, left)[k])

    sides = [[side(ch, k) for k in range(2)] for ch in range(2)]

    fill_sides(0)
    fill_sides(1)
    to_mate.wait()

    def add_mate(i, _):
        mine[half * core + i] += mate_part[i]
        return 0

    lax.fori_loop(0, half, add_mate, 0)
    copies = []
    for i, (dx, dy) in enumerate(planes):
        to = plane(dx, dy)
        owner = to[0] // 4 * 4 + to[1] // 4
        copies.append(
            send(mine.at[half * core + owner], plane_part.at[i], psend.at[i], precv.at[i], to)
        )
    finish_copy(corner_r, corner_right, corner_left)
    finish_copy(corner_l, corner_left, corner_right)
    for ch in range(2):
        for k in range(2):
            inside = (has_left & jnp.logical_not(far_left), has_right & jnp.logical_not(far_right))[k]
            row_out[k, ch] = grad[ch, 1 + 2 * k, edge, :] + jnp.where(inside, corner_in[k, ch], 0.0)
    strip = make(row_out, row_in, hsend.at[6], hrecv.at[6], beyond)
    when(outer_ok, strip.start)
    for copy in copies:
        copy.wait()
    total = mine[half * core + own]
    for i in range(15):
        total = total + plane_part[i]
    deep[0:PIECE, :] = total
    deep[PIECE:128, :] = jnp.zeros((128 - PIECE, 128), f32)
    copies = []
    for d in range(1, 8):
        there = lax.rem(z + d, 8)
        copies.append(
            send(
                deep.at[pl.ds(pl.multiple_of(there * 16, 16), 16)],
                deep_part.at[d - 1],
                zsend.at[d - 1],
                zrecv.at[d - 1],
                along(d),
            )
        )
    for copy in copies:
        copy.wait()
    total = deep[pl.ds(pl.multiple_of(z * 16, 16), 16), :]
    for d in range(7):
        total = total + deep_part[d]
    here = deep_all.at[pl.ds(pl.multiple_of(z * 16, 16), 16)]
    deep_all[pl.ds(pl.multiple_of(z * 16, 16), 16), :] = total
    copies = [send(here, here, zsend.at[6 + d], zrecv.at[6 + d], along(d)) for d in range(1, 8)]
    for ch in range(2):
        when(has_right, sides[ch][0].start)
        when(has_left, sides[ch][1].start)
    for copy in copies:
        copy.wait()
    all_sum[half * core + own] = deep_all[0:PIECE, :]
    block = all_sum.at[half * core + own]
    copies = [
        send(block, block, psend.at[15 + i], precv.at[15 + i], plane(*p)) for i, p in enumerate(planes)
    ]
    for copy in copies:
        copy.wait()
    block = all_sum.at[pl.ds(half * core, half)]
    to_mate = send(block, block, csend.at[1], crecv.at[1], mate)

    def peak(i, top):
        rows = pl.ds(pl.multiple_of(i * 8, 8), 8)
        power = probe[0, 0, rows, :] ** 2 + probe[0, 1, rows, :] ** 2
        power = power + probe[1, 0, rows, :] ** 2 + probe[1, 1, rows, :] ** 2
        return jnp.maximum(top, power)

    top = lax.fori_loop(0, WIN // 8, peak, jnp.zeros((8, WIN), f32))
    floor = 0.1 * jnp.max(top, axis=(0, 1), keepdims=True)

    to_mate.wait()

    def spread(i, _):
        flat[pl.ds(pl.multiple_of(i * SHARD, SHARD), SHARD), :] = all_sum[i, 0:SHARD, :]
        return 0

    lax.fori_loop(0, SHARDS, spread, 0)

    def peak_sum(i, top):
        return jnp.maximum(top, flat[pl.ds(pl.multiple_of(2048 + i * 8, 8), 8), :])

    top = lax.fori_loop(0, 64, peak_sum, jnp.zeros((8, 128), f32))
    floor_p = 0.1 * jnp.max(top, axis=(0, 1), keepdims=True)

    def renew(i, _):
        rows = pl.ds(pl.multiple_of(i * 8, 8), 8)
        for j in range(2):
            cols = slice(128 * j, 128 * (j + 1))

            def at(k):
                return flat[pl.ds(pl.multiple_of((2 * k + j) * WIN + i * 8, 8), 8), :]

            wp = at(4)
            scale = 1.0 / (wp + floor_p)
            for m in range(2):
                for ch in range(2):
                    old = probe[m, ch, rows, cols]
                    probe_new[m, ch, rows, cols] = old + (at(2 * m + ch) - old * wp) * scale
        return 0

    lax.fori_loop(0, WIN // 8, renew, 0)

    rows8 = lax.broadcasted_iota(jnp.int32, (8, 128), 0)
    lanes8 = lax.broadcasted_iota(jnp.int32, (8, 128), 1)
    is_count = (rows8 == 7) & (lanes8 == 2)
    sums = all_sum[0, SHARD:PIECE, :]
    count = jnp.sum(jnp.where(is_count, sums, 0.0), axis=(0, 1), keepdims=True)
    mine_count = jnp.sum(jnp.where(is_count, raw[...], 0.0), axis=(0, 1), keepdims=True)
    mean = jnp.sum(sums, axis=0, keepdims=True) / count
    step[...] = jnp.where(rows8.astype(f32) < mine_count, raw[...] - mean, 0.0)

    finish_copy(middle, outer_ok, outer_ok)
    finish_copy(strip, outer_ok, outer_ok)
    for tiles in ((1,), (0, 2)):
        if 0 in tiles:
            for ch in range(2):
                finish_copy(sides[ch][0], has_right, has_left)
                finish_copy(sides[ch][1], has_left, has_right)
        for band, start in ((1, 128), (2, inner_to), (0, outer_to)):

            def update(i, _, band=band, start=start, tiles=tiles):
                rows = pl.ds(pl.multiple_of(start + i * 8, 8), 8)
                thin = pl.ds(pl.multiple_of(i * 8, 8), 8)
                for t in tiles:
                    k = t // 2
                    cols = slice(128 * t, 128 * (t + 1))
                    down = weight[rows, cols] + floor
                    for ch in range(2):
                        g = grad[ch, 1 + t, pl.ds(pl.multiple_of(136 + start + i * 8, 8), 8), :]
                        if band == 0:
                            v = middle_in[ch, thin, :] if t == 1 else row_in[k, ch, thin, :]
                            g = g + jnp.where(outer_ok, v, 0.0)
                            if t != 1:
                                g = g + jnp.where(jumped[k], corner_in[k, ch, thin, :], 0.0)
                        if band == 2:
                            g = g + mate_rows[ch, 1 + t, thin, :]
                        if t != 1:
                            g = g + jnp.where(col_ok[k], side_in[k, ch, rows, :], 0.0)
                        obj_new[ch, rows, cols] = obj[ch, rows, cols] + g / down
                return 0

            lax.fori_loop(0, 16, update, 0, unroll=2)


def sums(grad, weight, obj, probe, part, raw):
    v = pl.BlockSpec(memory_space=VMEM)
    dma = pltpu.SemaphoreType.DMA
    return pl.pallas_call(
        sums_kernel,
        out_shape=(
            jax.ShapeDtypeStruct((2, TILE, TILE), f32),
            jax.ShapeDtypeStruct((2, 2, WIN, WIN), f32),
            jax.ShapeDtypeStruct((8, 128), f32),
        ),
        in_specs=[v] * 6,
        out_specs=[v] * 3,
        scratch_shapes=[
            VMEM((2, 5, 128, 128), f32),
            VMEM((2, 2, 128, 128), f32),
            VMEM((2, 2, 128, 128), f32),
            VMEM((2, 2, 128, 128), f32),
            VMEM((2, 128, 128), f32),
            VMEM((2, 2, TILE, 128), f32),
            VMEM((2, 2, TILE, 128), f32),
            VMEM((SHARDS, PIECE, 128), f32),
            VMEM((SHARDS // 2, PIECE, 128), f32),
            VMEM((15, PIECE, 128), f32),
            VMEM((128, 128), f32),
            VMEM((7, 16, 128), f32),
            VMEM((128, 128), f32),
            VMEM((SHARDS, PIECE, 128), f32),
            VMEM((SHARDS * SHARD, 128), f32),
            dma((8,)),
            dma((8,)),
            dma((3,)),
            dma((3,)),
            dma((30,)),
            dma((30,)),
            dma((14,)),
            dma((14,)),
        ],
        compiler_params=pltpu.CompilerParams(
            collective_id=1, has_side_effects=True, vmem_limit_bytes=28 * 2**20
        ),
        name="sums",
    )(grad, weight, obj, probe, part, raw)


def on_device(object_field, probe, patterns, positions, counts):
    meta = jnp.concatenate([positions.reshape(1, 2 * CAP), counts.reshape(1, 1)], axis=1)
    meta = jnp.pad(meta, ((0, 7), (0, 128 - 2 * CAP - 1)))
    ext, spat, where = halo(object_field, patterns[0, 0], meta)
    grad, weight, part, raw = slots(where, ext, probe, spat, jnp.asarray(dft_tables()))
    object_new, probe_new, step = sums(
        grad, weight, object_field, probe, part.reshape(SHARDS * SHARD, 128), raw
    )
    return object_new, probe_new, step[:CAP, :2].reshape(1, 1, CAP, 2)


def solution(mesh):
    placed = (
        P(None, "row", "col"),
        P(),
        P("row", "col", None, None, None),
        P("row", "col", None, None),
        P("row", "col"),
    )
    return jax.shard_map(
        on_device,
        mesh=mesh,
        in_specs=placed,
        out_specs=(P(None, "row", "col"), P(), P("row", "col", None, None)),
        check_vma=False,
    )
```
